512 devices in a mesh: dp: 8 (over x, core), vocab: 64 (over z, y).
Axes of the slice: x: 4, y: 4, z: 16, core: 2. Of those that a mesh axis runs over, the one named last changes fastest.
Arguments:
- hidden_states: bfloat16 [1280, 4096], P('dp', 'vocab'), may hold values from -40 to 40
- head_weight: bfloat16 [10240, 4096], P('vocab'), may hold values from -1 to 1
- cluster_weight: bfloat16 [2, 4096], replicated, may hold values from -0.09375 to 0.09375
- proj_one: bfloat16 [4096, 1024], P('vocab'), may hold values from -1 to 1
- tail_one: bfloat16 [20480, 1024], P('vocab'), may hold values from -4 to 4
- proj_two: bfloat16 [4096, 256], P('vocab'), may hold values from -1 to 1
- tail_two: bfloat16 [106496, 256], P('vocab'), may hold values from -4 to 4
- targets: int32 [1280], P('dp'), may hold values from 0 to 106495, as said below
- token_cluster: int32 [1280], P('dp'), may hold values from 0 to 2, as said below
- tail_rows: int32 [8, 2, 40], P('dp'), may hold values from 0 to 159, as said below
- tail_counts: int32 [8, 2], P('dp'), may hold values from 20 to 40, as said below
Outputs:
- token_loss: float32 [1280], P('dp')
- grad_hidden: float32 [1280, 4096], P('dp', 'vocab')
- grad_head: float32 [10240, 4096], P('vocab', 'dp')
- grad_cluster: float32 [2, 4096], replicated
- grad_proj_one: float32 [4096, 1024], P('vocab')
- grad_tail_one: float32 [20480, 1024], P('vocab', 'dp')
- grad_proj_two: float32 [4096, 256], P('vocab')
- grad_tail_two: float32 [106496, 256], P('vocab', 'dp')
The draws below stay inside these ranges and needn't reach their ends.
Inputs may be any that keep to these rules, and one draw needn't show every extreme that they name: `tail_counts`: for each tail cluster some group has all 40 slots live. `tail_rows`: live slots of group g and tail cluster c name distinct tokens of group g whose token_cluster is c + 1; dead slots hold 0. `token_cluster`: group g has exactly tail_counts[g, c] tokens of cluster c + 1, those named in tail_rows. `targets`: below 10240 for cluster 0, below 20480 for cluster 1, below 106496 for cluster 2.
All inputs are finite; a program needn't handle non-finite values.
Results may differ from the reference program's by a relative error of at most 0.0038.
Values may be sent and summed in bfloat16 or wider, within the bound.
A program may use at most 64 MiB of HBM per device.

```python
import math
import jax
import jax.numpy as jnp
from jax import lax

D = 4096
D1 = 1024
D2 = 256
TOK_DEV = 160
CAP = 40
GROUPS = 8
TOKENS = 1280
HEAD = 10240
TAIL1 = 20480
TAIL2 = 106496


def routing(key):
    group_keys = jax.random.split(key, GROUPS)
    orders = jax.vmap(lambda single: jax.random.permutation(single, TOK_DEV))(group_keys).astype(jnp.int32)
    counts = jax.random.randint(jax.random.fold_in(key, 101), (GROUPS, 2), CAP // 2, CAP + 1).astype(jnp.int32)
    fullest = jax.random.randint(jax.random.fold_in(key, 102), (2,), 0, GROUPS)
    counts = counts.at[fullest[0], 0].set(CAP).at[fullest[1], 1].set(CAP)
    return (orders, counts)


def cluster_of(orders, counts):
    position = jnp.argsort(orders, axis=1).astype(jnp.int32)
    first_tail = position < counts[:, 0:1]
    second_tail = (position >= CAP) & (position < CAP + counts[:, 1:2])
    return jnp.where(first_tail, 1, jnp.where(second_tail, 2, 0)).astype(jnp.int32).reshape(TOKENS)


def shared_rows(key):
    return jnp.clip(jax.random.normal(jax.random.fold_in(key, 900), (HEAD, D), jnp.float32), -5.0, 5.0)


def draw_tail_counts(key, part):
    orders, counts = routing(key)
    return counts


def draw_tail_rows(key, part):
    orders, counts = routing(key)
    slot_ids = jnp.arange(CAP, dtype=jnp.int32)
    stacked = jnp.stack([orders[:, :CAP], orders[:, CAP:2 * CAP]], axis=1)
    return jnp.where(slot_ids[None, None, :] < counts[:, :, None], stacked, 0).astype(jnp.int32)


def draw_token_cluster(key, part):
    orders, counts = routing(key)
    return cluster_of(orders, counts)


def draw_targets(key, part):
    orders, counts = routing(key)
    cluster = cluster_of(orders, counts)
    key = jax.random.fold_in(key, 7)
    head_ids = jax.random.randint(jax.random.fold_in(key, 1), (TOKENS,), 0, HEAD)
    first_ids = jax.random.randint(jax.random.fold_in(key, 2), (TOKENS,), 0, TAIL1)
    second_ids = jax.random.randint(jax.random.fold_in(key, 3), (TOKENS,), 0, TAIL2)
    return jnp.where(cluster == 0, head_ids, jnp.where(cluster == 1, first_ids, second_ids)).astype(jnp.int32)


def draw_head_weight(key, part):
    return (shared_rows(key) / math.sqrt(D)).astype(jnp.bfloat16)


def draw_proj_one(key, part):
    key = jax.random.fold_in(key, 21)
    values = jnp.clip(jax.random.normal(key, (D, D1), jnp.float32), -6.0, 6.0) / math.sqrt(D)
    return values.astype(jnp.bfloat16)


def draw_proj_two(key, part):
    key = jax.random.fold_in(key, 22)
    values = jnp.clip(jax.random.normal(key, (D, D2), jnp.float32), -6.0, 6.0) / math.sqrt(D)
    return values.astype(jnp.bfloat16)


def draw_tail_one(key, part):
    key = jax.random.fold_in(key, 23)
    values = jnp.clip(jax.random.normal(key, (TAIL1, D1), jnp.float32), -6.0, 6.0) / math.sqrt(D1)
    return values.astype(jnp.bfloat16)


def draw_tail_two(key, part):
    key = jax.random.fold_in(key, 24)
    values = jnp.clip(jax.random.normal(key, (TAIL2, D2), jnp.float32), -6.0, 6.0) / math.sqrt(D2)
    return values.astype(jnp.bfloat16)


def draw_hidden_states(key, part):
    key = jax.random.fold_in(key, 3)
    values = jnp.clip(jax.random.normal(jax.random.fold_in(key, 1), (TOKENS, D), jnp.float32), -6.0, 6.0)
    return values.astype(jnp.bfloat16)


def noise(rng, extent, deviation, reach, kind=jnp.bfloat16):
    values = deviation * jax.random.normal(rng, extent, jnp.float32)
    return jnp.clip(values, min=-reach, max=reach).astype(kind)


def setup_inputs(seed: int = 0) -> dict:
    seeds = jax.random.split(jax.random.key(seed), 12)
    return {
        "hidden_states": draw_hidden_states(jax.random.fold_in(seeds[11], 71), 0),
        "head_weight": draw_head_weight(jax.random.fold_in(seeds[11], 71), 0),
        "cluster_weight": noise(seeds[2], (2, D), D ** -0.5, 0.09375),
        "proj_one": draw_proj_one(jax.random.fold_in(seeds[11], 71), 0),
        "tail_one": draw_tail_one(jax.random.fold_in(seeds[11], 71), 0),
        "proj_two": draw_proj_two(jax.random.fold_in(seeds[11], 71), 0),
        "tail_two": draw_tail_two(jax.random.fold_in(seeds[11], 71), 0),
        "targets": draw_targets(jax.random.fold_in(seeds[11], 71), 0),
        "token_cluster": draw_token_cluster(jax.random.fold_in(seeds[11], 71), 0),
        "tail_rows": draw_tail_rows(jax.random.fold_in(seeds[11], 71), 0),
        "tail_counts": draw_tail_counts(jax.random.fold_in(seeds[11], 71), 0),
    }


loss_scale = 64.0


def log_total(logits):
    highest = jnp.max(logits, axis=1, keepdims=True)
    return highest[:, 0] + jnp.log(jnp.sum(jnp.exp(logits - highest), axis=1))


def group_sum(left, right):
    groups_left = left.reshape(GROUPS, -1, left.shape[1])
    groups_right = right.reshape(GROUPS, -1, right.shape[1])

    def accumulate(running, operands):
        product = jnp.dot(operands[0].T, operands[1], preferred_element_type=jnp.float32)
        rounded = lax.optimization_barrier(product.astype(jnp.bfloat16)).astype(jnp.float32)
        return running + rounded, None

    start_sum = jnp.zeros((left.shape[1], right.shape[1]), jnp.float32)
    result, unused = lax.scan(accumulate, start_sum, (groups_left, groups_right))
    return result


def reference(hidden_states, head_weight, cluster_weight, proj_one, tail_one, proj_two, tail_two, targets, token_cluster, tail_rows, tail_counts):
    word_logits = jnp.dot(hidden_states, head_weight.T, preferred_element_type=jnp.float32)
    entry_logits = jnp.dot(hidden_states, cluster_weight.T, preferred_element_type=jnp.float32)
    all_logits = jnp.concatenate([word_logits, entry_logits], axis=1)
    head_target = jnp.where(token_cluster == 0, targets, HEAD + token_cluster - 1).astype(jnp.int32)
    head_total = log_total(all_logits)
    picked = jnp.take_along_axis(all_logits, head_target[:, None], axis=1)[:, 0]
    token_loss = head_total - picked
    onehot = (lax.broadcasted_iota(jnp.int32, all_logits.shape, 1) == head_target[:, None]).astype(jnp.float32)
    head_grad = (loss_scale * (jnp.exp(all_logits - head_total[:, None]) - onehot)).astype(jnp.bfloat16)
    grad_hidden = jnp.dot(head_grad[:, :HEAD], head_weight, preferred_element_type=jnp.float32) + jnp.dot(head_grad[:, HEAD:], cluster_weight, preferred_element_type=jnp.float32)
    grad_head = group_sum(head_grad[:, :HEAD], hidden_states)
    grad_cluster = jnp.dot(head_grad[:, HEAD:].T, hidden_states, preferred_element_type=jnp.float32)
    results = []
    offsets = (jnp.arange(GROUPS, dtype=jnp.int32) * TOK_DEV)[:, None]
    for cluster, projection, embedding in ((0, proj_one, tail_one), (1, proj_two, tail_two)):
        global_rows = (tail_rows[:, cluster, :] + offsets).reshape(-1).astype(jnp.int32)
        usable = (jnp.arange(CAP, dtype=jnp.int32)[None, :] < tail_counts[:, cluster:cluster + 1]).reshape(-1)
        chosen_rows = hidden_states[global_rows]
        projected = jnp.dot(chosen_rows, projection, preferred_element_type=jnp.float32).astype(jnp.bfloat16)
        logits = jnp.dot(projected, embedding.T, preferred_element_type=jnp.float32)
        goal_ids = jnp.where(usable, targets[global_rows], 0).astype(jnp.int32)
        tail_total = log_total(logits)
        tail_pick = jnp.take_along_axis(logits, goal_ids[:, None], axis=1)[:, 0]
        token_loss = token_loss.at[global_rows].add(jnp.where(usable, tail_total - tail_pick, jnp.float32(0.0)))
        tail_hot = (lax.broadcasted_iota(jnp.int32, logits.shape, 1) == goal_ids[:, None]).astype(jnp.float32)
        tail_grad = jnp.where(usable[:, None], loss_scale * (jnp.exp(logits - tail_total[:, None]) - tail_hot), jnp.float32(0.0)).astype(jnp.bfloat16)
        back_rows = jnp.dot(tail_grad, embedding, preferred_element_type=jnp.float32).astype(jnp.bfloat16)
        grad_hidden = grad_hidden.at[global_rows].add(jnp.dot(back_rows, projection.T, preferred_element_type=jnp.float32))
        results.append((jnp.dot(chosen_rows.T, back_rows, preferred_element_type=jnp.float32), group_sum(tail_grad, projected)))
    return token_loss, grad_hidden, grad_head, grad_cluster, results[0][0], results[0][1], results[1][0], results[1][1]
```

```python
import jax
import jax.numpy as jnp
from jax import lax
from jax.experimental import pallas as pl
from jax.experimental.pallas import tpu as pltpu
from jax.sharding import PartitionSpec as P

MESH = pl.DeviceIdType.MESH
F32 = jnp.float32
BF16 = jnp.bfloat16
SCALE = 64.0
FAR = (1, 2, 3)
NEAR = (1, 15, 2)
NEAR_FROM = (15, 1, 14)
SEMS = 128
NT = (((1,), (1,)), ((), ()))
TN = (((0,), (0,)), ((), ()))
NN = (((1,), (0,)), ((), ()))


def dot(a, b, dims=NN):
    return lax.dot_general(a, b, dims, preferred_element_type=F32)


def dot_exact(a, b):
    return lax.dot_general(a, b, NN, precision=lax.Precision.HIGHEST, preferred_element_type=F32)


def lanes(shape):
    return lax.broadcasted_iota(jnp.int32, shape, len(shape) - 1)


def rows_of(shape):
    return lax.broadcasted_iota(jnp.int32, shape, len(shape) - 2)


def pack_rest(rest, height):
    out = None
    total = rest.shape[0]
    for q in range(4):
        lo, hi = q * height, min((q + 1) * height, total)
        part = rest[lo:hi]
        if q:
            part = pltpu.roll(part, 32 * q, 1)
        if hi - lo < height:
            part = jnp.concatenate([part, jnp.zeros((height - (hi - lo), 128), F32)], axis=0)
        out = part if out is None else out + part
    return out


def unpack_rest(packed, q):
    part = packed if q == 0 else pltpu.roll(packed, 128 - 32 * q, 1)
    return jnp.where(lanes(part.shape) < 32, part, 0.0).astype(BF16)


def kernel(
    hid_ref, hw_ref, cw_ref, p1_ref, t1_ref, p2_ref, t2_ref, meta_ref,
    loss_ref, gh_ref, head_ref, cl_ref, gp1_ref, gt1_ref, gp2_ref, gt2_ref,
    hp, G, WT, hwx, hwxT, HG, HU,
    CH, PT, PRY, PRN, PRF, PS1, PS2, PG, Xf, PJ,
    P1f, P2f, P1b, P2b,
    ST, STF, STN, STY, TS,
    LG, L1s, L2s, INF, GP, GU, GC,
    BT, BRY, BRN, BRF, BS1, BS2, BG, BK, C1f, C2f,
    GB, GRY, GS1, GRN, GS2, GRF,
    ssem, rsem, lsem,
):
    d = lax.axis_index("dp")
    v = lax.axis_index("vocab")
    x, c = lax.div(d, 2), lax.rem(d, 2)
    z, y = lax.div(v, 4), lax.rem(v, 4)
    zhi, zlo = lax.div(z, 4), lax.rem(z, 4)

    def far_dev(k):
        return (d, lax.rem(z + 4 * k, 16) * 4 + y)

    def near_dev(o):
        return (d, lax.rem(z + o, 16) * 4 + y)

    def y_dev(k):
        return (d, z * 4 + lax.rem(y + k, 4))

    def x_dev(k):
        return (lax.rem(x + k, 4) * 2 + c, v)

    core_dev = (x * 2 + 1 - c, v)

    def dp_dev(k):
        return (lax.rem(d + k, 8), v)

    counter = [0]
    sent = []

    def send(src, dst, dev):
        i = counter[0]
        counter[0] += 1
        copy = pltpu.make_async_remote_copy(
            src_ref=src, dst_ref=dst, send_sem=ssem.at[i], recv_sem=rsem.at[i],
            device_id=dev, device_id_type=MESH,
        )
        copy.start()
        sent.append(copy)
        return i

    def recv(i, slot):
        pltpu.make_async_remote_copy(
            src_ref=slot, dst_ref=slot, send_sem=ssem.at[i], recv_sem=rsem.at[i],
            device_id=core_dev, device_id_type=MESH,
        ).wait_recv()

    hw_copy = pltpu.make_async_copy(hw_ref, hwx.at[0:160], lsem)
    hw_copy.start()

    barrier = pltpu.get_barrier_semaphore()
    greeted = 0
    for k in FAR:
        pl.semaphore_signal(barrier, inc=1, device_id=far_dev(k), device_id_type=MESH)
        pl.semaphore_signal(barrier, inc=1, device_id=y_dev(k), device_id_type=MESH)
        greeted += 2
    for o in NEAR_FROM:
        pl.semaphore_signal(barrier, inc=1, device_id=near_dev(o), device_id_type=MESH)
        greeted += 1
    for k in range(1, 8):
        pl.semaphore_signal(barrier, inc=1, device_id=dp_dev(k), device_id_type=MESH)
        greeted += 1

    hp[...] = jnp.zeros_like(hp)
    hp[:, 0:160] = hid_ref[...].astype(F32)
    G[y, zlo, zhi, 0:64, :] = hp[:, 0:128].astype(BF16)
    G[y, zlo, zhi, 64:80, :] = pack_rest(hp[:, 128:256], 16).astype(BF16)

    TS[...] = jnp.zeros_like(TS)
    TS[0:8, :] = meta_ref[:, 256:384].astype(F32)
    row_col = jnp.transpose(TS[...])[0:80, 0:1].astype(jnp.int32)
    target = meta_ref[0:1, 0:256]
    cluster = meta_ref[1:2, 0:256]
    slot_hit = lanes((80, 256)) == row_col
    onehot = jnp.where(slot_hit, 1.0, 0.0).astype(BF16)
    live = row_col >= 0
    goal = jnp.sum(jnp.where(slot_hit, target, 0).astype(F32), axis=1, keepdims=True).astype(jnp.int32)
    goal = jnp.where(live, goal, -1)

    hidb = hp[...].astype(BF16)
    chosen = dot(onehot, hidb, NT)
    CH[d, :, 64:128] = jnp.zeros((80, 64), BF16)
    CH[d, :, 0:64] = chosen.astype(BF16)
    part1 = dot(chosen[0:40].astype(BF16), p1_ref[...])
    part2 = dot(chosen[40:80].astype(BF16), p2_ref[...])

    def to_tiles(tiles, a, b):
        for t in range(64):
            at = tiles.at[t // 16, (t // 4) % 4, t % 4]
            i, j = t // 10, t % 10
            if t >= 50:
                at[...] = jnp.zeros((8, 128), F32)
            elif j < 8:
                at[...] = a[8 * i : 8 * i + 8, 128 * j : 128 * j + 128]
            else:
                at[...] = b[8 * i : 8 * i + 8, 128 * j - 1024 : 128 * j - 896]

    to_tiles(PT, part1, part2)

    pl.semaphore_wait(barrier, greeted)

    own = G.at[y, zlo, zhi]
    hid_far = [send(own, own, far_dev(k)) for k in FAR]

    def small_y(tiles, slots):
        return [send(tiles.at[lax.rem(y + k, 4)], slots.at[k - 1], y_dev(k)) for k in FAR]

    def small_near(tiles, slots, ids, sums, nslots):
        for n, i in enumerate(ids):
            recv(i, slots.at[n])
        sums[...] = (tiles[y] + slots[0]) + (slots[1] + slots[2])
        return [
            send(sums.at[lax.rem(zlo + o, 4)], nslots.at[n], near_dev(o))
            for n, o in enumerate(NEAR)
        ]

    def small_far(sums, nslots, ids, sums2, fslots):
        for n, i in enumerate(ids):
            recv(i, nslots.at[n])
        sums2[...] = (sums[zlo] + nslots[0]) + (nslots[1] + nslots[2])
        return [
            send(sums2.at[lax.rem(zhi + k, 4)], fslots.at[k - 1], far_dev(k)) for k in FAR
        ]

    def small_back_far(sums2, fslots, ids, full):
        for n, i in enumerate(ids):
            recv(i, fslots.at[n])
        full[y, zlo, zhi] = (sums2[zhi] + fslots[0]) + (fslots[1] + fslots[2])
        return [send(full.at[y, zlo, zhi], full.at[y, zlo, zhi], far_dev(k)) for k in FAR]

    def small_back_near(full, ids):
        for k, i in zip(FAR, ids):
            recv(i, full.at[y, zlo, lax.rem(zhi + 4 - k, 4)])
        return [send(full.at[y, zlo], full.at[y, zlo], near_dev(o)) for o in NEAR]

    def small_back_y(full, ids):
        for o, i in zip(NEAR, ids):
            recv(i, full.at[y, lax.rem(zlo + 16 - o, 4)])
        return [send(full.at[y], full.at[y], y_dev(k)) for k in FAR]

    def small_done(full, ids):
        for k, i in zip(FAR, ids):
            recv(i, full.at[lax.rem(y + 4 - k, 4)])
        for t in range(50):
            i, j = t // 10, t % 10
            r, l = (8 * i, 128 * j) if j < 5 else (40 + 8 * i, 128 * j - 640)
            Xf[r : r + 8, l : l + 128] = full[t // 16, (t // 4) % 4, t % 4]

    def dp_x(buf):
        return [send(buf.at[x, c], buf.at[x, c], x_dev(k)) for k in FAR]

    def dp_core(buf, ids):
        for k, i in zip(FAR, ids):
            recv(i, buf.at[lax.rem(x + 4 - k, 4), c])
        return send(buf.at[:, c], buf.at[:, c], core_dev)

    def dp_done(buf, i):
        recv(i, buf.at[:, 1 - c])

    pr_y = small_y(PT, PRY)
    CHv = CH.reshape(4, 2, 80, 128)
    ch_x = dp_x(CHv)

    cw = cw_ref[...].astype(F32)
    row16 = rows_of((16, 4096))
    hwx[160:176, :] = jnp.where(
        row16 == 0, cw[0:1, :], jnp.where(row16 == 1, cw[1:2, :], 0.0)
    ).astype(BF16)
    hwx[176:256, :] = jnp.zeros((80, 4096), BF16)
    hw_copy.wait()

    def turn(j, _):
        at = pl.ds(pl.multiple_of(j * 128, 128), 128)
        hwxT[at, :] = jnp.transpose(hwx[:, at].astype(F32)).astype(BF16)
        return 0

    lax.fori_loop(0, 32, turn, 0)

    for k, i in zip(FAR, hid_far):
        recv(i, G.at[y, zlo, lax.rem(zhi + 4 - k, 4)])
    hid_near = [send(G.at[y, zlo], G.at[y, zlo], near_dev(o)) for o in NEAR]
    hid_y = [[send(G.at[y, zlo], G.at[y, zlo], y_dev(k)) for k in FAR]]
    pr_n = small_near(PT, PRY, pr_y, PS1, PRN)
    for o, i in zip(NEAR, hid_near):
        at = lax.rem(zlo + 16 - o, 4)
        recv(i, G.at[y, at])
        hid_y.append([send(G.at[y, at], G.at[y, at], y_dev(k)) for k in FAR])
    pr_f = small_far(PS1, PRN, pr_n, PS2, PRF)
    pr_bf = small_back_far(PS2, PRF, pr_f, PG)
    pr_bn = small_back_near(PG, pr_bf)
    pr_by = small_back_y(PG, pr_bn)
    ch_c = dp_core(CHv, ch_x)
    small_done(PG, pr_by)
    PJ[d] = Xf[...].astype(BF16)
    PJv = PJ.reshape(4, 2, 80, 640)
    pj_x = dp_x(PJv)

    left, right = Xf[0:40, :].astype(BF16), Xf[40:80, :].astype(BF16)
    log1 = dot(left, t1_ref[:, 0:640], NT) + dot(right[:, 0:384], t1_ref[:, 640:1024], NT)
    log2 = dot(right[:, 384:640], t2_ref[...], NT)
    L1s[...] = log1
    L2s[...] = log2

    def column_stats(values, goals):
        high = jnp.max(values, axis=1, keepdims=True)
        total = jnp.sum(jnp.exp(values - high), axis=1, keepdims=True)
        hit = lanes(values.shape) == goals
        return high, total, jnp.sum(jnp.where(hit, values, 0.0), axis=1, keepdims=True)

    stat1 = column_stats(log1, goal[0:40] - v * 320)
    stat2 = column_stats(log2, goal[40:80] - v * 1664)
    lane = lanes((80, 128))
    table = jnp.zeros((80, 128), F32)
    for n in range(3):
        table = jnp.where(lane == 3 + n, jnp.concatenate([stat1[n], stat2[n]], axis=0), table)
    TS[0:80, :] = table
    TS[80:128, :] = jnp.zeros((48, 128), F32)
    tail_tile = jnp.transpose(TS[...])[0:8, :]

    for n, ids in enumerate(hid_y):
        at = zlo if n == 0 else lax.rem(zlo + 16 - NEAR[n - 1], 4)
        for k, i in zip(FAR, ids):
            recv(i, G.at[lax.rem(y + 4 - k, 4), at])

    slices = []
    for k in range(1, 8):
        peer = lax.rem(d + k, 8)
        src = G.at[:, pl.ds(lax.rem(2 * peer, 4), 2), lax.div(peer, 2)]
        slices.append(send(src, HG.at[d], dp_dev(k)))

    def spread(n, _):
        zz, yy = lax.div(n, 4), lax.rem(n, 4)
        block = G.at[yy, lax.rem(zz, 4), lax.div(zz, 4)]
        base = pl.multiple_of(n * 64, 64)
        WT[pl.ds(base, 64), 0:128] = block[0:64, :]
        packed = block[64:80, :].astype(F32)
        for q in range(4):
            WT[pl.ds(pl.multiple_of(base + 16 * q, 16), 16), 128:256] = unpack_rest(packed, q)
        return 0

    lax.fori_loop(0, 64, spread, 0)

    LG[...] = dot(hwx[...], WT[...])
    words = LG[0:160, :]
    head_goal = jnp.where(cluster == 0, target, -1) - v * 160
    head_hit = rows_of((160, 256)) == head_goal
    high = jnp.max(words, axis=0, keepdims=True)
    total = jnp.sum(jnp.exp(words - high), axis=0, keepdims=True)
    picked = jnp.sum(jnp.where(head_hit, words, 0.0), axis=0, keepdims=True)
    row8 = rows_of((8, 256))
    wide_tail = jnp.concatenate([tail_tile, jnp.zeros((8, 128), F32)], axis=1)
    tile = jnp.where(
        row8 == 0, high, jnp.where(row8 == 1, total, jnp.where(row8 == 2, picked, wide_tail))
    )

    def join(slots):
        parts = [slots[i] for i in range(4)]
        result = []
        for base in (0, 3):
            m = [p[base : base + 1] for p in parts]
            top = jnp.maximum(jnp.maximum(m[0], m[1]), jnp.maximum(m[2], m[3]))
            s = [p[base + 1 : base + 2] * jnp.exp(mm - top) for p, mm in zip(parts, m)]
            t = [p[base + 2 : base + 3] for p in parts]
            result += [top, (s[0] + s[1]) + (s[2] + s[3]), (t[0] + t[1]) + (t[2] + t[3])]
        return result

    def as_tile(result):
        out = jnp.zeros((8, 256), F32)
        for n in range(6):
            out = jnp.where(row8 == n, result[n], out)
        return out

    STF[zhi] = tile
    ids = [send(STF.at[zhi], STF.at[zhi], far_dev(k)) for k in FAR]
    pj_c = dp_core(PJv, pj_x)
    for k, i in zip(FAR, ids):
        recv(i, STF.at[lax.rem(zhi + 4 - k, 4)])
    STN[zlo] = as_tile(join(STF))
    ids = [send(STN.at[zlo], STN.at[zlo], near_dev(o)) for o in NEAR]
    for o, i in zip(NEAR, ids):
        recv(i, STN.at[lax.rem(zlo + 16 - o, 4)])
    STY[y] = as_tile(join(STN))
    ids = [send(STY.at[y], STY.at[y], y_dev(k)) for k in FAR]
    for k, i in zip(FAR, ids):
        recv(i, STY.at[lax.rem(y + 4 - k, 4)])
    stats = join(STY)

    tail_lse = stats[3] + jnp.log(stats[4])
    TS[...] = jnp.zeros_like(TS)
    TS[0:1, :] = tail_lse[:, 0:128]
    TS[1:2, :] = (tail_lse - stats[5])[:, 0:128]
    columns = jnp.transpose(TS[...])[0:80, :]
    lse_col = jnp.where(live, columns[:, 0:1], 1e30)
    loss_col = columns[:, 1:2]

    def tail_gradient(values, lse, goals):
        hit = (lanes(values.shape) == goals).astype(F32)
        return (SCALE * (jnp.exp(values - lse) - hit)).astype(BF16)

    own1 = tail_gradient(L1s[...], lse_col[0:40], goal[0:40] - v * 320)
    own2 = tail_gradient(L2s[...], lse_col[40:80], jnp.where(live, goal, -(1 << 20))[40:80] - v * 1664)
    back1 = dot(own1, t1_ref[...])
    back2 = dot(own2, t2_ref[...])
    to_tiles(BT, back1, back2)
    bk_y = small_y(BT, BRY)

    INF[d] = jnp.where(lane == 0, lse_col, jnp.where(lane == 1, goal.astype(F32), 0.0))
    INFv = INF.reshape(4, 2, 80, 128)
    inf_x = dp_x(INFv)

    entry0, entry1 = LG[160:161, :], LG[161:162, :]
    top = jnp.maximum(stats[0], jnp.maximum(entry0, entry1))
    summed = stats[1] * jnp.exp(stats[0] - top) + (jnp.exp(entry0 - top) + jnp.exp(entry1 - top))
    lse = top + jnp.log(summed)
    is1, is2 = (cluster == 1).astype(F32), (cluster == 2).astype(F32)
    chosen_logit = stats[2] + (is1 * entry0 + is2 * entry1)
    tail_loss = jnp.sum(jnp.where(slot_hit, loss_col, 0.0), axis=0, keepdims=True)
    loss_ref[...] = (lse - chosen_logit) + tail_loss

    inside = lanes((160, 256)) < 160
    grad = jnp.where(inside, SCALE * (jnp.exp(LG[0:160, :] - lse) - head_hit.astype(F32)), 0.0)
    inside1 = lanes((1, 256)) < 160
    ge0 = jnp.where(inside1, SCALE * (jnp.exp(entry0 - lse) - is1), 0.0)
    ge1 = jnp.where(inside1, SCALE * (jnp.exp(entry1 - lse) - is2), 0.0)
    GP[d, 0:160, :] = grad[:, 0:128].astype(BF16)
    rounded_rest = grad[:, 128:256]
    GP[d, 160:208, :] = pack_rest(rounded_rest, 48).astype(BF16)
    GPv = GP.reshape(4, 2, 208, 128)
    gp_x = dp_x(GPv)

    row96 = rows_of((96, 256))
    mine = (v == 0).astype(F32)
    low = jnp.where(row96 == 0, ge0 * mine, jnp.where(row96 == 1, ge1 * mine, 0.0))
    grad_ext = jnp.concatenate([grad, low], axis=0).astype(BF16)

    def part(n, _):
        zz = lax.rem(n, 16)
        at = pl.ds(pl.multiple_of(zz * 256, 256), 256)
        product = dot(hwxT[at, :], grad_ext)
        for yy in range(4):
            block = GB.at[yy, lax.rem(zz, 4), lax.div(zz, 4)]
            piece = product[64 * yy : 64 * yy + 64]
            block[0:64, :] = piece[:, 0:128].astype(BF16)
            block[64:80, :] = pack_rest(piece[:, 128:256], 16).astype(BF16)
        return 0

    lax.fori_loop(0, 16, part, 0)
    gh_y = []
    for o in NEAR + (0,):
        at = lax.rem(zlo + o, 4)
        gh_y.append(
            [
                send(GB.at[lax.rem(y + k, 4), at], GRY.at[k - 1, at], y_dev(k))
                for k in FAR
            ]
        )

    bk_n = small_near(BT, BRY, bk_y, BS1, BRN)
    entries = jnp.where(rows_of((8, 256)) % 2 == 0, ge0, ge1).astype(BF16)
    full = dot(entries, WT[...], NT)
    pair = lax.div(rows_of((8, 1024)), 2)
    packed_cl = jnp.zeros((8, 1024), F32)
    for k in range(4):
        packed_cl = jnp.where(pair == k, full[:, 1024 * k : 1024 * k + 1024], packed_cl)
    GC[d] = packed_cl
    GCv = GC.reshape(4, 2, 8, 1024)
    gc_x = dp_x(GCv)

    bk_f = small_far(BS1, BRN, bk_n, BS2, BRF)
    bk_bf = small_back_far(BS2, BRF, bk_f, BG)

    inf_c = dp_core(INFv, inf_x)
    gp_c = dp_core(GPv, gp_x)
    bk_bn = small_back_near(BG, bk_bf)

    gh_n = []
    for n, o in enumerate(NEAR):
        at = lax.rem(zlo + o, 4)
        for k, i in zip(FAR, gh_y[n]):
            recv(i, GRY.at[k - 1, at])
        GS1[n] = (
            (GB[y, at].astype(F32) + GRY[0, at].astype(F32))
            + (GRY[1, at].astype(F32) + GRY[2, at].astype(F32))
        ).astype(BF16)
        gh_n.append(send(GS1.at[n], GRN.at[n], near_dev(o)))
        if n == 0:
            bk_by = small_back_y(BG, bk_bn)
    gc_c = dp_core(GCv, gc_x)
    small_done(BG, bk_by)
    BK[d] = Xf[...].astype(BF16)
    BKv = BK.reshape(4, 2, 80, 640)
    bk_x = dp_x(BKv)

    for k, i in zip(FAR, gh_y[3]):
        recv(i, GRY.at[k - 1, zlo])
    mine_sum = (GB[y, zlo].astype(F32) + GRY[0, zlo].astype(F32)) + (
        GRY[1, zlo].astype(F32) + GRY[2, zlo].astype(F32)
    )
    for n, i in enumerate(gh_n):
        recv(i, GRN.at[n])
    GS2[...] = mine_sum + (
        GRN[0].astype(F32) + (GRN[1].astype(F32) + GRN[2].astype(F32))
    )
    GRF[3] = GS2[zhi].astype(BF16)
    for k in FAR:
        GRF[3 + k] = GS2[lax.rem(zhi + k, 4)].astype(BF16)
    gh_f = [send(GRF.at[3 + k], GRF.at[k - 1], far_dev(k)) for k in FAR]

    def assemble(src, dst1, dst2):
        for g in range(8):
            both = src[g].astype(F32)
            dst1[40 * g : 40 * g + 40, 0:640] = both[0:40, :]
            dst1[40 * g : 40 * g + 40, 640:1024] = both[40:80, 0:384]
            dst2[40 * g : 40 * g + 40, :] = both[40:80, 384:640]

    dp_done(PJv, pj_c)
    dp_done(INFv, inf_c)
    assemble(PJ, P1f, P2f)
    P1b[...] = P1f[...].astype(BF16)
    P2b[...] = P2f[...].astype(BF16)

    def gather_column(lo, lane_at):
        return jnp.concatenate([INF[g, lo : lo + 40, lane_at : lane_at + 1] for g in range(8)], axis=0)

    lse1, goal1 = gather_column(0, 0), gather_column(0, 1).astype(jnp.int32)
    all1 = dot(P1b[...], t1_ref[...], NT)
    base1 = jnp.where(goal1 < 0, -(1 << 20), goal1 - v * 320)
    grad1 = tail_gradient(all1, lse1, base1)
    gt1_ref[...] = dot(grad1, P1b[:, pl.ds(pl.multiple_of(d * 128, 128), 128)], TN)

    lse2, goal2 = gather_column(40, 0), gather_column(40, 1).astype(jnp.int32)
    base2 = jnp.where(goal2 < 0, -(1 << 20), goal2 - v * 1664)
    select = jnp.where(lanes((32, 256)) == rows_of((32, 256)) + d * 32, 1.0, 0.0).astype(BF16)
    mine2 = dot(select, P2b[...], NT).astype(BF16)
    P1f[:, 0:128] = jnp.broadcast_to(lse2, (320, 128))
    P1f[:, 128:256] = jnp.broadcast_to(base2.astype(F32), (320, 128))

    def tail_two(j, _):
        at = pl.multiple_of(j * 128, 128)
        logits = dot(P2b[...], t2_ref[pl.ds(at, 128), :], NT)
        hit = (lanes((320, 128)).astype(F32) + (j * 128).astype(F32)) == P1f[:, 128:256]
        grads = (SCALE * (jnp.exp(logits - P1f[:, 0:128]) - hit.astype(F32))).astype(BF16)
        gt2_ref[:, pl.ds(at, 128)] = dot(mine2, grads)
        return 0

    lax.fori_loop(0, 13, tail_two, 0)
    bk_c = dp_core(BKv, bk_x)

    HG[d] = G[:, pl.ds(lax.rem(2 * d, 4), 2), lax.div(d, 2)]
    dp_done(GPv, gp_c)
    for k, i in zip(range(1, 8), slices):
        recv(i, HG.at[lax.rem(d + 8 - k, 8)])
    head_ref[...] = jnp.zeros_like(head_ref)

    def head_group(g, _):
        GU[:, 0:128] = GP[g, 0:160, :]
        rest = GP[g, 160:208, :].astype(F32)
        for q in range(4):
            rows = 48 if q < 3 else 16
            GU[48 * q : 48 * q + rows, 128:256] = unpack_rest(rest[0:rows], q)
        for b in range(8):
            block = HG.at[g, b % 4, b // 4]
            HU[64 * b : 64 * b + 64, 0:128] = block[0:64, :]
            packed = block[64:80, :].astype(F32)
            for q in range(4):
                HU[64 * b + 16 * q : 64 * b + 16 * q + 16, 128:256] = unpack_rest(packed, q)
        head_ref[...] += dot(GU[...], HU[...], NT)
        return 0

    lax.fori_loop(0, 8, head_group, 0)

    dp_done(GCv, gc_c)
    cl_ref[...] = ((GC[0] + GC[1]) + (GC[2] + GC[3])) + ((GC[4] + GC[5]) + (GC[6] + GC[7]))

    both = BK[d].astype(F32)
    b1a, b1b = both[0:40, :].astype(BF16), both[40:80, 0:384].astype(BF16)
    b2 = both[40:80, 384:640].astype(BF16)
    hot1 = jnp.where(slot_hit[0:40], 1.0, 0.0)
    hot2 = jnp.where(slot_hit[40:80], 1.0, 0.0)
    back_one = dot(p1_ref[:, 0:640], b1a, NT) + dot(p1_ref[:, 640:1024], b1b, NT)
    add = dot_exact(back_one, hot1) + dot_exact(dot(p2_ref[...], b2, NT), hot2)
    for n, i in enumerate(gh_f):
        recv(i, GRF.at[n])
    block = GS2[zhi] + (GRF[0].astype(F32) + (GRF[1].astype(F32) + GRF[2].astype(F32)))
    hp[:, 0:128] = block[0:64, :]
    for q in range(4):
        part_q = block[64:80, :]
        hp[16 * q : 16 * q + 16, 128:256] = part_q if q == 0 else pltpu.roll(part_q, 128 - 32 * q, 1)
    gh_ref[...] = (hp[...] + add)[:, 0:160]

    dp_done(CHv, ch_c)
    dp_done(BKv, bk_c)
    assemble(BK, P1f, P2f)
    for g in range(8):
        rows_g = CH[g].astype(F32)
        C1f[40 * g : 40 * g + 40, :] = rows_g[0:40, :]
        C2f[40 * g : 40 * g + 40, :] = rows_g[40:80, :]
    gp1_ref[...] = dot(C1f[...].astype(BF16), P1f[...].astype(BF16), TN)[0:64, :]
    gp2_ref[...] = dot(C2f[...].astype(BF16), P2f[...].astype(BF16), TN)[0:64, :]

    for copy in sent:
        copy.wait_send()


def on_device(
    hidden_states, head_weight, cluster_weight, proj_one, tail_one, proj_two, tail_two,
    targets, token_cluster, tail_rows, tail_counts,
):
    slot = jnp.arange(40, dtype=jnp.int32)[None, :]
    rows = jnp.where(slot < tail_counts[0][:, None], tail_rows[0], -1).reshape(1, 80)
    meta = jnp.concatenate(
        [
            jnp.pad(jnp.stack([targets, token_cluster]), ((0, 6), (0, 96)), constant_values=-1),
            jnp.pad(rows, ((0, 7), (0, 48)), constant_values=-1),
        ],
        axis=1,
    )
    vmem = pl.BlockSpec(memory_space=pltpu.VMEM)
    shapes = [
        ((1, 256), F32), ((64, 160), F32), ((160, 512), F32), ((8, 1024), F32),
        ((64, 1024), F32), ((320, 128), F32), ((64, 256), F32), ((32, 1664), F32),
    ]
    V = pltpu.VMEM
    scratch = [
        V((64, 256), F32), V((4, 4, 4, 80, 128), BF16), V((4096, 256), BF16), V((256, 4096), BF16),
        V((4096, 256), BF16), V((8, 4, 2, 80, 128), BF16), V((512, 256), BF16),
        V((8, 80, 128), BF16), V((4, 4, 4, 8, 128), F32), V((3, 4, 4, 8, 128), F32),
        V((3, 4, 8, 128), F32), V((3, 8, 128), F32), V((4, 4, 8, 128), F32), V((4, 8, 128), F32),
        V((4, 4, 4, 8, 128), F32), V((80, 640), F32), V((8, 80, 640), BF16),
        V((320, 1024), F32), V((320, 256), F32), V((320, 1024), BF16), V((320, 256), BF16),
        V((8, 256), F32), V((4, 8, 256), F32), V((4, 8, 256), F32), V((4, 8, 256), F32), V((128, 128), F32),
        V((256, 256), F32), V((40, 320), F32), V((40, 1664), F32), V((8, 80, 128), F32),
        V((8, 208, 128), BF16), V((160, 256), BF16), V((8, 8, 1024), F32),
        V((4, 4, 4, 8, 128), F32), V((3, 4, 4, 8, 128), F32), V((3, 4, 8, 128), F32), V((3, 8, 128), F32),
        V((4, 4, 8, 128), F32), V((4, 8, 128), F32), V((4, 4, 4, 8, 128), F32), V((8, 80, 640), BF16),
        V((320, 128), F32), V((320, 128), F32),
        V((4, 4, 4, 80, 128), BF16), V((3, 4, 4, 80, 128), BF16), V((3, 4, 80, 128), BF16),
        V((3, 4, 80, 128), BF16), V((4, 80, 128), F32), V((7, 80, 128), BF16),
        pltpu.SemaphoreType.DMA((SEMS,)), pltpu.SemaphoreType.DMA((SEMS,)), pltpu.SemaphoreType.DMA,
    ]
    out = pl.pallas_call(
        kernel,
        out_shape=[jax.ShapeDtypeStruct(s, t) for s, t in shapes],
        in_specs=[vmem, pl.BlockSpec(memory_space=pl.ANY)] + [vmem] * 6,
        out_specs=[vmem] * 8,
        scratch_shapes=scratch,
        compiler_params=pltpu.CompilerParams(
            collective_id=0, has_side_effects=True, vmem_limit_bytes=56 * 1024 * 1024
        ),
    )(
        hidden_states.T, head_weight, cluster_weight, proj_one, tail_one, proj_two, tail_two, meta
    )
    loss, gh, head, cl, gp1, gt1, gp2, gt2 = out
    return (
        loss[0, :160],
        gh.T,
        head,
        cl.reshape(4, 2, 1024).transpose(1, 0, 2).reshape(2, 4096),
        gp1,
        gt1,
        gp2,
        gt2.T,
    )


def solution(mesh):
    return jax.shard_map(
        on_device,
        mesh=mesh,
        in_specs=(
            P("dp", "vocab"), P("vocab", None), P(), P("vocab", None), P("vocab", None),
            P("vocab", None), P("vocab", None), P("dp"), P("dp"), P("dp", None, None), P("dp", None),
        ),
        out_specs=(
            P("dp"), P("dp", "vocab"), P("vocab", "dp"), P(), P("vocab", None),
            P("vocab", "dp"), P("vocab", None), P("vocab", "dp"),
        ),
        check_vma=False,
    )
```

```python
import jax
import jax.numpy as jnp
from jax import lax
from jax.experimental import pallas as pl
from jax.experimental.pallas import tpu as pltpu
from jax.sharding import PartitionSpec as P

MESH = pl.DeviceIdType.MESH
F32 = jnp.float32
BF16 = jnp.bfloat16
SCALE = 64.0
FAR = (1, 2, 3)
NEAR = (1, 15, 2)
NEAR_FROM = (15, 1, 14)
SEMS = 128
NT = (((1,), (1,)), ((), ()))
TN = (((0,), (0,)), ((), ()))
NN = (((1,), (0,)), ((), ()))


def dot(a, b, dims=NN):
    return lax.dot_general(a, b, dims, preferred_element_type=F32)


def dot_exact(a, b):
    return lax.dot_general(a, b, NN, precision=lax.Precision.HIGHEST, preferred_element_type=F32)


def lanes(shape):
    return lax.broadcasted_iota(jnp.int32, shape, len(shape) - 1)


def rows_of(shape):
    return lax.broadcasted_iota(jnp.int32, shape, len(shape) - 2)


def pack_rest(rest, height):
    out = None
    total = rest.shape[0]
    for q in range(4):
        lo, hi = q * height, min((q + 1) * height, total)
        part = rest[lo:hi]
        if q:
            part = pltpu.roll(part, 32 * q, 1)
        if hi - lo < height:
            part = jnp.concatenate([part, jnp.zeros((height - (hi - lo), 128), F32)], axis=0)
        out = part if out is None else out + part
    return out


def unpack_rest(packed, q):
    part = packed if q == 0 else pltpu.roll(packed, 128 - 32 * q, 1)
    return jnp.where(lanes(part.shape) < 32, part, 0.0).astype(BF16)


def kernel(
    hid_ref, hw_ref, cw_ref, p1_ref, t1_hbm, p2_ref, t2_hbm, tgt_ref, clu_ref, rows_ref, count_ref,
    loss_ref, gh_ref, head_ref, cl_ref, gp1_ref, gt1_ref, gp2_ref, gt2_ref,
    t1_ref, t2_ref, ids, hp, G, WT, hwx, hwxT, HG, HU,
    CH, PT, PRY, PRN, PRF, PS1, PS2, PG, Xf, PJ,
    P1f, P2f, P1b, P2b,
    ST, STF, STN, STY, TS,
    LG, L1s, L2s, INF, GP, GU, GC,
    BT, BRY, BRN, BRF, BS1, BS2, BG, BK, C1f, C2f,
    GB, GRY, GS1, GRN, GS2, GRF,
    ssem, rsem, lsem, tsem,
):
    d = lax.axis_index("dp")
    v = lax.axis_index("vocab")
    x, c = lax.div(d, 2), lax.rem(d, 2)
    z, y = lax.div(v, 4), lax.rem(v, 4)
    zhi, zlo = lax.div(z, 4), lax.rem(z, 4)

    def far_dev(k):
        return (d, lax.rem(z + 4 * k, 16) * 4 + y)

    def near_dev(o):
        return (d, lax.rem(z + o, 16) * 4 + y)

    def y_dev(k):
        return (d, z * 4 + lax.rem(y + k, 4))

    def x_dev(k):
        return (lax.rem(x + k, 4) * 2 + c, v)

    core_dev = (x * 2 + 1 - c, v)

    def dp_dev(k):
        return (lax.rem(d + k, 8), v)

    counter = [0]
    sent = []

    def send(src, dst, dev):
        i = counter[0]
        counter[0] += 1
        copy = pltpu.make_async_remote_copy(
            src_ref=src, dst_ref=dst, send_sem=ssem.at[i], recv_sem=rsem.at[i],
            device_id=dev, device_id_type=MESH,
        )
        copy.start()
        sent.append(copy)
        return i

    def recv(i, slot):
        pltpu.make_async_remote_copy(
            src_ref=slot, dst_ref=slot, send_sem=ssem.at[i], recv_sem=rsem.at[i],
            device_id=core_dev, device_id_type=MESH,
        ).wait_recv()

    hw_copy = pltpu.make_async_copy(hw_ref, hwx.at[0:160], lsem)
    t1_copy = pltpu.make_async_copy(t1_hbm, t1_ref, tsem.at[0])
    t2_copy = pltpu.make_async_copy(t2_hbm, t2_ref, tsem.at[1])
    hw_copy.start()
    t1_copy.start()
    t2_copy.start()

    barrier = pltpu.get_barrier_semaphore()
    greeted = 0
    for k in FAR:
        pl.semaphore_signal(barrier, inc=1, device_id=far_dev(k), device_id_type=MESH)
        pl.semaphore_signal(barrier, inc=1, device_id=y_dev(k), device_id_type=MESH)
        greeted += 2
    for o in NEAR_FROM:
        pl.semaphore_signal(barrier, inc=1, device_id=near_dev(o), device_id_type=MESH)
        greeted += 1
    for k in range(1, 8):
        pl.semaphore_signal(barrier, inc=1, device_id=dp_dev(k), device_id_type=MESH)
        greeted += 1

    hp[...] = jnp.zeros_like(hp)
    hp[:, 0:160] = hid_ref[...].astype(F32)
    G[y, zlo, zhi, 0:64, :] = hp[:, 0:128].astype(BF16)
    G[y, zlo, zhi, 64:80, :] = pack_rest(hp[:, 128:256], 16).astype(BF16)

    TS[...] = jnp.zeros_like(TS)
    lane40 = lanes((1, 40))
    for n in range(2):
        TS[n : n + 1, 0:40] = jnp.where(
            lane40 < count_ref[0:1, n : n + 1], rows_ref[n : n + 1, :], -1
        ).astype(F32)
    turned = jnp.transpose(TS[...])
    row_col = jnp.concatenate([turned[0:40, 0:1], turned[0:40, 1:2]], axis=0).astype(jnp.int32)
    ids[...] = jnp.full((2, 256), -1, jnp.int32)
    ids[0:1, 0:160] = tgt_ref[...]
    ids[1:2, 0:160] = clu_ref[...]
    target = ids[0:1, :]
    cluster = ids[1:2, :]
    slot_hit = lanes((80, 256)) == row_col
    onehot = jnp.where(slot_hit, 1.0, 0.0).astype(BF16)
    live = row_col >= 0
    goal = jnp.sum(jnp.where(slot_hit, target, 0).astype(F32), axis=1, keepdims=True).astype(jnp.int32)
    goal = jnp.where(live, goal, -1)

    hidb = hp[...].astype(BF16)
    chosen = dot(onehot, hidb, NT)
    CH[d, :, 64:128] = jnp.zeros((80, 64), BF16)
    CH[d, :, 0:64] = chosen.astype(BF16)
    part1 = dot(chosen[0:40].astype(BF16), p1_ref[...])
    part2 = dot(chosen[40:80].astype(BF16), p2_ref[...])

    def to_tiles(tiles, a, b):
        for t in range(64):
            at = tiles.at[t // 16, (t // 4) % 4, t % 4]
            i, j = t // 10, t % 10
            if t >= 50:
                at[...] = jnp.zeros((8, 128), F32)
            elif j < 8:
                at[...] = a[8 * i : 8 * i + 8, 128 * j : 128 * j + 128]
            else:
                at[...] = b[8 * i : 8 * i + 8, 128 * j - 1024 : 128 * j - 896]

    to_tiles(PT, part1, part2)

    pl.semaphore_wait(barrier, greeted)

    own = G.at[y, zlo, zhi]
    hid_far = [send(own, own, far_dev(k)) for k in FAR]

    def small_y(tiles, slots):
        return [send(tiles.at[lax.rem(y + k, 4)], slots.at[k - 1], y_dev(k)) for k in FAR]

    def small_near(tiles, slots, ids, sums, nslots):
        for n, i in enumerate(ids):
            recv(i, slots.at[n])
        sums[...] = (tiles[y] + slots[0]) + (slots[1] + slots[2])
        return [
            send(sums.at[lax.rem(zlo + o, 4)], nslots.at[n], near_dev(o))
            for n, o in enumerate(NEAR)
        ]

    def small_far(sums, nslots, ids, sums2, fslots):
        for n, i in enumerate(ids):
            recv(i, nslots.at[n])
        sums2[...] = (sums[zlo] + nslots[0]) + (nslots[1] + nslots[2])
        return [
            send(sums2.at[lax.rem(zhi + k, 4)], fslots.at[k - 1], far_dev(k)) for k in FAR
        ]

    def small_sum_y(sums2, fslots, ids, full):
        for n, i in enumerate(ids):
            recv(i, fslots.at[n])
        full[y, zlo, zhi] = (sums2[zhi] + fslots[0]) + (fslots[1] + fslots[2])
        return [send(full.at[y, zlo, zhi], full.at[y, zlo, zhi], y_dev(k)) for k in FAR]

    def small_spread_far(full, ids):
        for k, i in zip(FAR, ids):
            recv(i, full.at[lax.rem(y + 4 - k, 4), zlo, zhi])
        return [send(full.at[:, zlo, zhi], full.at[:, zlo, zhi], far_dev(k)) for k in FAR]

    def small_spread_near(full, ids):
        for k, i in zip(FAR, ids):
            recv(i, full.at[:, zlo, lax.rem(zhi + 4 - k, 4)])
        return [send(full.at[:, zlo], full.at[:, zlo], near_dev(o)) for o in NEAR]

    def small_sum_far(sums2, fslots, ids, full):
        for n, i in enumerate(ids):
            recv(i, fslots.at[n])
        full[y, zlo, zhi] = (sums2[zhi] + fslots[0]) + (fslots[1] + fslots[2])
        return [send(full.at[y, zlo, zhi], full.at[y, zlo, zhi], far_dev(k)) for k in FAR]

    def small_back_near(full, ids):
        for k, i in zip(FAR, ids):
            recv(i, full.at[y, zlo, lax.rem(zhi + 4 - k, 4)])
        return [send(full.at[y, zlo], full.at[y, zlo], near_dev(o)) for o in NEAR]

    def small_back_y(full, ids):
        for o, i in zip(NEAR, ids):
            recv(i, full.at[y, lax.rem(zlo + 16 - o, 4)])
        return [send(full.at[y], full.at[y], y_dev(k)) for k in FAR]

    def small_done(full, waits):
        for i, yy, zl in waits:
            recv(i, full.at[yy] if zl is None else full.at[yy, zl])
        for t in range(50):
            i, j = t // 10, t % 10
            r, l = (8 * i, 128 * j) if j < 5 else (40 + 8 * i, 128 * j - 640)
            Xf[r : r + 8, l : l + 128] = full[t // 16, (t // 4) % 4, t % 4]

    def dp_x(buf):
        return [send(buf.at[x, c], buf.at[x, c], x_dev(k)) for k in FAR]

    def dp_core(buf, ids):
        for k, i in zip(FAR, ids):
            recv(i, buf.at[lax.rem(x + 4 - k, 4), c])
        return send(buf.at[:, c], buf.at[:, c], core_dev)

    def dp_done(buf, i):
        recv(i, buf.at[:, 1 - c])

    pr_y = small_y(PT, PRY)
    CHv = CH.reshape(4, 2, 80, 128)
    ch_x = dp_x(CHv)

    cw = cw_ref[...].astype(F32)
    row16 = rows_of((16, 4096))
    hwx[160:176, :] = jnp.where(
        row16 == 0, cw[0:1, :], jnp.where(row16 == 1, cw[1:2, :], 0.0)
    ).astype(BF16)
    hwx[176:256, :] = jnp.zeros((80, 4096), BF16)
    hw_copy.wait()

    def turn(j, _):
        at = pl.ds(pl.multiple_of(j * 128, 128), 128)
        hwxT[at, :] = jnp.transpose(hwx[:, at])
        return 0

    def spread(yy, zl):
        for zh in range(4):
            block = G.at[yy, zl, zh]
            base = pl.multiple_of(((zh * 4 + zl) * 4 + yy) * 64, 64)
            WT[pl.ds(base, 64), 0:128] = block[0:64, :]
            packed = block[64:80, :].astype(F32)
            for q in range(4):
                WT[pl.ds(pl.multiple_of(base + 16 * q, 16), 16), 128:256] = unpack_rest(packed, q)

    pr_n = small_near(PT, PRY, pr_y, PS1, PRN)
    lax.fori_loop(0, 8, turn, 0)
    for k, i in zip(FAR, hid_far):
        recv(i, G.at[y, zlo, lax.rem(zhi + 4 - k, 4)])
    hid_near = [send(G.at[y, zlo], G.at[y, zlo], near_dev(o)) for o in NEAR]
    pr_f = small_far(PS1, PRN, pr_n, PS2, PRF)
    hid_y = [[send(G.at[y, zlo], G.at[y, zlo], y_dev(k)) for k in FAR]]
    lax.fori_loop(8, 16, turn, 0)
    pr_by = small_sum_y(PS2, PRF, pr_f, PG)
    for o, i in zip(NEAR, hid_near):
        at = lax.rem(zlo + 16 - o, 4)
        recv(i, G.at[y, at])
        hid_y.append([send(G.at[y, at], G.at[y, at], y_dev(k)) for k in FAR])
    pr_bf = small_spread_far(PG, pr_by)
    lax.fori_loop(16, 24, turn, 0)
    pr_bn = small_spread_near(PG, pr_bf)
    ch_c = dp_core(CHv, ch_x)
    lax.fori_loop(24, 32, turn, 0)
    for zl in range(4):
        spread(y, zl)
    small_done(PG, [(i, slice(None), lax.rem(zlo + 16 - o, 4)) for o, i in zip(NEAR, pr_bn)])
    PJ[d] = Xf[...].astype(BF16)
    PJv = PJ.reshape(4, 2, 80, 640)
    pj_x = dp_x(PJv)

    t1_copy.wait()
    t2_copy.wait()
    left, right = Xf[0:40, :].astype(BF16), Xf[40:80, :].astype(BF16)
    log1 = dot(left, t1_ref[:, 0:640], NT) + dot(right[:, 0:384], t1_ref[:, 640:1024], NT)
    log2 = dot(right[:, 384:640], t2_ref[...], NT)
    L1s[...] = log1
    L2s[...] = log2

    def column_stats(values, goals):
        high = jnp.max(values, axis=1, keepdims=True)
        total = jnp.sum(jnp.exp(values - high), axis=1, keepdims=True)
        hit = lanes(values.shape) == goals
        return high, total, jnp.sum(jnp.where(hit, values, 0.0), axis=1, keepdims=True)

    stat1 = column_stats(log1, goal[0:40] - v * 320)
    stat2 = column_stats(log2, goal[40:80] - v * 1664)
    lane = lanes((80, 128))
    table = jnp.zeros((80, 128), F32)
    for n in range(3):
        table = jnp.where(lane == 3 + n, jnp.concatenate([stat1[n], stat2[n]], axis=0), table)
    TS[0:80, :] = table
    TS[80:128, :] = jnp.zeros((48, 128), F32)
    tail_tile = jnp.transpose(TS[...])[0:8, :]

    for n, ids_y in enumerate(hid_y):
        at = zlo if n == 0 else lax.rem(zlo + 16 - NEAR[n - 1], 4)
        for k, i in zip(FAR, ids_y):
            yy = lax.rem(y + 4 - k, 4)
            recv(i, G.at[yy, at])
            spread(yy, at)

    slices = []
    for k in range(1, 8):
        peer = lax.rem(d + k, 8)
        src = G.at[:, pl.ds(lax.rem(2 * peer, 4), 2), lax.div(peer, 2)]
        slices.append(send(src, HG.at[d], dp_dev(k)))

    LG[...] = dot(hwx[...], WT[...])
    words = LG[0:160, :]
    head_goal = jnp.where(cluster == 0, target, -1) - v * 160
    head_hit = rows_of((160, 256)) == head_goal
    high = jnp.max(words, axis=0, keepdims=True)
    total = jnp.sum(jnp.exp(words - high), axis=0, keepdims=True)
    picked = jnp.sum(jnp.where(head_hit, words, 0.0), axis=0, keepdims=True)
    row8 = rows_of((8, 256))
    wide_tail = jnp.concatenate([tail_tile, jnp.zeros((8, 128), F32)], axis=1)
    tile = jnp.where(
        row8 == 0, high, jnp.where(row8 == 1, total, jnp.where(row8 == 2, picked, wide_tail))
    )

    def join(slots):
        parts = [slots[i] for i in range(4)]
        result = []
        for base in (0, 3):
            m = [p[base : base + 1] for p in parts]
            top = jnp.maximum(jnp.maximum(m[0], m[1]), jnp.maximum(m[2], m[3]))
            s = [p[base + 1 : base + 2] * jnp.exp(mm - top) for p, mm in zip(parts, m)]
            t = [p[base + 2 : base + 3] for p in parts]
            result += [top, (s[0] + s[1]) + (s[2] + s[3]), (t[0] + t[1]) + (t[2] + t[3])]
        return result

    def as_tile(result):
        out = jnp.zeros((8, 256), F32)
        for n in range(6):
            out = jnp.where(row8 == n, result[n], out)
        return out

    STF[zhi] = tile
    near_ids = [send(STF.at[zhi], STF.at[zhi], far_dev(k)) for k in FAR]
    pj_c = dp_core(PJv, pj_x)
    for k, i in zip(FAR, near_ids):
        recv(i, STF.at[lax.rem(zhi + 4 - k, 4)])
    STN[zlo] = as_tile(join(STF))
    near_ids = [send(STN.at[zlo], STN.at[zlo], near_dev(o)) for o in NEAR]
    for o, i in zip(NEAR, near_ids):
        recv(i, STN.at[lax.rem(zlo + 16 - o, 4)])
    STY[y] = as_tile(join(STN))
    near_ids = [send(STY.at[y], STY.at[y], y_dev(k)) for k in FAR]
    for k, i in zip(FAR, near_ids):
        recv(i, STY.at[lax.rem(y + 4 - k, 4)])
    stats = join(STY)

    tail_lse = stats[3] + jnp.log(stats[4])
    TS[...] = jnp.zeros_like(TS)
    TS[0:1, :] = tail_lse[:, 0:128]
    TS[1:2, :] = (tail_lse - stats[5])[:, 0:128]
    columns = jnp.transpose(TS[...])[0:80, :]
    lse_col = jnp.where(live, columns[:, 0:1], 1e30)
    loss_col = columns[:, 1:2]

    def tail_gradient(values, lse, goals):
        hit = (lanes(values.shape) == goals).astype(F32)
        return (SCALE * (jnp.exp(values - lse) - hit)).astype(BF16)

    own1 = tail_gradient(L1s[...], lse_col[0:40], goal[0:40] - v * 320)
    own2 = tail_gradient(L2s[...], lse_col[40:80], jnp.where(live, goal, -(1 << 20))[40:80] - v * 1664)
    back1 = dot(own1, t1_ref[...])
    back2 = dot(own2, t2_ref[...])
    to_tiles(BT, back1, back2)
    bk_y = small_y(BT, BRY)

    INF[d] = jnp.where(lane == 0, lse_col, jnp.where(lane == 1, goal.astype(F32), 0.0))
    INFv = INF.reshape(4, 2, 80, 128)
    inf_x = dp_x(INFv)

    entry0, entry1 = LG[160:161, :], LG[161:162, :]
    top = jnp.maximum(stats[0], jnp.maximum(entry0, entry1))
    summed = stats[1] * jnp.exp(stats[0] - top) + (jnp.exp(entry0 - top) + jnp.exp(entry1 - top))
    lse = top + jnp.log(summed)
    is1, is2 = (cluster == 1).astype(F32), (cluster == 2).astype(F32)
    chosen_logit = stats[2] + (is1 * entry0 + is2 * entry1)
    tail_loss = jnp.sum(jnp.where(slot_hit, loss_col, 0.0), axis=0, keepdims=True)
    loss_ref[...] = ((lse - chosen_logit) + tail_loss)[:, 0:160]

    inside = lanes((160, 256)) < 160
    grad = jnp.where(inside, SCALE * (jnp.exp(LG[0:160, :] - lse) - head_hit.astype(F32)), 0.0)
    inside1 = lanes((1, 256)) < 160
    ge0 = jnp.where(inside1, SCALE * (jnp.exp(entry0 - lse) - is1), 0.0)
    ge1 = jnp.where(inside1, SCALE * (jnp.exp(entry1 - lse) - is2), 0.0)
    GP[d, 0:160, :] = grad[:, 0:128].astype(BF16)
    rounded_rest = grad[:, 128:256]
    GP[d, 160:208, :] = pack_rest(rounded_rest, 48).astype(BF16)
    GPv = GP.reshape(4, 2, 208, 128)
    gp_x = dp_x(GPv)

    row96 = rows_of((96, 256))
    mine = (v == 0).astype(F32)
    low = jnp.where(row96 == 0, ge0 * mine, jnp.where(row96 == 1, ge1 * mine, 0.0))
    grad_ext = jnp.concatenate([grad, low], axis=0).astype(BF16)

    gh_y = []

    def part(o):
        at = lax.rem(zlo + o, 4)
        for zh in range(4):
            rows = pl.ds(pl.multiple_of((zh * 4 + at) * 256, 256), 256)
            product = dot(hwxT[rows, :], grad_ext)
            for yy in range(4):
                block = GB.at[yy, at, zh]
                piece = product[64 * yy : 64 * yy + 64]
                block[0:64, :] = piece[:, 0:128].astype(BF16)
                block[64:80, :] = pack_rest(piece[:, 128:256], 16).astype(BF16)
        gh_y.append(
            [send(GB.at[lax.rem(y + k, 4), at], GRY.at[k - 1, at], y_dev(k)) for k in FAR]
        )

    part(NEAR[0])
    bk_n = small_near(BT, BRY, bk_y, BS1, BRN)
    part(NEAR[1])
    part(NEAR[2])
    bk_f = small_far(BS1, BRN, bk_n, BS2, BRF)
    part(0)
    entries = jnp.where(rows_of((8, 256)) % 2 == 0, ge0, ge1).astype(BF16)
    full = dot(entries, WT[...], NT)
    pair = lax.div(rows_of((8, 1024)), 2)
    packed_cl = jnp.zeros((8, 1024), F32)
    for k in range(4):
        packed_cl = jnp.where(pair == k, full[:, 1024 * k : 1024 * k + 1024], packed_cl)
    GC[d] = packed_cl
    GCv = GC.reshape(4, 2, 8, 1024)
    gc_x = dp_x(GCv)
    bk_bf = small_sum_far(BS2, BRF, bk_f, BG)
    inf_c = dp_core(INFv, inf_x)
    gp_c = dp_core(GPv, gp_x)

    gh_n = []

    def chunk_near(n):
        at = lax.rem(zlo + NEAR[n], 4)
        for k, i in zip(FAR, gh_y[n]):
            recv(i, GRY.at[k - 1, at])
        GS1[n] = (
            (GB[y, at].astype(F32) + GRY[0, at].astype(F32))
            + (GRY[1, at].astype(F32) + GRY[2, at].astype(F32))
        ).astype(BF16)
        gh_n.append(send(GS1.at[n], GRN.at[n], near_dev(NEAR[n])))

    chunk_near(0)
    bk_bn = small_back_near(BG, bk_bf)
    chunk_near(1)
    bk_by = small_back_y(BG, bk_bn)
    chunk_near(2)
    gc_c = dp_core(GCv, gc_x)
    for k, i in zip(FAR, gh_y[3]):
        recv(i, GRY.at[k - 1, zlo])
    mine_sum = (GB[y, zlo].astype(F32) + GRY[0, zlo].astype(F32)) + (
        GRY[1, zlo].astype(F32) + GRY[2, zlo].astype(F32)
    )
    for n, i in enumerate(gh_n):
        recv(i, GRN.at[n])
    GS2[...] = mine_sum + (
        GRN[0].astype(F32) + (GRN[1].astype(F32) + GRN[2].astype(F32))
    )
    for k in FAR:
        GRF[2 + k] = GS2[lax.rem(zhi + k, 4)].astype(BF16)
    gh_f = [send(GRF.at[2 + k], GRF.at[k - 1], far_dev(k)) for k in FAR]
    small_done(BG, [(i, lax.rem(y + 4 - k, 4), None) for k, i in zip(FAR, bk_by)])
    BK[d] = Xf[...].astype(BF16)
    BKv = BK.reshape(4, 2, 80, 640)
    bk_x = dp_x(BKv)

    def assemble(src, dst1, dst2):
        for g in range(8):
            both = src[g].astype(F32)
            dst1[40 * g : 40 * g + 40, 0:640] = both[0:40, :]
            dst1[40 * g : 40 * g + 40, 640:1024] = both[40:80, 0:384]
            dst2[40 * g : 40 * g + 40, :] = both[40:80, 384:640]

    dp_done(PJv, pj_c)
    dp_done(INFv, inf_c)
    assemble(PJ, P1f, P2f)
    P1b[...] = P1f[...].astype(BF16)
    P2b[...] = P2f[...].astype(BF16)

    def gather_column(lo, lane_at):
        return jnp.concatenate([INF[g, lo : lo + 40, lane_at : lane_at + 1] for g in range(8)], axis=0)

    lse1, goal1 = gather_column(0, 0), gather_column(0, 1).astype(jnp.int32)
    all1 = dot(P1b[...], t1_ref[...], NT)
    base1 = jnp.where(goal1 < 0, -(1 << 20), goal1 - v * 320)
    grad1 = tail_gradient(all1, lse1, base1)
    gt1_ref[...] = dot(grad1, P1b[:, pl.ds(pl.multiple_of(d * 128, 128), 128)], TN)

    lse2, goal2 = gather_column(40, 0), gather_column(40, 1).astype(jnp.int32)
    base2 = jnp.where(goal2 < 0, -(1 << 20), goal2 - v * 1664)
    select = jnp.where(lanes((32, 256)) == rows_of((32, 256)) + d * 32, 1.0, 0.0).astype(BF16)
    mine2 = dot(select, P2b[...], NT).astype(BF16)
    P1f[:, 0:128] = jnp.broadcast_to(lse2, (320, 128))
    P1f[:, 128:256] = jnp.broadcast_to(base2.astype(F32), (320, 128))

    def tail_two(j, _):
        at = pl.multiple_of(j * 128, 128)
        logits = dot(P2b[...], t2_ref[pl.ds(at, 128), :], NT)
        hit = (lanes((320, 128)).astype(F32) + (j * 128).astype(F32)) == P1f[:, 128:256]
        grads = (SCALE * (jnp.exp(logits - P1f[:, 0:128]) - hit.astype(F32))).astype(BF16)
        gt2_ref[:, pl.ds(at, 128)] = dot(mine2, grads)
        return 0

    lax.fori_loop(0, 13, tail_two, 0)
    bk_c = dp_core(BKv, bk_x)

    HG[d] = G[:, pl.ds(lax.rem(2 * d, 4), 2), lax.div(d, 2)]
    dp_done(GPv, gp_c)
    for k, i in zip(range(1, 8), slices):
        recv(i, HG.at[lax.rem(d + 8 - k, 8)])
    head_ref[...] = jnp.zeros_like(head_ref)

    def head_group(g, _):
        GU[:, 0:128] = GP[g, 0:160, :]
        rest = GP[g, 160:208, :].astype(F32)
        for q in range(4):
            rows = 48 if q < 3 else 16
            GU[48 * q : 48 * q + rows, 128:256] = unpack_rest(rest[0:rows], q)
        for b in range(8):
            block = HG.at[g, b % 4, b // 4]
            HU[64 * b : 64 * b + 64, 0:128] = block[0:64, :]
            packed = block[64:80, :].astype(F32)
            for q in range(4):
                HU[64 * b + 16 * q : 64 * b + 16 * q + 16, 128:256] = unpack_rest(packed, q)
        head_ref[...] += dot(GU[...], HU[...], NT)
        return 0

    lax.fori_loop(0, 8, head_group, 0)

    dp_done(GCv, gc_c)
    cl_sum = ((GC[0] + GC[1]) + (GC[2] + GC[3])) + ((GC[4] + GC[5]) + (GC[6] + GC[7]))
    for k in range(4):
        cl_ref[:, 1024 * k : 1024 * k + 1024] = cl_sum[2 * k : 2 * k + 2, :]

    both = BK[d].astype(F32)
    b1a, b1b = both[0:40, :].astype(BF16), both[40:80, 0:384].astype(BF16)
    b2 = both[40:80, 384:640].astype(BF16)
    hot1 = jnp.where(slot_hit[0:40], 1.0, 0.0)
    hot2 = jnp.where(slot_hit[40:80], 1.0, 0.0)
    back_one = dot(p1_ref[:, 0:640], b1a, NT) + dot(p1_ref[:, 640:1024], b1b, NT)
    add = dot_exact(back_one, hot1) + dot_exact(dot(p2_ref[...], b2, NT), hot2)
    for n, i in enumerate(gh_f):
        recv(i, GRF.at[n])
    block = GS2[zhi] + (GRF[0].astype(F32) + (GRF[1].astype(F32) + GRF[2].astype(F32)))
    hp[:, 0:128] = block[0:64, :]
    for q in range(4):
        part_q = block[64:80, :]
        hp[16 * q : 16 * q + 16, 128:256] = part_q if q == 0 else pltpu.roll(part_q, 128 - 32 * q, 1)
    gh_ref[...] = (hp[...] + add)[:, 0:160]

    dp_done(CHv, ch_c)
    dp_done(BKv, bk_c)
    assemble(BK, P1f, P2f)
    for g in range(8):
        rows_g = CH[g].astype(F32)
        C1f[40 * g : 40 * g + 40, :] = rows_g[0:40, :]
        C2f[40 * g : 40 * g + 40, :] = rows_g[40:80, :]
    gp1_ref[...] = dot(C1f[...].astype(BF16), P1f[...].astype(BF16), TN)[0:64, :]
    gp2_ref[...] = dot(C2f[...].astype(BF16), P2f[...].astype(BF16), TN)[0:64, :]

    for copy in sent:
        copy.wait_send()


def hand_over(*refs):
    copies = [pltpu.make_async_copy(refs[i], refs[8 + i], refs[16].at[i]) for i in range(8)]
    for copy in copies:
        copy.start()
    for copy in copies:
        copy.wait()


def on_device(
    hidden_states, head_weight, cluster_weight, proj_one, tail_one, proj_two, tail_two,
    targets, token_cluster, tail_rows, tail_counts,
):
    vmem = pl.BlockSpec(memory_space=pltpu.VMEM)
    hbm = pl.BlockSpec(memory_space=pl.ANY)
    shapes = [
        ((1, 160), F32), ((64, 160), F32), ((160, 512), F32), ((2, 4096), F32),
        ((64, 1024), F32), ((320, 128), F32), ((64, 256), F32), ((32, 1664), F32),
    ]
    V = pltpu.VMEM
    scratch = [
        V((320, 1024), BF16), V((1664, 256), BF16), V((2, 256), jnp.int32),
        V((64, 256), F32), V((4, 4, 4, 80, 128), BF16), V((4096, 256), BF16), V((256, 4096), BF16),
        V((4096, 256), BF16), V((8, 4, 2, 80, 128), BF16), V((512, 256), BF16),
        V((8, 80, 128), BF16), V((4, 4, 4, 8, 128), F32), V((3, 4, 4, 8, 128), F32),
        V((3, 4, 8, 128), F32), V((3, 8, 128), F32), V((4, 4, 8, 128), F32), V((4, 8, 128), F32),
        V((4, 4, 4, 8, 128), F32), V((80, 640), F32), V((8, 80, 640), BF16),
        V((320, 1024), F32), V((320, 256), F32), V((320, 1024), BF16), V((320, 256), BF16),
        V((8, 256), F32), V((4, 8, 256), F32), V((4, 8, 256), F32), V((4, 8, 256), F32), V((128, 128), F32),
        V((256, 256), F32), V((40, 320), F32), V((40, 1664), F32), V((8, 80, 128), F32),
        V((8, 208, 128), BF16), V((160, 256), BF16), V((8, 8, 1024), F32),
        V((4, 4, 4, 8, 128), F32), V((3, 4, 4, 8, 128), F32), V((3, 4, 8, 128), F32), V((3, 8, 128), F32),
        V((4, 4, 8, 128), F32), V((4, 8, 128), F32), V((4, 4, 4, 8, 128), F32), V((8, 80, 640), BF16),
        V((320, 128), F32), V((320, 128), F32),
        V((4, 4, 4, 80, 128), BF16), V((3, 4, 4, 80, 128), BF16), V((3, 4, 80, 128), BF16),
        V((3, 4, 80, 128), BF16), V((4, 80, 128), F32), V((6, 80, 128), BF16),
        pltpu.SemaphoreType.DMA((SEMS,)), pltpu.SemaphoreType.DMA((SEMS,)), pltpu.SemaphoreType.DMA,
        pltpu.SemaphoreType.DMA((2,)),
    ]
    out = pl.pallas_call(
        kernel,
        out_shape=[jax.ShapeDtypeStruct(s, t) for s, t in shapes],
        in_specs=[vmem, hbm, vmem, vmem, hbm, vmem, hbm] + [vmem] * 4,
        out_specs=[vmem] * 8,
        scratch_shapes=scratch,
        compiler_params=pltpu.CompilerParams(
            collective_id=0, has_side_effects=True, vmem_limit_bytes=56 * 1024 * 1024
        ),
    )(
        hidden_states.T, head_weight, cluster_weight, proj_one, tail_one, proj_two, tail_two,
        targets.reshape(1, 160), token_cluster.reshape(1, 160), tail_rows[0], tail_counts,
    )
    loss, gh, head, cl, gp1, gt1, gp2, gt2 = pl.pallas_call(
        hand_over,
        out_shape=[jax.ShapeDtypeStruct(s, t) for s, t in shapes],
        in_specs=[hbm] * 8,
        out_specs=[hbm] * 8,
        scratch_shapes=[pltpu.SemaphoreType.DMA((8,))],
    )(*out)
    return (
        loss.reshape(160),
        gh.T,
        head,
        cl,
        gp1,
        gt1,
        gp2,
        gt2.T,
    )


def solution(mesh):
    return jax.shard_map(
        on_device,
        mesh=mesh,
        in_specs=(
            P("dp", "vocab"), P("vocab", None), P(), P("vocab", None), P("vocab", None),
            P("vocab", None), P("vocab", None), P("dp"), P("dp"), P("dp", None, None), P("dp", None),
        ),
        out_specs=(
            P("dp"), P("dp", "vocab"), P("vocab", "dp"), P(), P("vocab", None),
            P("vocab", "dp"), P("vocab", None), P("vocab", "dp"),
        ),
        check_vma=False,
    )
```

```python
import jax
import jax.numpy as jnp
from jax import lax
from jax.experimental import pallas as pl
from jax.experimental.pallas import tpu as pltpu
from jax.sharding import PartitionSpec as P

MESH = pl.DeviceIdType.MESH
F32 = jnp.float32
BF16 = jnp.bfloat16
SCALE = 64.0
FAR = (1, 2, 3)
NEAR = (1, 15, 2)
NEAR_FROM = (15, 1, 14)
SEMS = 128
NT = (((1,), (1,)), ((), ()))
TN = (((0,), (0,)), ((), ()))
NN = (((1,), (0,)), ((), ()))


def dot(a, b, dims=NN):
    return lax.dot_general(a, b, dims, preferred_element_type=F32)


def dot_exact(a, b):
    return lax.dot_general(a, b, NN, precision=lax.Precision.HIGHEST, preferred_element_type=F32)


def lanes(shape):
    return lax.broadcasted_iota(jnp.int32, shape, len(shape) - 1)


def rows_of(shape):
    return lax.broadcasted_iota(jnp.int32, shape, len(shape) - 2)


def pack_rest(rest, height):
    out = None
    total = rest.shape[0]
    for q in range(4):
        lo, hi = q * height, min((q + 1) * height, total)
        part = rest[lo:hi]
        if q:
            part = pltpu.roll(part, 32 * q, 1)
        if hi - lo < height:
            part = jnp.concatenate([part, jnp.zeros((height - (hi - lo), 128), F32)], axis=0)
        out = part if out is None else out + part
    return out


def unpack_rest(packed, q):
    part = packed if q == 0 else pltpu.roll(packed, 128 - 32 * q, 1)
    return jnp.where(lanes(part.shape) < 32, part, 0.0).astype(BF16)


def kernel(
    hid_ref, hw_ref, cw_ref, p1_ref, t1_hbm, p2_ref, t2_hbm, tgt_ref, clu_ref, rows_ref, count_ref,
    loss_ref, gh_ref, head_ref, cl_ref, gp1_ref, gt1_ref, gp2_ref, gt2_ref,
    t1_ref, t2_ref, ids, hp, G, WT, hwx, hwxT, HG, HU,
    CH, PT, PRY, PRN, PRF, PS1, PG, Xf, PJ,
    P1f, P2f, P1b, P2b,
    STF, STN, STY, TTF, TTN, TTY, TS,
    LG, L1s, L2s, INF, GP, GU, GC,
    BT, BRY, BRN, BRF, BS1, BG, BK, C1f, C2f,
    GB, GRY, GS1, GRN, GS2, GRF,
    ssem, rsem, lsem, tsem,
):
    d = lax.axis_index("dp")
    v = lax.axis_index("vocab")
    x, c = lax.div(d, 2), lax.rem(d, 2)
    z, y = lax.div(v, 4), lax.rem(v, 4)
    zhi, zlo = lax.div(z, 4), lax.rem(z, 4)

    def far_dev(k):
        return (d, lax.rem(z + 4 * k, 16) * 4 + y)

    def near_dev(o):
        return (d, lax.rem(z + o, 16) * 4 + y)

    def y_dev(k):
        return (d, z * 4 + lax.rem(y + k, 4))

    def x_dev(k):
        return (lax.rem(x + k, 4) * 2 + c, v)

    core_dev = (x * 2 + 1 - c, v)

    def dp_dev(k):
        return (lax.rem(d + k, 8), v)

    counter = [0]
    sent = []

    def send(src, dst, dev):
        i = counter[0]
        counter[0] += 1
        copy = pltpu.make_async_remote_copy(
            src_ref=src, dst_ref=dst, send_sem=ssem.at[i], recv_sem=rsem.at[i],
            device_id=dev, device_id_type=MESH,
        )
        copy.start()
        sent.append(copy)
        return i

    def recv(i, slot):
        pltpu.make_async_remote_copy(
            src_ref=slot, dst_ref=slot, send_sem=ssem.at[i], recv_sem=rsem.at[i],
            device_id=core_dev, device_id_type=MESH,
        ).wait_recv()

    hw_copy = pltpu.make_async_copy(hw_ref, hwx.at[0:160], lsem)
    t1_copy = pltpu.make_async_copy(t1_hbm, t1_ref, tsem.at[0])
    t2_copy = pltpu.make_async_copy(t2_hbm, t2_ref, tsem.at[1])
    hw_copy.start()
    t1_copy.start()
    t2_copy.start()

    barrier = pltpu.get_barrier_semaphore()
    greeted = 0
    for k in FAR:
        pl.semaphore_signal(barrier, inc=1, device_id=far_dev(k), device_id_type=MESH)
        pl.semaphore_signal(barrier, inc=1, device_id=y_dev(k), device_id_type=MESH)
        greeted += 2
    for o in NEAR_FROM:
        pl.semaphore_signal(barrier, inc=1, device_id=near_dev(o), device_id_type=MESH)
        greeted += 1
    for k in range(1, 8):
        pl.semaphore_signal(barrier, inc=1, device_id=dp_dev(k), device_id_type=MESH)
        greeted += 1

    hp[...] = jnp.zeros_like(hp)
    hp[:, 0:160] = hid_ref[...].astype(F32)
    G[y, zlo, zhi, 0:64, :] = hp[:, 0:128].astype(BF16)
    G[y, zlo, zhi, 64:80, :] = pack_rest(hp[:, 128:256], 16).astype(BF16)

    TS[...] = jnp.zeros_like(TS)
    lane40 = lanes((1, 40))
    for n in range(2):
        TS[n : n + 1, 0:40] = jnp.where(
            lane40 < count_ref[0:1, n : n + 1], rows_ref[n : n + 1, :], -1
        ).astype(F32)
    turned = jnp.transpose(TS[...])
    row_col = jnp.concatenate([turned[0:40, 0:1], turned[0:40, 1:2]], axis=0).astype(jnp.int32)
    ids[...] = jnp.full((2, 256), -1, jnp.int32)
    ids[0:1, 0:160] = tgt_ref[...]
    ids[1:2, 0:160] = clu_ref[...]
    target = ids[0:1, :]
    cluster = ids[1:2, :]
    slot_hit = lanes((80, 256)) == row_col
    onehot = jnp.where(slot_hit, 1.0, 0.0).astype(BF16)
    live = row_col >= 0
    goal = jnp.sum(jnp.where(slot_hit, target, 0).astype(F32), axis=1, keepdims=True).astype(jnp.int32)
    goal = jnp.where(live, goal, -1)

    hidb = hp[...].astype(BF16)
    chosen = dot(onehot, hidb, NT)
    CH[d, :, 64:128] = jnp.zeros((80, 64), BF16)
    CH[d, :, 0:64] = chosen.astype(BF16)
    part1 = dot(chosen[0:40].astype(BF16), p1_ref[...])
    part2 = dot(chosen[40:80].astype(BF16), p2_ref[...])

    def to_tiles(tiles, a, b):
        for t in range(64):
            at = tiles.at[t // 16, (t // 4) % 4, t % 4]
            i, j = t // 10, t % 10
            if t >= 50:
                at[...] = jnp.zeros((8, 128), F32)
            elif j < 8:
                at[...] = a[8 * i : 8 * i + 8, 128 * j : 128 * j + 128]
            else:
                at[...] = b[8 * i : 8 * i + 8, 128 * j - 1024 : 128 * j - 896]

    to_tiles(PT, part1, part2)

    pl.semaphore_wait(barrier, greeted)

    own = G.at[y, zlo, zhi]
    hid_far = [send(own, own, far_dev(k)) for k in FAR]

    def small_y(tiles, slots):
        return [send(tiles.at[lax.rem(y + k, 4)], slots.at[k - 1], y_dev(k)) for k in FAR]

    def small_near(tiles, slots, ids, sums, nslots):
        for n, i in enumerate(ids):
            recv(i, slots.at[n])
        sums[...] = (tiles[y] + slots[0]) + (slots[1] + slots[2])
        return [
            send(sums.at[lax.rem(zlo + o, 4)], nslots.at[n], near_dev(o))
            for n, o in enumerate(NEAR)
        ]

    def small_far(sums, nslots, ids, fslots):
        for n, i in enumerate(ids):
            recv(i, nslots.at[n])
        fslots[zhi] = (sums[zlo] + nslots[0]) + (nslots[1] + nslots[2])
        return [send(fslots.at[zhi], fslots.at[zhi], far_dev(k)) for k in FAR]

    def small_total(fslots, ids, full):
        for k, i in zip(FAR, ids):
            recv(i, fslots.at[lax.rem(zhi + 4 - k, 4)])
        full[y, zlo] = (fslots[0] + fslots[1]) + (fslots[2] + fslots[3])

    def back_y_first(full):
        return [send(full.at[y, zlo], full.at[y, zlo], y_dev(k)) for k in FAR]

    def back_near_second(full, ids):
        for k, i in zip(FAR, ids):
            recv(i, full.at[lax.rem(y + 4 - k, 4), zlo])
        return [send(full.at[:, zlo], full.at[:, zlo], near_dev(o)) for o in NEAR]

    def back_near_first(full):
        return [send(full.at[y, zlo], full.at[y, zlo], near_dev(o)) for o in NEAR]

    def back_y_second(full, ids):
        for o, i in zip(NEAR, ids):
            recv(i, full.at[y, lax.rem(zlo + 16 - o, 4)])
        return [send(full.at[y], full.at[y], y_dev(k)) for k in FAR]

    def small_done(full, waits):
        for i, yy, zl in waits:
            recv(i, full.at[yy] if zl is None else full.at[yy, zl])
        for t in range(50):
            i, j = t // 10, t % 10
            r, l = (8 * i, 128 * j) if j < 5 else (40 + 8 * i, 128 * j - 640)
            Xf[r : r + 8, l : l + 128] = full[t // 16, (t // 4) % 4, t % 4]

    def dp_x(buf):
        return [send(buf.at[x, c], buf.at[x, c], x_dev(k)) for k in FAR]

    def dp_core(buf, ids):
        for k, i in zip(FAR, ids):
            recv(i, buf.at[lax.rem(x + 4 - k, 4), c])
        return send(buf.at[:, c], buf.at[:, c], core_dev)

    def dp_done(buf, i):
        recv(i, buf.at[:, 1 - c])

    pr_y = small_y(PT, PRY)
    CHv = CH.reshape(4, 2, 80, 128)
    ch_x = dp_x(CHv)

    cw = cw_ref[...].astype(F32)
    row16 = rows_of((16, 4096))
    hwx[160:176, :] = jnp.where(
        row16 == 0, cw[0:1, :], jnp.where(row16 == 1, cw[1:2, :], 0.0)
    ).astype(BF16)
    hwx[176:256, :] = jnp.zeros((80, 4096), BF16)
    hw_copy.wait()

    def turn(j, _):
        at = pl.ds(pl.multiple_of(j * 128, 128), 128)
        hwxT[at, :] = jnp.transpose(hwx[:, at])
        return 0

    def spread(yy, zl):
        for zh in range(4):
            block = G.at[yy, zl, zh]
            base = pl.multiple_of(((zh * 4 + zl) * 4 + yy) * 64, 64)
            WT[pl.ds(base, 64), 0:128] = block[0:64, :]
            packed = block[64:80, :].astype(F32)
            for q in range(4):
                WT[pl.ds(pl.multiple_of(base + 16 * q, 16), 16), 128:256] = unpack_rest(packed, q)

    pr_n = small_near(PT, PRY, pr_y, PS1, PRN)
    lax.fori_loop(0, 8, turn, 0)
    pr_f = small_far(PS1, PRN, pr_n, PRF)
    for k, i in zip(FAR, hid_far):
        recv(i, G.at[y, zlo, lax.rem(zhi + 4 - k, 4)])
    hid_near = [send(G.at[y, zlo], G.at[y, zlo], near_dev(o)) for o in NEAR]
    hid_y = [[send(G.at[y, zlo], G.at[y, zlo], y_dev(k)) for k in FAR]]
    lax.fori_loop(8, 20, turn, 0)
    spread(y, zlo)

    def pass_on(n):
        at = lax.rem(zlo + 16 - NEAR[n], 4)
        recv(hid_near[n], G.at[y, at])
        hid_y.append([send(G.at[y, at], G.at[y, at], y_dev(k)) for k in FAR])

    pass_on(0)
    small_total(PRF, pr_f, PG)
    pr_by = back_y_first(PG)
    pass_on(1)
    pass_on(2)
    pr_bn = back_near_second(PG, pr_by)
    ch_c = dp_core(CHv, ch_x)
    lax.fori_loop(20, 32, turn, 0)
    for n in range(3):
        spread(y, lax.rem(zlo + 16 - NEAR[n], 4))
    small_done(PG, [(i, slice(None), lax.rem(zlo + 16 - o, 4)) for o, i in zip(NEAR, pr_bn)])
    PJ[d] = Xf[...].astype(BF16)
    PJv = PJ.reshape(4, 2, 80, 640)
    pj_x = dp_x(PJv)

    t1_copy.wait()
    t2_copy.wait()
    left, right = Xf[0:40, :].astype(BF16), Xf[40:80, :].astype(BF16)
    log1 = dot(left, t1_ref[:, 0:640], NT) + dot(right[:, 0:384], t1_ref[:, 640:1024], NT)
    log2 = dot(right[:, 384:640], t2_ref[...], NT)
    L1s[...] = log1
    L2s[...] = log2

    def column_stats(values, goals):
        high = jnp.max(values, axis=1, keepdims=True)
        total = jnp.sum(jnp.exp(values - high), axis=1, keepdims=True)
        hit = lanes(values.shape) == goals
        return high, total, jnp.sum(jnp.where(hit, values, 0.0), axis=1, keepdims=True)

    stat1 = column_stats(log1, goal[0:40] - v * 320)
    stat2 = column_stats(log2, goal[40:80] - v * 1664)
    lane = lanes((80, 128))
    table = jnp.zeros((80, 128), F32)
    for n in range(3):
        table = jnp.where(lane == n, jnp.concatenate([stat1[n], stat2[n]], axis=0), table)
    TS[0:80, :] = table
    TS[80:128, :] = jnp.zeros((48, 128), F32)
    TTF[zhi] = jnp.transpose(TS[...])[0:8, :]
    tail_ids = [send(TTF.at[zhi], TTF.at[zhi], far_dev(k)) for k in FAR]

    def join(slots):
        parts = [slots[i] for i in range(4)]
        m = [p[0:1] for p in parts]
        top = jnp.maximum(jnp.maximum(m[0], m[1]), jnp.maximum(m[2], m[3]))
        s = [p[1:2] * jnp.exp(mm - top) for p, mm in zip(parts, m)]
        t = [p[2:3] for p in parts]
        return top, (s[0] + s[1]) + (s[2] + s[3]), (t[0] + t[1]) + (t[2] + t[3])

    def as_tile(result):
        row = rows_of((8, result[0].shape[1]))
        return jnp.where(
            row == 0, result[0], jnp.where(row == 1, result[1], jnp.where(row == 2, result[2], 0.0))
        )

    def join_far(far, near, ids):
        for k, i in zip(FAR, ids):
            recv(i, far.at[lax.rem(zhi + 4 - k, 4)])
        near[zlo] = as_tile(join(far))
        return [send(near.at[zlo], near.at[zlo], near_dev(o)) for o in NEAR]

    def join_near(near, last, ids):
        for o, i in zip(NEAR, ids):
            recv(i, near.at[lax.rem(zlo + 16 - o, 4)])
        last[y] = as_tile(join(near))
        return [send(last.at[y], last.at[y], y_dev(k)) for k in FAR]

    def join_last(last, ids):
        for k, i in zip(FAR, ids):
            recv(i, last.at[lax.rem(y + 4 - k, 4)])
        return join(last)


    for n, ids_y in enumerate(hid_y):
        at = zlo if n == 0 else lax.rem(zlo + 16 - NEAR[n - 1], 4)
        for k, i in zip(FAR, ids_y):
            yy = lax.rem(y + 4 - k, 4)
            recv(i, G.at[yy, at])
            spread(yy, at)

    slices = []
    for k in range(1, 8):
        peer = lax.rem(d + k, 8)
        src = G.at[:, pl.ds(lax.rem(2 * peer, 4), 2), lax.div(peer, 2)]
        slices.append(send(src, HG.at[d], dp_dev(k)))

    LG[...] = dot(hwx[...], WT[...])
    words = LG[0:160, :]
    head_goal = jnp.where(cluster == 0, target, -1) - v * 160
    head_hit = rows_of((160, 256)) == head_goal
    high = jnp.max(words, axis=0, keepdims=True)
    total = jnp.sum(jnp.exp(words - high), axis=0, keepdims=True)
    picked = jnp.sum(jnp.where(head_hit, words, 0.0), axis=0, keepdims=True)
    STF[zhi] = as_tile((high, total, picked))
    head_ids = [send(STF.at[zhi], STF.at[zhi], far_dev(k)) for k in FAR]
    tail_ids = join_far(TTF, TTN, tail_ids)
    pj_c = dp_core(PJv, pj_x)
    tail_ids = join_near(TTN, TTY, tail_ids)
    tail_stats = join_last(TTY, tail_ids)

    tail_lse = tail_stats[0] + jnp.log(tail_stats[1])
    TS[...] = jnp.zeros_like(TS)
    TS[0:1, :] = tail_lse
    TS[1:2, :] = tail_lse - tail_stats[2]
    columns = jnp.transpose(TS[...])[0:80, :]
    lse_col = jnp.where(live, columns[:, 0:1], 1e30)
    loss_col = columns[:, 1:2]

    def tail_gradient(values, lse, goals):
        hit = (lanes(values.shape) == goals).astype(F32)
        return (SCALE * (jnp.exp(values - lse) - hit)).astype(BF16)

    own1 = tail_gradient(L1s[...], lse_col[0:40], goal[0:40] - v * 320)
    own2 = tail_gradient(L2s[...], lse_col[40:80], goal[40:80] - v * 1664)
    to_tiles(BT, dot(own1, t1_ref[...]), dot(own2, t2_ref[...]))
    bk_y = small_y(BT, BRY)

    INF[d] = jnp.where(lane == 0, lse_col, jnp.where(lane == 1, goal.astype(F32), 0.0))
    INFv = INF.reshape(4, 2, 80, 128)
    inf_x = dp_x(INFv)
    head_ids = join_far(STF, STN, head_ids)
    bk_n = small_near(BT, BRY, bk_y, BS1, BRN)
    head_ids = join_near(STN, STY, head_ids)
    bk_f = small_far(BS1, BRN, bk_n, BRF)
    stats = join_last(STY, head_ids)

    entry0, entry1 = LG[160:161, :], LG[161:162, :]
    top = jnp.maximum(stats[0], jnp.maximum(entry0, entry1))
    summed = stats[1] * jnp.exp(stats[0] - top) + (jnp.exp(entry0 - top) + jnp.exp(entry1 - top))
    lse = top + jnp.log(summed)
    is1, is2 = (cluster == 1).astype(F32), (cluster == 2).astype(F32)
    chosen_logit = stats[2] + (is1 * entry0 + is2 * entry1)
    tail_loss = jnp.sum(jnp.where(slot_hit, loss_col, 0.0), axis=0, keepdims=True)
    loss_ref[...] = ((lse - chosen_logit) + tail_loss)[:, 0:160]

    inside = lanes((160, 256)) < 160
    grad = jnp.where(inside, SCALE * (jnp.exp(LG[0:160, :] - lse) - head_hit.astype(F32)), 0.0)
    inside1 = lanes((1, 256)) < 160
    ge0 = jnp.where(inside1, SCALE * (jnp.exp(entry0 - lse) - is1), 0.0)
    ge1 = jnp.where(inside1, SCALE * (jnp.exp(entry1 - lse) - is2), 0.0)
    GP[d, 0:160, :] = grad[:, 0:128].astype(BF16)
    rounded_rest = grad[:, 128:256]
    GP[d, 160:208, :] = pack_rest(rounded_rest, 48).astype(BF16)
    GPv = GP.reshape(4, 2, 208, 128)
    gp_x = dp_x(GPv)

    row96 = rows_of((96, 256))
    mine = (v == 0).astype(F32)
    low = jnp.where(row96 == 0, ge0 * mine, jnp.where(row96 == 1, ge1 * mine, 0.0))
    grad_ext = jnp.concatenate([grad, low], axis=0).astype(BF16)

    gh_y = []

    def part(o):
        at = lax.rem(zlo + o, 4)
        for zh in range(4):
            rows = pl.ds(pl.multiple_of((zh * 4 + at) * 256, 256), 256)
            product = dot(hwxT[rows, :], grad_ext)
            for yy in range(4):
                block = GB.at[yy, at, zh]
                piece = product[64 * yy : 64 * yy + 64]
                block[0:64, :] = piece[:, 0:128].astype(BF16)
                block[64:80, :] = pack_rest(piece[:, 128:256], 16).astype(BF16)
        gh_y.append(
            [send(GB.at[lax.rem(y + k, 4), at], GRY.at[k - 1, at], y_dev(k)) for k in FAR]
        )

    part(NEAR[0])
    part(NEAR[1])
    part(NEAR[2])
    part(0)
    entries = jnp.where(rows_of((8, 256)) % 2 == 0, ge0, ge1).astype(BF16)
    full = dot(entries, WT[...], NT)
    pair = lax.div(rows_of((8, 1024)), 2)
    packed_cl = jnp.zeros((8, 1024), F32)
    for k in range(4):
        packed_cl = jnp.where(pair == k, full[:, 1024 * k : 1024 * k + 1024], packed_cl)
    GC[d] = packed_cl
    GCv = GC.reshape(4, 2, 8, 1024)
    gc_x = dp_x(GCv)
    small_total(BRF, bk_f, BG)
    bk_bn = back_near_first(BG)
    inf_c = dp_core(INFv, inf_x)
    gp_c = dp_core(GPv, gp_x)

    gh_n = []

    def chunk_near(n):
        at = lax.rem(zlo + NEAR[n], 4)
        for k, i in zip(FAR, gh_y[n]):
            recv(i, GRY.at[k - 1, at])
        GS1[n] = (
            (GB[y, at].astype(F32) + GRY[0, at].astype(F32))
            + (GRY[1, at].astype(F32) + GRY[2, at].astype(F32))
        ).astype(BF16)
        gh_n.append(send(GS1.at[n], GRN.at[n], near_dev(NEAR[n])))

    chunk_near(0)
    bk_by = back_y_second(BG, bk_bn)
    chunk_near(1)
    chunk_near(2)
    gc_c = dp_core(GCv, gc_x)
    for k, i in zip(FAR, gh_y[3]):
        recv(i, GRY.at[k - 1, zlo])
    mine_sum = (GB[y, zlo].astype(F32) + GRY[0, zlo].astype(F32)) + (
        GRY[1, zlo].astype(F32) + GRY[2, zlo].astype(F32)
    )
    for n, i in enumerate(gh_n):
        recv(i, GRN.at[n])
    GS2[...] = mine_sum + (
        GRN[0].astype(F32) + (GRN[1].astype(F32) + GRN[2].astype(F32))
    )
    for k in FAR:
        GRF[2 + k] = GS2[lax.rem(zhi + k, 4)].astype(BF16)
    gh_f = [send(GRF.at[2 + k], GRF.at[k - 1], far_dev(k)) for k in FAR]
    small_done(BG, [(i, lax.rem(y + 4 - k, 4), None) for k, i in zip(FAR, bk_by)])
    BK[d] = Xf[...].astype(BF16)
    BKv = BK.reshape(4, 2, 80, 640)
    bk_x = dp_x(BKv)

    def assemble(src, dst1, dst2):
        for g in range(8):
            both = src[g].astype(F32)
            dst1[40 * g : 40 * g + 40, 0:640] = both[0:40, :]
            dst1[40 * g : 40 * g + 40, 640:1024] = both[40:80, 0:384]
            dst2[40 * g : 40 * g + 40, :] = both[40:80, 384:640]

    dp_done(PJv, pj_c)
    dp_done(INFv, inf_c)
    assemble(PJ, P1f, P2f)
    P1b[...] = P1f[...].astype(BF16)
    P2b[...] = P2f[...].astype(BF16)

    def gather_column(lo, lane_at):
        return jnp.concatenate([INF[g, lo : lo + 40, lane_at : lane_at + 1] for g in range(8)], axis=0)

    lse1, goal1 = gather_column(0, 0), gather_column(0, 1).astype(jnp.int32)
    all1 = dot(P1b[...], t1_ref[...], NT)
    base1 = jnp.where(goal1 < 0, -(1 << 20), goal1 - v * 320)
    grad1 = tail_gradient(all1, lse1, base1)
    gt1_ref[...] = dot(grad1, P1b[:, pl.ds(pl.multiple_of(d * 128, 128), 128)], TN)

    lse2, goal2 = gather_column(40, 0), gather_column(40, 1).astype(jnp.int32)
    base2 = jnp.where(goal2 < 0, -(1 << 20), goal2 - v * 1664)
    select = jnp.where(lanes((32, 256)) == rows_of((32, 256)) + d * 32, 1.0, 0.0).astype(BF16)
    mine2 = dot(select, P2b[...], NT).astype(BF16)
    P1f[:, 0:128] = jnp.broadcast_to(lse2, (320, 128))
    P1f[:, 128:256] = jnp.broadcast_to(base2.astype(F32), (320, 128))

    def tail_two(j, _):
        at = pl.multiple_of(j * 128, 128)
        logits = dot(P2b[...], t2_ref[pl.ds(at, 128), :], NT)
        hit = (lanes((320, 128)).astype(F32) + (j * 128).astype(F32)) == P1f[:, 128:256]
        grads = (SCALE * (jnp.exp(logits - P1f[:, 0:128]) - hit.astype(F32))).astype(BF16)
        gt2_ref[:, pl.ds(at, 128)] = dot(mine2, grads)
        return 0

    lax.fori_loop(0, 13, tail_two, 0)
    bk_c = dp_core(BKv, bk_x)

    HG[d] = G[:, pl.ds(lax.rem(2 * d, 4), 2), lax.div(d, 2)]
    dp_done(GPv, gp_c)
    for k, i in zip(range(1, 8), slices):
        recv(i, HG.at[lax.rem(d + 8 - k, 8)])
    head_ref[...] = jnp.zeros_like(head_ref)

    def head_group(g, _):
        GU[:, 0:128] = GP[g, 0:160, :]
        rest = GP[g, 160:208, :].astype(F32)
        for q in range(4):
            rows = 48 if q < 3 else 16
            GU[48 * q : 48 * q + rows, 128:256] = unpack_rest(rest[0:rows], q)
        for b in range(8):
            block = HG.at[g, b % 4, b // 4]
            HU[64 * b : 64 * b + 64, 0:128] = block[0:64, :]
            packed = block[64:80, :].astype(F32)
            for q in range(4):
                HU[64 * b + 16 * q : 64 * b + 16 * q + 16, 128:256] = unpack_rest(packed, q)
        head_ref[...] += dot(GU[...], HU[...], NT)
        return 0

    lax.fori_loop(0, 8, head_group, 0)

    dp_done(GCv, gc_c)
    cl_sum = ((GC[0] + GC[1]) + (GC[2] + GC[3])) + ((GC[4] + GC[5]) + (GC[6] + GC[7]))
    for k in range(4):
        cl_ref[:, 1024 * k : 1024 * k + 1024] = cl_sum[2 * k : 2 * k + 2, :]

    both = BK[d].astype(F32)
    b1a, b1b = both[0:40, :].astype(BF16), both[40:80, 0:384].astype(BF16)
    b2 = both[40:80, 384:640].astype(BF16)
    hot1 = jnp.where(slot_hit[0:40], 1.0, 0.0)
    hot2 = jnp.where(slot_hit[40:80], 1.0, 0.0)
    back_one = dot(p1_ref[:, 0:640], b1a, NT) + dot(p1_ref[:, 640:1024], b1b, NT)
    add = dot_exact(back_one, hot1) + dot_exact(dot(p2_ref[...], b2, NT), hot2)
    for n, i in enumerate(gh_f):
        recv(i, GRF.at[n])
    block = GS2[zhi] + (GRF[0].astype(F32) + (GRF[1].astype(F32) + GRF[2].astype(F32)))
    hp[:, 0:128] = block[0:64, :]
    for q in range(4):
        part_q = block[64:80, :]
        hp[16 * q : 16 * q + 16, 128:256] = part_q if q == 0 else pltpu.roll(part_q, 128 - 32 * q, 1)
    gh_ref[...] = (hp[...] + add)[:, 0:160]

    dp_done(CHv, ch_c)
    dp_done(BKv, bk_c)
    assemble(BK, P1f, P2f)
    for g in range(8):
        rows_g = CH[g].astype(F32)
        C1f[40 * g : 40 * g + 40, :] = rows_g[0:40, :]
        C2f[40 * g : 40 * g + 40, :] = rows_g[40:80, :]
    gp1_ref[...] = dot(C1f[...].astype(BF16), P1f[...].astype(BF16), TN)[0:64, :]
    gp2_ref[...] = dot(C2f[...].astype(BF16), P2f[...].astype(BF16), TN)[0:64, :]

    for copy in sent:
        copy.wait_send()


def hand_over(*refs):
    for i in range(8):
        refs[8 + i][...] = refs[i][...]


def on_device(
    hidden_states, head_weight, cluster_weight, proj_one, tail_one, proj_two, tail_two,
    targets, token_cluster, tail_rows, tail_counts,
):
    vmem = pl.BlockSpec(memory_space=pltpu.VMEM)
    hbm = pl.BlockSpec(memory_space=pl.ANY)
    shapes = [
        ((1, 160), F32), ((64, 160), F32), ((160, 512), F32), ((2, 4096), F32),
        ((64, 1024), F32), ((320, 128), F32), ((64, 256), F32), ((32, 1664), F32),
    ]
    V = pltpu.VMEM
    scratch = [
        V((320, 1024), BF16), V((1664, 256), BF16), V((2, 256), jnp.int32),
        V((64, 256), F32), V((4, 4, 4, 80, 128), BF16), V((4096, 256), BF16), V((256, 4096), BF16),
        V((4096, 256), BF16), V((8, 4, 2, 80, 128), BF16), V((512, 256), BF16),
        V((8, 80, 128), BF16), V((4, 4, 4, 8, 128), F32), V((3, 4, 4, 8, 128), F32),
        V((3, 4, 8, 128), F32), V((4, 4, 8, 128), F32), V((4, 4, 8, 128), F32),
        V((4, 4, 4, 8, 128), F32), V((80, 640), F32), V((8, 80, 640), BF16),
        V((320, 1024), F32), V((320, 256), F32), V((320, 1024), BF16), V((320, 256), BF16),
        V((4, 8, 256), F32), V((4, 8, 256), F32), V((4, 8, 256), F32),
        V((4, 8, 128), F32), V((4, 8, 128), F32), V((4, 8, 128), F32), V((128, 128), F32),
        V((256, 256), F32), V((40, 320), F32), V((40, 1664), F32), V((8, 80, 128), F32),
        V((8, 208, 128), BF16), V((160, 256), BF16), V((8, 8, 1024), F32),
        V((4, 4, 4, 8, 128), F32), V((3, 4, 4, 8, 128), F32), V((3, 4, 8, 128), F32), V((4, 4, 8, 128), F32),
        V((4, 4, 8, 128), F32), V((4, 4, 4, 8, 128), F32), V((8, 80, 640), BF16),
        V((320, 128), F32), V((320, 128), F32),
        V((4, 4, 4, 80, 128), BF16), V((3, 4, 4, 80, 128), BF16), V((3, 4, 80, 128), BF16),
        V((3, 4, 80, 128), BF16), V((4, 80, 128), F32), V((6, 80, 128), BF16),
        pltpu.SemaphoreType.DMA((SEMS,)), pltpu.SemaphoreType.DMA((SEMS,)), pltpu.SemaphoreType.DMA,
        pltpu.SemaphoreType.DMA((2,)),
    ]
    out = pl.pallas_call(
        kernel,
        out_shape=[jax.ShapeDtypeStruct(s, t) for s, t in shapes],
        in_specs=[vmem, hbm, vmem, vmem, hbm, vmem, hbm] + [vmem] * 4,
        out_specs=[vmem] * 8,
        scratch_shapes=scratch,
        compiler_params=pltpu.CompilerParams(
            collective_id=0, has_side_effects=True, vmem_limit_bytes=56 * 1024 * 1024
        ),
    )(
        hidden_states.T, head_weight, cluster_weight, proj_one, tail_one, proj_two, tail_two,
        targets.reshape(1, 160), token_cluster.reshape(1, 160), tail_rows[0], tail_counts,
    )
    loss, gh, head, cl, gp1, gt1, gp2, gt2 = pl.pallas_call(
        hand_over,
        out_shape=[jax.ShapeDtypeStruct(s, t) for s, t in shapes],
        in_specs=[vmem] * 8,
        out_specs=[vmem] * 8,
    )(*out)
    return (
        loss.reshape(160),
        gh.T,
        head,
        cl,
        gp1,
        gt1,
        gp2,
        gt2.T,
    )


def solution(mesh):
    return jax.shard_map(
        on_device,
        mesh=mesh,
        in_specs=(
            P("dp", "vocab"), P("vocab", None), P(), P("vocab", None), P("vocab", None),
            P("vocab", None), P("vocab", None), P("dp"), P("dp"), P("dp", None, None), P("dp", None),
        ),
        out_specs=(
            P("dp"), P("dp", "vocab"), P("vocab", "dp"), P(), P("vocab", None),
            P("vocab", "dp"), P("vocab", None), P("vocab", "dp"),
        ),
        check_vma=False,
    )
```

```python
import jax
import jax.numpy as jnp
from jax import lax
from jax.experimental import pallas as pl
from jax.experimental.pallas import tpu as pltpu
from jax.sharding import PartitionSpec as P

MESH = pl.DeviceIdType.MESH
F32 = jnp.float32
BF16 = jnp.bfloat16
SCALE = 64.0
FAR = (1, 2, 3)
NEAR = (1, 15, 2)
OFFS = (8, 7, 9, 6, 10, 5, 11, 4, 12, 3, 13, 14, 2, 15, 1, 0)
SEMS = 144
NT = (((1,), (1,)), ((), ()))
TN = (((0,), (0,)), ((), ()))
NN = (((1,), (0,)), ((), ()))


def dot(a, b, dims=NN):
    return lax.dot_general(a, b, dims, preferred_element_type=F32)


def dot_exact(a, b):
    return lax.dot_general(a, b, NN, precision=lax.Precision.HIGHEST, preferred_element_type=F32)


def lanes(shape):
    return lax.broadcasted_iota(jnp.int32, shape, len(shape) - 1)


def rows_of(shape):
    return lax.broadcasted_iota(jnp.int32, shape, len(shape) - 2)


def pack_rest(rest, height):
    out = None
    total = rest.shape[0]
    for q in range(4):
        lo, hi = q * height, min((q + 1) * height, total)
        part = rest[lo:hi]
        if q:
            part = pltpu.roll(part, 32 * q, 1)
        if hi - lo < height:
            part = jnp.concatenate([part, jnp.zeros((height - (hi - lo), 128), F32)], axis=0)
        out = part if out is None else out + part
    return out


def unpack_rest(packed, q):
    part = packed if q == 0 else pltpu.roll(packed, 128 - 32 * q, 1)
    return jnp.where(lanes(part.shape) < 32, part, 0.0).astype(BF16)


def kernel(
    hid_hbm, hw_ref, cw_ref, p1_hbm, t1_hbm, p2_hbm, t2_hbm, tgt_hbm, clu_hbm, rows_hbm, count_hbm,
    loss_out, gh_out, head_out, cl_out, gp1_out, gt1_out, gp2_out, gt2_out,
    hid_ref, p1_ref, p2_ref, tgt_ref, clu_ref, rows_ref, count_ref,
    loss_ref, gh_ref, head_ref, cl_ref, gp1_ref, gt1_ref, gp2_ref, gt2_ref,
    t1_ref, t2_ref, ids, hp, G, WT, hwx, hwxT, HG, HU,
    CH, PT, PRY, PRN, PRF, PS1, PG, Xf, PJ,
    P1f, P2f, P1b, P2b,
    STF, STN, STY, TTF, TTN, TTY, TS,
    LG, L1s, L2s, INF, GP, GU, GC,
    BT, BRY, BRN, BRF, BS1, BG, BK, C1f, C2f,
    GB, GRY, GZS, GRZ, GS2,
    ssem, rsem, lsem, tsem, isem, osem,
):
    d = lax.axis_index("dp")
    v = lax.axis_index("vocab")
    x, c = lax.div(d, 2), lax.rem(d, 2)
    z, y = lax.div(v, 4), lax.rem(v, 4)
    zhi, zlo = lax.div(z, 4), lax.rem(z, 4)

    def far_dev(k):
        return (d, lax.rem(z + 4 * k, 16) * 4 + y)

    def near_dev(o):
        return (d, lax.rem(z + o, 16) * 4 + y)

    def y_dev(k):
        return (d, z * 4 + lax.rem(y + k, 4))

    def x_dev(k):
        return (lax.rem(x + k, 4) * 2 + c, v)

    core_dev = (x * 2 + 1 - c, v)

    def dp_dev(k):
        return (lax.rem(d + k, 8), v)

    counter = [0]
    sent = []

    def send(src, dst, dev):
        i = counter[0]
        counter[0] += 1
        copy = pltpu.make_async_remote_copy(
            src_ref=src, dst_ref=dst, send_sem=ssem.at[i], recv_sem=rsem.at[i],
            device_id=dev, device_id_type=MESH,
        )
        copy.start()
        sent.append(copy)
        return i

    def recv(i, slot):
        pltpu.make_async_remote_copy(
            src_ref=slot, dst_ref=slot, send_sem=ssem.at[i], recv_sem=rsem.at[i],
            device_id=core_dev, device_id_type=MESH,
        ).wait_recv()

    barrier = pltpu.get_barrier_semaphore()
    greeted = 0
    for k in FAR:
        pl.semaphore_signal(barrier, inc=1, device_id=y_dev(k), device_id_type=MESH)
        greeted += 1
    for o in (8, 7, 9, 6, 10, 5, 11, 4, 12, 3, 13, 2, 14, 1, 15):
        pl.semaphore_signal(barrier, inc=1, device_id=near_dev(o), device_id_type=MESH)
        greeted += 1
    for k in range(1, 8):
        pl.semaphore_signal(barrier, inc=1, device_id=dp_dev(k), device_id_type=MESH)
        greeted += 1

    loads = [
        pltpu.make_async_copy(src, dst, isem.at[n])
        for n, (src, dst) in enumerate(
            (
                (hid_hbm, hid_ref), (rows_hbm, rows_ref), (count_hbm, count_ref), (tgt_hbm, tgt_ref),
                (clu_hbm, clu_ref), (p1_hbm, p1_ref), (p2_hbm, p2_ref),
            )
        )
    ]
    hw_copy = pltpu.make_async_copy(hw_ref, hwx.at[0:160], lsem)
    t1_copy = pltpu.make_async_copy(t1_hbm, t1_ref, tsem.at[0])
    t2_copy = pltpu.make_async_copy(t2_hbm, t2_ref, tsem.at[1])
    for copy in loads:
        copy.start()
    hw_copy.start()
    t1_copy.start()
    t2_copy.start()
    stores = []

    def store(src, dst):
        copy = pltpu.make_async_copy(src, dst, osem.at[len(stores)])
        copy.start()
        stores.append(copy)

    for copy in loads:
        copy.wait()

    hp[...] = jnp.zeros_like(hp)
    hp[:, 0:160] = hid_ref[...].astype(F32)
    G[y, zlo, zhi, 0:64, :] = hp[:, 0:128].astype(BF16)
    G[y, zlo, zhi, 64:80, :] = pack_rest(hp[:, 128:256], 16).astype(BF16)

    TS[...] = jnp.zeros_like(TS)
    lane40 = lanes((1, 40))
    for n in range(2):
        TS[n : n + 1, 0:40] = jnp.where(
            lane40 < count_ref[0:1, n : n + 1], rows_ref[n : n + 1, :], -1
        ).astype(F32)
    turned = jnp.transpose(TS[...])
    row_col = jnp.concatenate([turned[0:40, 0:1], turned[0:40, 1:2]], axis=0).astype(jnp.int32)
    ids[...] = jnp.full((2, 256), -1, jnp.int32)
    ids[0:1, 0:160] = tgt_ref[...]
    ids[1:2, 0:160] = clu_ref[...]
    target = ids[0:1, :]
    cluster = ids[1:2, :]
    slot_hit = lanes((80, 256)) == row_col
    onehot = jnp.where(slot_hit, 1.0, 0.0).astype(BF16)
    live = row_col >= 0
    goal = jnp.sum(jnp.where(slot_hit, target, 0).astype(F32), axis=1, keepdims=True).astype(jnp.int32)
    goal = jnp.where(live, goal, -1)

    hidb = hp[...].astype(BF16)
    chosen = dot(onehot, hidb, NT)
    CH[d, :, 64:128] = jnp.zeros((80, 64), BF16)
    CH[d, :, 0:64] = chosen.astype(BF16)
    part1 = dot(chosen[0:40].astype(BF16), p1_ref[...])
    part2 = dot(chosen[40:80].astype(BF16), p2_ref[...])

    def to_tiles(tiles, a, b):
        for t in range(64):
            at = tiles.at[t // 16, (t // 4) % 4, t % 4]
            i, j = t // 10, t % 10
            if t >= 50:
                at[...] = jnp.zeros((8, 128), F32)
            elif j < 8:
                at[...] = a[8 * i : 8 * i + 8, 128 * j : 128 * j + 128]
            else:
                at[...] = b[8 * i : 8 * i + 8, 128 * j - 1024 : 128 * j - 896]

    to_tiles(PT, part1, part2)

    pl.semaphore_wait(barrier, greeted)

    own = G.at[y, zlo, zhi]
    hid_far = [send(own, own, far_dev(k)) for k in FAR]

    def small_y(tiles, slots):
        return [send(tiles.at[lax.rem(y + k, 4)], slots.at[k - 1], y_dev(k)) for k in FAR]

    def small_near(tiles, slots, ids, sums, nslots):
        for n, i in enumerate(ids):
            recv(i, slots.at[n])
        sums[...] = (tiles[y] + slots[0]) + (slots[1] + slots[2])
        return [
            send(sums.at[lax.rem(zlo + o, 4)], nslots.at[n], near_dev(o))
            for n, o in enumerate(NEAR)
        ]

    def small_far(sums, nslots, ids, fslots):
        for n, i in enumerate(ids):
            recv(i, nslots.at[n])
        fslots[zhi] = (sums[zlo] + nslots[0]) + (nslots[1] + nslots[2])
        return [send(fslots.at[zhi], fslots.at[zhi], far_dev(k)) for k in FAR]

    def small_total(fslots, ids, full):
        for k, i in zip(FAR, ids):
            recv(i, fslots.at[lax.rem(zhi + 4 - k, 4)])
        full[y, zlo] = (fslots[0] + fslots[1]) + (fslots[2] + fslots[3])

    def back_y_first(full):
        return [send(full.at[y, zlo], full.at[y, zlo], y_dev(k)) for k in FAR]

    def back_near_second(full, ids):
        for k, i in zip(FAR, ids):
            recv(i, full.at[lax.rem(y + 4 - k, 4), zlo])
        return [send(full.at[:, zlo], full.at[:, zlo], near_dev(o)) for o in NEAR]

    def back_near_first(full):
        return [send(full.at[y, zlo], full.at[y, zlo], near_dev(o)) for o in NEAR]

    def back_y_second(full, ids):
        for o, i in zip(NEAR, ids):
            recv(i, full.at[y, lax.rem(zlo + 16 - o, 4)])
        return [send(full.at[y], full.at[y], y_dev(k)) for k in FAR]

    def small_done(full, waits):
        for i, yy, zl in waits:
            recv(i, full.at[yy] if zl is None else full.at[yy, zl])
        for t in range(50):
            i, j = t // 10, t % 10
            r, l = (8 * i, 128 * j) if j < 5 else (40 + 8 * i, 128 * j - 640)
            Xf[r : r + 8, l : l + 128] = full[t // 16, (t // 4) % 4, t % 4]

    def dp_x(buf):
        return [send(buf.at[x, c], buf.at[x, c], x_dev(k)) for k in FAR]

    def dp_core(buf, ids):
        for k, i in zip(FAR, ids):
            recv(i, buf.at[lax.rem(x + 4 - k, 4), c])
        return send(buf.at[:, c], buf.at[:, c], core_dev)

    def dp_done(buf, i):
        recv(i, buf.at[:, 1 - c])

    pr_y = small_y(PT, PRY)
    CHv = CH.reshape(4, 2, 80, 128)
    ch_x = dp_x(CHv)

    cw = cw_ref[...].astype(F32)
    row16 = rows_of((16, 4096))
    hwx[160:176, :] = jnp.where(
        row16 == 0, cw[0:1, :], jnp.where(row16 == 1, cw[1:2, :], 0.0)
    ).astype(BF16)
    hwx[176:256, :] = jnp.zeros((80, 4096), BF16)
    hw_copy.wait()

    def turn(j, _):
        at = pl.ds(pl.multiple_of(j * 128, 128), 128)
        hwxT[at, :] = jnp.transpose(hwx[:, at])
        return 0

    def spread(yy, zl):
        for zh in range(4):
            block = G.at[yy, zl, zh]
            base = pl.multiple_of(((zh * 4 + zl) * 4 + yy) * 64, 64)
            WT[pl.ds(base, 64), 0:128] = block[0:64, :]
            packed = block[64:80, :].astype(F32)
            for q in range(4):
                WT[pl.ds(pl.multiple_of(base + 16 * q, 16), 16), 128:256] = unpack_rest(packed, q)

    pr_n = small_near(PT, PRY, pr_y, PS1, PRN)
    lax.fori_loop(0, 8, turn, 0)
    pr_f = small_far(PS1, PRN, pr_n, PRF)
    for k, i in zip(FAR, hid_far):
        recv(i, G.at[y, zlo, lax.rem(zhi + 4 - k, 4)])
    hid_near = [send(G.at[y, zlo], G.at[y, zlo], near_dev(o)) for o in NEAR]
    hid_y = [[send(G.at[y, zlo], G.at[y, zlo], y_dev(k)) for k in FAR]]
    lax.fori_loop(8, 20, turn, 0)
    spread(y, zlo)

    def pass_on(n):
        at = lax.rem(zlo + 16 - NEAR[n], 4)
        recv(hid_near[n], G.at[y, at])
        hid_y.append([send(G.at[y, at], G.at[y, at], y_dev(k)) for k in FAR])

    pass_on(0)
    small_total(PRF, pr_f, PG)
    pr_by = back_y_first(PG)
    pass_on(1)
    pass_on(2)
    pr_bn = back_near_second(PG, pr_by)
    ch_c = dp_core(CHv, ch_x)
    lax.fori_loop(20, 32, turn, 0)
    for n in range(3):
        spread(y, lax.rem(zlo + 16 - NEAR[n], 4))
    small_done(PG, [(i, slice(None), lax.rem(zlo + 16 - o, 4)) for o, i in zip(NEAR, pr_bn)])
    PJ[d] = Xf[...].astype(BF16)
    PJv = PJ.reshape(4, 2, 80, 640)
    pj_x = dp_x(PJv)

    t1_copy.wait()
    t2_copy.wait()
    left, right = Xf[0:40, :].astype(BF16), Xf[40:80, :].astype(BF16)
    log1 = dot(left, t1_ref[:, 0:640], NT) + dot(right[:, 0:384], t1_ref[:, 640:1024], NT)
    log2 = dot(right[:, 384:640], t2_ref[...], NT)
    L1s[...] = log1
    L2s[...] = log2

    def column_stats(values, goals):
        high = jnp.max(values, axis=1, keepdims=True)
        total = jnp.sum(jnp.exp(values - high), axis=1, keepdims=True)
        hit = lanes(values.shape) == goals
        return high, total, jnp.sum(jnp.where(hit, values, 0.0), axis=1, keepdims=True)

    stat1 = column_stats(log1, goal[0:40] - v * 320)
    stat2 = column_stats(log2, goal[40:80] - v * 1664)
    lane = lanes((80, 128))
    table = jnp.zeros((80, 128), F32)
    for n in range(3):
        table = jnp.where(lane == n, jnp.concatenate([stat1[n], stat2[n]], axis=0), table)
    TS[0:80, :] = table
    TS[80:128, :] = jnp.zeros((48, 128), F32)
    TTF[zhi] = jnp.transpose(TS[...])[0:8, :]
    tail_ids = [send(TTF.at[zhi], TTF.at[zhi], far_dev(k)) for k in FAR]

    def join(slots):
        parts = [slots[i] for i in range(4)]
        m = [p[0:1] for p in parts]
        top = jnp.maximum(jnp.maximum(m[0], m[1]), jnp.maximum(m[2], m[3]))
        s = [p[1:2] * jnp.exp(mm - top) for p, mm in zip(parts, m)]
        t = [p[2:3] for p in parts]
        return top, (s[0] + s[1]) + (s[2] + s[3]), (t[0] + t[1]) + (t[2] + t[3])

    def as_tile(result):
        row = rows_of((8, result[0].shape[1]))
        return jnp.where(
            row == 0, result[0], jnp.where(row == 1, result[1], jnp.where(row == 2, result[2], 0.0))
        )

    def join_far(far, near, ids):
        for k, i in zip(FAR, ids):
            recv(i, far.at[lax.rem(zhi + 4 - k, 4)])
        near[zlo] = as_tile(join(far))
        return [send(near.at[zlo], near.at[zlo], near_dev(o)) for o in NEAR]

    def join_near(near, last, ids):
        for o, i in zip(NEAR, ids):
            recv(i, near.at[lax.rem(zlo + 16 - o, 4)])
        last[y] = as_tile(join(near))
        return [send(last.at[y], last.at[y], y_dev(k)) for k in FAR]

    def join_last(last, ids):
        for k, i in zip(FAR, ids):
            recv(i, last.at[lax.rem(y + 4 - k, 4)])
        return join(last)


    for n, ids_y in enumerate(hid_y):
        at = zlo if n == 0 else lax.rem(zlo + 16 - NEAR[n - 1], 4)
        for k, i in zip(FAR, ids_y):
            yy = lax.rem(y + 4 - k, 4)
            recv(i, G.at[yy, at])
            spread(yy, at)

    slices = []
    for k in range(1, 8):
        peer = lax.rem(d + k, 8)
        src = G.at[:, pl.ds(lax.rem(2 * peer, 4), 2), lax.div(peer, 2)]
        slices.append(send(src, HG.at[d], dp_dev(k)))

    LG[...] = dot(hwx[...], WT[...])
    words = LG[0:160, :]
    head_goal = jnp.where(cluster == 0, target, -1) - v * 160
    head_hit = rows_of((160, 256)) == head_goal
    high = jnp.max(words, axis=0, keepdims=True)
    total = jnp.sum(jnp.exp(words - high), axis=0, keepdims=True)
    picked = jnp.sum(jnp.where(head_hit, words, 0.0), axis=0, keepdims=True)
    STF[zhi] = as_tile((high, total, picked))
    head_ids = [send(STF.at[zhi], STF.at[zhi], far_dev(k)) for k in FAR]
    tail_ids = join_far(TTF, TTN, tail_ids)
    pj_c = dp_core(PJv, pj_x)
    tail_ids = join_near(TTN, TTY, tail_ids)
    head_ids = join_far(STF, STN, head_ids)
    tail_stats = join_last(TTY, tail_ids)

    tail_lse = tail_stats[0] + jnp.log(tail_stats[1])
    TS[...] = jnp.zeros_like(TS)
    TS[0:1, :] = tail_lse
    TS[1:2, :] = tail_lse - tail_stats[2]
    columns = jnp.transpose(TS[...])[0:80, :]
    lse_col = jnp.where(live, columns[:, 0:1], 1e30)
    loss_col = columns[:, 1:2]

    def tail_gradient(values, lse, goals):
        hit = (lanes(values.shape) == goals).astype(F32)
        return (SCALE * (jnp.exp(values - lse) - hit)).astype(BF16)

    own1 = tail_gradient(L1s[...], lse_col[0:40], goal[0:40] - v * 320)
    own2 = tail_gradient(L2s[...], lse_col[40:80], goal[40:80] - v * 1664)
    to_tiles(BT, dot(own1, t1_ref[...]), dot(own2, t2_ref[...]))
    bk_y = small_y(BT, BRY)

    head_ids = join_near(STN, STY, head_ids)
    INF[d] = jnp.where(lane == 0, lse_col, jnp.where(lane == 1, goal.astype(F32), 0.0))
    INFv = INF.reshape(4, 2, 80, 128)
    inf_x = dp_x(INFv)
    bk_n = small_near(BT, BRY, bk_y, BS1, BRN)
    stats = join_last(STY, head_ids)

    entry0, entry1 = LG[160:161, :], LG[161:162, :]
    top = jnp.maximum(stats[0], jnp.maximum(entry0, entry1))
    summed = stats[1] * jnp.exp(stats[0] - top) + (jnp.exp(entry0 - top) + jnp.exp(entry1 - top))
    lse = top + jnp.log(summed)
    is1, is2 = (cluster == 1).astype(F32), (cluster == 2).astype(F32)
    chosen_logit = stats[2] + (is1 * entry0 + is2 * entry1)
    tail_loss = jnp.sum(jnp.where(slot_hit, loss_col, 0.0), axis=0, keepdims=True)
    loss_ref[...] = ((lse - chosen_logit) + tail_loss)[:, 0:160]
    store(loss_ref, loss_out)

    inside = lanes((160, 256)) < 160
    grad = jnp.where(inside, SCALE * (jnp.exp(LG[0:160, :] - lse) - head_hit.astype(F32)), 0.0)
    inside1 = lanes((1, 256)) < 160
    ge0 = jnp.where(inside1, SCALE * (jnp.exp(entry0 - lse) - is1), 0.0)
    ge1 = jnp.where(inside1, SCALE * (jnp.exp(entry1 - lse) - is2), 0.0)
    GP[d, 0:160, :] = grad[:, 0:128].astype(BF16)
    rounded_rest = grad[:, 128:256]
    GP[d, 160:208, :] = pack_rest(rounded_rest, 48).astype(BF16)
    GPv = GP.reshape(4, 2, 208, 128)
    gp_x = dp_x(GPv)

    row96 = rows_of((96, 256))
    mine = (v == 0).astype(F32)
    low = jnp.where(row96 == 0, ge0 * mine, jnp.where(row96 == 1, ge1 * mine, 0.0))
    grad_ext = jnp.concatenate([grad, low], axis=0).astype(BF16)

    gh_y = []

    def part(n):
        for j in range(4 * n, 4 * n + 4):
            zz = lax.rem(z + OFFS[j], 16)
            product = dot(hwxT[pl.ds(pl.multiple_of(zz * 256, 256), 256), :], grad_ext)
            for yy in range(4):
                block = GB.at[yy, j]
                piece = product[64 * yy : 64 * yy + 64]
                block[0:64, :] = piece[:, 0:128].astype(BF16)
                block[64:80, :] = pack_rest(piece[:, 128:256], 16).astype(BF16)
        at = pl.ds(4 * n, 4)
        gh_y.append(
            [send(GB.at[lax.rem(y + k, 4), at], GRY.at[k - 1, at], y_dev(k)) for k in FAR]
        )

    part(0)
    part(1)
    bk_f = small_far(BS1, BRN, bk_n, BRF)
    part(2)
    part(3)
    entries = jnp.where(rows_of((8, 256)) % 2 == 0, ge0, ge1).astype(BF16)
    full = dot(entries, WT[...], NT)
    pair = lax.div(rows_of((8, 1024)), 2)
    packed_cl = jnp.zeros((8, 1024), F32)
    for k in range(4):
        packed_cl = jnp.where(pair == k, full[:, 1024 * k : 1024 * k + 1024], packed_cl)
    GC[d] = packed_cl
    GCv = GC.reshape(4, 2, 8, 1024)
    gc_x = dp_x(GCv)
    inf_c = dp_core(INFv, inf_x)
    gp_c = dp_core(GPv, gp_x)

    gh_z = []

    def chunk_z(n):
        at = pl.ds(4 * n, 4)
        for k, i in zip(FAR, gh_y[n]):
            recv(i, GRY.at[k - 1, at])
        for j in range(4 * n, 4 * n + 4):
            total = (GB[y, j].astype(F32) + GRY[0, j].astype(F32)) + (
                GRY[1, j].astype(F32) + GRY[2, j].astype(F32)
            )
            if OFFS[j]:
                GZS[j] = total.astype(BF16)
                gh_z.append(send(GZS.at[j], GRZ.at[j], near_dev(OFFS[j])))
            else:
                GS2[...] = total

    chunk_z(0)
    small_total(BRF, bk_f, BG)
    bk_bn = back_near_first(BG)
    chunk_z(1)
    bk_by = back_y_second(BG, bk_bn)
    chunk_z(2)
    gc_c = dp_core(GCv, gc_x)
    chunk_z(3)
    small_done(BG, [(i, lax.rem(y + 4 - k, 4), None) for k, i in zip(FAR, bk_by)])
    BK[d] = Xf[...].astype(BF16)
    BKv = BK.reshape(4, 2, 80, 640)
    bk_x = dp_x(BKv)

    def assemble(src, dst1, dst2):
        for g in range(8):
            both = src[g].astype(F32)
            dst1[40 * g : 40 * g + 40, 0:640] = both[0:40, :]
            dst1[40 * g : 40 * g + 40, 640:1024] = both[40:80, 0:384]
            dst2[40 * g : 40 * g + 40, :] = both[40:80, 384:640]

    dp_done(PJv, pj_c)
    dp_done(INFv, inf_c)
    assemble(PJ, P1f, P2f)
    P1b[...] = P1f[...].astype(BF16)
    P2b[...] = P2f[...].astype(BF16)

    def gather_column(lo, lane_at):
        return jnp.concatenate([INF[g, lo : lo + 40, lane_at : lane_at + 1] for g in range(8)], axis=0)

    lse1, goal1 = gather_column(0, 0), gather_column(0, 1).astype(jnp.int32)
    all1 = dot(P1b[...], t1_ref[...], NT)
    base1 = jnp.where(goal1 < 0, -(1 << 20), goal1 - v * 320)
    grad1 = tail_gradient(all1, lse1, base1)
    gt1_ref[...] = dot(grad1, P1b[:, pl.ds(pl.multiple_of(d * 128, 128), 128)], TN)
    store(gt1_ref, gt1_out)

    lse2, goal2 = gather_column(40, 0), gather_column(40, 1).astype(jnp.int32)
    base2 = jnp.where(goal2 < 0, -(1 << 20), goal2 - v * 1664)
    select = jnp.where(lanes((32, 256)) == rows_of((32, 256)) + d * 32, 1.0, 0.0).astype(BF16)
    mine2 = dot(select, P2b[...], NT).astype(BF16)
    P1f[:, 0:128] = jnp.broadcast_to(lse2, (320, 128))
    P1f[:, 128:256] = jnp.broadcast_to(base2.astype(F32), (320, 128))

    def tail_two(j, _):
        at = pl.multiple_of(j * 128, 128)
        logits = dot(P2b[...], t2_ref[pl.ds(at, 128), :], NT)
        hit = (lanes((320, 128)).astype(F32) + (j * 128).astype(F32)) == P1f[:, 128:256]
        grads = (SCALE * (jnp.exp(logits - P1f[:, 0:128]) - hit.astype(F32))).astype(BF16)
        gt2_ref[:, pl.ds(at, 128)] = dot(mine2, grads)
        return 0

    lax.fori_loop(0, 13, tail_two, 0)
    store(gt2_ref, gt2_out)
    bk_c = dp_core(BKv, bk_x)

    HG[d] = G[:, pl.ds(lax.rem(2 * d, 4), 2), lax.div(d, 2)]
    dp_done(GPv, gp_c)
    for k, i in zip(range(1, 8), slices):
        recv(i, HG.at[lax.rem(d + 8 - k, 8)])
    head_ref[...] = jnp.zeros_like(head_ref)

    def head_group(g, _):
        GU[:, 0:128] = GP[g, 0:160, :]
        rest = GP[g, 160:208, :].astype(F32)
        for q in range(4):
            rows = 48 if q < 3 else 16
            GU[48 * q : 48 * q + rows, 128:256] = unpack_rest(rest[0:rows], q)
        for b in range(8):
            block = HG.at[g, b % 4, b // 4]
            HU[64 * b : 64 * b + 64, 0:128] = block[0:64, :]
            packed = block[64:80, :].astype(F32)
            for q in range(4):
                HU[64 * b + 16 * q : 64 * b + 16 * q + 16, 128:256] = unpack_rest(packed, q)
        head_ref[...] += dot(GU[...], HU[...], NT)
        return 0

    lax.fori_loop(0, 8, head_group, 0)
    store(head_ref, head_out)

    dp_done(GCv, gc_c)
    cl_sum = ((GC[0] + GC[1]) + (GC[2] + GC[3])) + ((GC[4] + GC[5]) + (GC[6] + GC[7]))
    for k in range(4):
        cl_ref[:, 1024 * k : 1024 * k + 1024] = cl_sum[2 * k : 2 * k + 2, :]
    store(cl_ref, cl_out)

    both = BK[d].astype(F32)
    b1a, b1b = both[0:40, :].astype(BF16), both[40:80, 0:384].astype(BF16)
    b2 = both[40:80, 384:640].astype(BF16)
    hot1 = jnp.where(slot_hit[0:40], 1.0, 0.0)
    hot2 = jnp.where(slot_hit[40:80], 1.0, 0.0)
    back_one = dot(p1_ref[:, 0:640], b1a, NT) + dot(p1_ref[:, 640:1024], b1b, NT)
    add = dot_exact(back_one, hot1) + dot_exact(dot(p2_ref[...], b2, NT), hot2)
    block = GS2[...]
    for j, i in enumerate(gh_z):
        recv(i, GRZ.at[j])
        block = block + GRZ[j].astype(F32)
    hp[:, 0:128] = block[0:64, :]
    for q in range(4):
        part_q = block[64:80, :]
        hp[16 * q : 16 * q + 16, 128:256] = part_q if q == 0 else pltpu.roll(part_q, 128 - 32 * q, 1)
    gh_ref[...] = (hp[...] + add)[:, 0:160]
    store(gh_ref, gh_out)

    dp_done(CHv, ch_c)
    dp_done(BKv, bk_c)
    assemble(BK, P1f, P2f)
    for g in range(8):
        rows_g = CH[g].astype(F32)
        C1f[40 * g : 40 * g + 40, :] = rows_g[0:40, :]
        C2f[40 * g : 40 * g + 40, :] = rows_g[40:80, :]
    gp1_ref[...] = dot(C1f[...].astype(BF16), P1f[...].astype(BF16), TN)[0:64, :]
    store(gp1_ref, gp1_out)
    gp2_ref[...] = dot(C2f[...].astype(BF16), P2f[...].astype(BF16), TN)[0:64, :]
    store(gp2_ref, gp2_out)
    for copy in stores:
        copy.wait()

    for copy in sent:
        copy.wait_send()


def hand_over(*refs):
    for i in range(8):
        refs[8 + i][...] = refs[i][...]


def on_device(
    hidden_states, head_weight, cluster_weight, proj_one, tail_one, proj_two, tail_two,
    targets, token_cluster, tail_rows, tail_counts,
):
    vmem = pl.BlockSpec(memory_space=pltpu.VMEM)
    hbm = pl.BlockSpec(memory_space=pl.ANY)
    shapes = [
        ((1, 160), F32), ((64, 160), F32), ((160, 512), F32), ((2, 4096), F32),
        ((64, 1024), F32), ((320, 128), F32), ((64, 256), F32), ((32, 1664), F32),
    ]
    V = pltpu.VMEM
    scratch = [
        V((64, 160), BF16), V((64, 1024), BF16), V((64, 256), BF16), V((1, 160), jnp.int32),
        V((1, 160), jnp.int32), V((2, 40), jnp.int32), V((1, 2), jnp.int32),
    ] + [V(s, t) for s, t in shapes] + [
        V((320, 1024), BF16), V((1664, 256), BF16), V((2, 256), jnp.int32),
        V((64, 256), F32), V((4, 4, 4, 80, 128), BF16), V((4096, 256), BF16), V((256, 4096), BF16),
        V((4096, 256), BF16), V((8, 4, 2, 80, 128), BF16), V((512, 256), BF16),
        V((8, 80, 128), BF16), V((4, 4, 4, 8, 128), F32), V((3, 4, 4, 8, 128), F32),
        V((3, 4, 8, 128), F32), V((4, 4, 8, 128), F32), V((4, 4, 8, 128), F32),
        V((4, 4, 4, 8, 128), F32), V((80, 640), F32), V((8, 80, 640), BF16),
        V((320, 1024), F32), V((320, 256), F32), V((320, 1024), BF16), V((320, 256), BF16),
        V((4, 8, 256), F32), V((4, 8, 256), F32), V((4, 8, 256), F32),
        V((4, 8, 128), F32), V((4, 8, 128), F32), V((4, 8, 128), F32), V((128, 128), F32),
        V((256, 256), F32), V((40, 320), F32), V((40, 1664), F32), V((8, 80, 128), F32),
        V((8, 208, 128), BF16), V((160, 256), BF16), V((8, 8, 1024), F32),
        V((4, 4, 4, 8, 128), F32), V((3, 4, 4, 8, 128), F32), V((3, 4, 8, 128), F32), V((4, 4, 8, 128), F32),
        V((4, 4, 8, 128), F32), V((4, 4, 4, 8, 128), F32), V((8, 80, 640), BF16),
        V((320, 128), F32), V((320, 128), F32),
        V((4, 16, 80, 128), BF16), V((3, 16, 80, 128), BF16), V((16, 80, 128), BF16),
        V((16, 80, 128), BF16), V((80, 128), F32),
        pltpu.SemaphoreType.DMA((SEMS,)), pltpu.SemaphoreType.DMA((SEMS,)), pltpu.SemaphoreType.DMA,
        pltpu.SemaphoreType.DMA((2,)), pltpu.SemaphoreType.DMA((7,)), pltpu.SemaphoreType.DMA((8,)),
    ]
    out = pl.pallas_call(
        kernel,
        out_shape=[jax.ShapeDtypeStruct(s, t) for s, t in shapes],
        in_specs=[hbm, hbm, vmem] + [hbm] * 8,
        out_specs=[hbm] * 8,
        scratch_shapes=scratch,
        compiler_params=pltpu.CompilerParams(
            collective_id=0, has_side_effects=True, vmem_limit_bytes=56 * 1024 * 1024
        ),
    )(
        hidden_states.T, head_weight, cluster_weight, proj_one, tail_one, proj_two, tail_two,
        targets.reshape(1, 160), token_cluster.reshape(1, 160), tail_rows[0], tail_counts,
    )
    loss, gh, head, cl, gp1, gt1, gp2, gt2 = pl.pallas_call(
        hand_over,
        out_shape=[jax.ShapeDtypeStruct(s, t) for s, t in shapes],
        in_specs=[vmem] * 8,
        out_specs=[vmem] * 8,
    )(*out)
    return (
        loss.reshape(160),
        gh.T,
        head,
        cl,
        gp1,
        gt1,
        gp2,
        gt2.T,
    )


def solution(mesh):
    return jax.shard_map(
        on_device,
        mesh=mesh,
        in_specs=(
            P("dp", "vocab"), P("vocab", None), P(), P("vocab", None), P("vocab", None),
            P("vocab", None), P("vocab", None), P("dp"), P("dp"), P("dp", None, None), P("dp", None),
        ),
        out_specs=(
            P("dp"), P("dp", "vocab"), P("vocab", "dp"), P(), P("vocab", None),
            P("vocab", "dp"), P("vocab", None), P("vocab", "dp"),
        ),
        check_vma=False,
    )
```

```python
import jax
import jax.numpy as jnp
from jax import lax
from jax.experimental import pallas as pl
from jax.experimental.pallas import tpu as pltpu
from jax.sharding import PartitionSpec as P

MESH = pl.DeviceIdType.MESH
F32 = jnp.float32
BF16 = jnp.bfloat16
SCALE = 64.0
FAR = (1, 2, 3)
NEAR = (1, 15, 2)
OFFS = (8, 7, 9, 6, 10, 5, 11, 4, 12, 3, 13, 14, 2, 15, 1, 0)
SEMS = 144
NT = (((1,), (1,)), ((), ()))
TN = (((0,), (0,)), ((), ()))
NN = (((1,), (0,)), ((), ()))


def dot(a, b, dims=NN):
    return lax.dot_general(a, b, dims, preferred_element_type=F32)


def dot_exact(a, b):
    return lax.dot_general(a, b, NN, precision=lax.Precision.HIGHEST, preferred_element_type=F32)


def lanes(shape):
    return lax.broadcasted_iota(jnp.int32, shape, len(shape) - 1)


def rows_of(shape):
    return lax.broadcasted_iota(jnp.int32, shape, len(shape) - 2)


def pack_rest(rest, height):
    out = None
    total = rest.shape[0]
    for q in range(4):
        lo, hi = q * height, min((q + 1) * height, total)
        part = rest[lo:hi]
        if q:
            part = pltpu.roll(part, 32 * q, 1)
        if hi - lo < height:
            part = jnp.concatenate([part, jnp.zeros((height - (hi - lo), 128), F32)], axis=0)
        out = part if out is None else out + part
    return out


def unpack_rest(packed, q):
    part = packed if q == 0 else pltpu.roll(packed, 128 - 32 * q, 1)
    return jnp.where(lanes(part.shape) < 32, part, 0.0).astype(BF16)


def kernel(
    hid_hbm, hw_ref, cw_ref, p1_hbm, t1_hbm, p2_hbm, t2_hbm, tgt_hbm, clu_hbm, rows_hbm, count_hbm,
    loss_out, gh_out, head_out, cl_out, gp1_out, gt1_out, gp2_out, gt2_out,
    hid_ref, p1_ref, p2_ref, tgt_ref, clu_ref, rows_ref, count_ref,
    loss_ref, gh_ref, head_ref, cl_ref, gp1_ref, gt1_ref, gp2_ref, gt2_ref,
    t1_ref, t2_ref, ids, hp, G, WT, hwx, hwxT, HG, HU,
    CH, PT, PRY, PRN, PRF, PS1, PG, Xf, PJ,
    P1f, P2f, P1b, P2b,
    STF, STN, STY, TTF, TTN, TTY, TS,
    LG, L1s, L2s, INF, GP, GU, GC,
    BT, BRY, BRN, BRF, BS1, BG, BK, C1f, C2f,
    GB, GRY, GZS, GRZ, GS2,
    ssem, rsem, lsem, tsem, isem, osem,
):
    d = lax.axis_index("dp")
    v = lax.axis_index("vocab")
    x, c = lax.div(d, 2), lax.rem(d, 2)
    z, y = lax.div(v, 4), lax.rem(v, 4)
    zhi, zlo = lax.div(z, 4), lax.rem(z, 4)

    def far_dev(k):
        return (d, lax.rem(z + 4 * k, 16) * 4 + y)

    def near_dev(o):
        return (d, lax.rem(z + o, 16) * 4 + y)

    def y_dev(k):
        return (d, z * 4 + lax.rem(y + k, 4))

    def x_dev(k):
        return (lax.rem(x + k, 4) * 2 + c, v)

    core_dev = (x * 2 + 1 - c, v)

    def dp_dev(k):
        return (lax.rem(d + k, 8), v)

    counter = [0]
    sent = []

    def send(src, dst, dev):
        i = counter[0]
        counter[0] += 1
        copy = pltpu.make_async_remote_copy(
            src_ref=src, dst_ref=dst, send_sem=ssem.at[i], recv_sem=rsem.at[i],
            device_id=dev, device_id_type=MESH,
        )
        copy.start()
        sent.append(copy)
        return i

    def recv(i, slot):
        pltpu.make_async_remote_copy(
            src_ref=slot, dst_ref=slot, send_sem=ssem.at[i], recv_sem=rsem.at[i],
            device_id=core_dev, device_id_type=MESH,
        ).wait_recv()

    barrier = pltpu.get_barrier_semaphore()
    greeted = 0
    for k in FAR:
        pl.semaphore_signal(barrier, inc=1, device_id=y_dev(k), device_id_type=MESH)
        greeted += 1
    for o in (8, 7, 9, 6, 10, 5, 11, 4, 12, 3, 13, 2, 14, 1, 15):
        pl.semaphore_signal(barrier, inc=1, device_id=near_dev(o), device_id_type=MESH)
        greeted += 1
    for k in range(1, 8):
        pl.semaphore_signal(barrier, inc=1, device_id=dp_dev(k), device_id_type=MESH)
        greeted += 1

    loads = [
        pltpu.make_async_copy(src, dst, isem.at[n])
        for n, (src, dst) in enumerate(
            (
                (hid_hbm, hid_ref), (rows_hbm, rows_ref), (count_hbm, count_ref), (tgt_hbm, tgt_ref),
                (clu_hbm, clu_ref), (p1_hbm, p1_ref), (p2_hbm, p2_ref),
            )
        )
    ]
    hw_copy = pltpu.make_async_copy(hw_ref, hwx.at[0:160], lsem)
    t1_copy = pltpu.make_async_copy(t1_hbm, t1_ref, tsem.at[0])
    t2_copy = pltpu.make_async_copy(t2_hbm, t2_ref, tsem.at[1])
    for copy in loads:
        copy.start()
    hw_copy.start()
    t1_copy.start()
    t2_copy.start()
    stores = []

    def store(src, dst):
        copy = pltpu.make_async_copy(src, dst, osem.at[len(stores)])
        copy.start()
        stores.append(copy)

    for copy in loads:
        copy.wait()

    hp[...] = jnp.zeros_like(hp)
    hp[:, 0:160] = hid_ref[...].astype(F32)
    G[y, zlo, zhi, 0:64, :] = hp[:, 0:128].astype(BF16)
    G[y, zlo, zhi, 64:80, :] = pack_rest(hp[:, 128:256], 16).astype(BF16)

    TS[...] = jnp.zeros_like(TS)
    lane40 = lanes((1, 40))
    for n in range(2):
        TS[n : n + 1, 0:40] = jnp.where(
            lane40 < count_ref[0:1, n : n + 1], rows_ref[n : n + 1, :], -1
        ).astype(F32)
    turned = jnp.transpose(TS[...])
    row_col = jnp.concatenate([turned[0:40, 0:1], turned[0:40, 1:2]], axis=0).astype(jnp.int32)
    ids[...] = jnp.full((2, 256), -1, jnp.int32)
    ids[0:1, 0:160] = tgt_ref[...]
    ids[1:2, 0:160] = clu_ref[...]
    target = ids[0:1, :]
    cluster = ids[1:2, :]
    slot_hit = lanes((80, 256)) == row_col
    onehot = jnp.where(slot_hit, 1.0, 0.0).astype(BF16)
    live = row_col >= 0
    goal = jnp.sum(jnp.where(slot_hit, target, 0).astype(F32), axis=1, keepdims=True).astype(jnp.int32)
    goal = jnp.where(live, goal, -1)

    hidb = hp[...].astype(BF16)
    chosen = dot(onehot, hidb, NT)
    CH[d, :, 64:128] = jnp.zeros((80, 64), BF16)
    CH[d, :, 0:64] = chosen.astype(BF16)
    part1 = dot(chosen[0:40].astype(BF16), p1_ref[...])
    part2 = dot(chosen[40:80].astype(BF16), p2_ref[...])

    def to_tiles(tiles, a, b):
        for t in range(64):
            at = tiles.at[t // 16, (t // 4) % 4, t % 4]
            i, j = t // 10, t % 10
            if t >= 50:
                at[...] = jnp.zeros((8, 128), F32)
            elif j < 8:
                at[...] = a[8 * i : 8 * i + 8, 128 * j : 128 * j + 128]
            else:
                at[...] = b[8 * i : 8 * i + 8, 128 * j - 1024 : 128 * j - 896]

    to_tiles(PT, part1, part2)

    pl.semaphore_wait(barrier, greeted)

    own = G.at[y, zlo, zhi]
    hid_far = [send(own, own, far_dev(k)) for k in FAR]

    def small_y(tiles, slots):
        return [send(tiles.at[lax.rem(y + k, 4)], slots.at[k - 1], y_dev(k)) for k in FAR]

    def small_near(tiles, slots, ids, sums, nslots):
        for n, i in enumerate(ids):
            recv(i, slots.at[n])
        sums[...] = (tiles[y] + slots[0]) + (slots[1] + slots[2])
        return [
            send(sums.at[lax.rem(zlo + o, 4)], nslots.at[n], near_dev(o))
            for n, o in enumerate(NEAR)
        ]

    def small_far(sums, nslots, ids, fslots):
        for n, i in enumerate(ids):
            recv(i, nslots.at[n])
        fslots[zhi] = (sums[zlo] + nslots[0]) + (nslots[1] + nslots[2])
        return [send(fslots.at[zhi], fslots.at[zhi], far_dev(k)) for k in FAR]

    def small_total(fslots, ids, full):
        for k, i in zip(FAR, ids):
            recv(i, fslots.at[lax.rem(zhi + 4 - k, 4)])
        full[y, zlo] = (fslots[0] + fslots[1]) + (fslots[2] + fslots[3])

    def back_y_first(full):
        return [send(full.at[y, zlo], full.at[y, zlo], y_dev(k)) for k in FAR]

    def back_near_second(full, ids):
        for k, i in zip(FAR, ids):
            recv(i, full.at[lax.rem(y + 4 - k, 4), zlo])
        return [send(full.at[:, zlo], full.at[:, zlo], near_dev(o)) for o in NEAR]

    def back_near_first(full):
        return [send(full.at[y, zlo], full.at[y, zlo], near_dev(o)) for o in NEAR]

    def back_y_second(full, ids):
        for o, i in zip(NEAR, ids):
            recv(i, full.at[y, lax.rem(zlo + 16 - o, 4)])
        return [send(full.at[y], full.at[y], y_dev(k)) for k in FAR]

    def small_done(full, waits):
        for i, yy, zl in waits:
            recv(i, full.at[yy] if zl is None else full.at[yy, zl])
        for t in range(50):
            i, j = t // 10, t % 10
            r, l = (8 * i, 128 * j) if j < 5 else (40 + 8 * i, 128 * j - 640)
            Xf[r : r + 8, l : l + 128] = full[t // 16, (t // 4) % 4, t % 4]

    def dp_x(buf):
        return [send(buf.at[x, c], buf.at[x, c], x_dev(k)) for k in FAR]

    def dp_core(buf, ids):
        for k, i in zip(FAR, ids):
            recv(i, buf.at[lax.rem(x + 4 - k, 4), c])
        return send(buf.at[:, c], buf.at[:, c], core_dev)

    def dp_done(buf, i):
        recv(i, buf.at[:, 1 - c])

    pr_y = small_y(PT, PRY)
    CHv = CH.reshape(4, 2, 80, 128)
    ch_x = dp_x(CHv)

    cw = cw_ref[...].astype(F32)
    row16 = rows_of((16, 4096))
    hwx[160:176, :] = jnp.where(
        row16 == 0, cw[0:1, :], jnp.where(row16 == 1, cw[1:2, :], 0.0)
    ).astype(BF16)
    hwx[176:256, :] = jnp.zeros((80, 4096), BF16)
    hw_copy.wait()

    def turn(j, _):
        at = pl.ds(pl.multiple_of(j * 128, 128), 128)
        hwxT[at, :] = jnp.transpose(hwx[:, at])
        return 0

    def spread(yy, zl):
        for zh in range(4):
            block = G.at[yy, zl, zh]
            base = pl.multiple_of(((zh * 4 + zl) * 4 + yy) * 64, 64)
            WT[pl.ds(base, 64), 0:128] = block[0:64, :]
            packed = block[64:80, :].astype(F32)
            for q in range(4):
                WT[pl.ds(pl.multiple_of(base + 16 * q, 16), 16), 128:256] = unpack_rest(packed, q)

    pr_n = small_near(PT, PRY, pr_y, PS1, PRN)
    lax.fori_loop(0, 8, turn, 0)
    pr_f = small_far(PS1, PRN, pr_n, PRF)
    for k, i in zip(FAR, hid_far):
        recv(i, G.at[y, zlo, lax.rem(zhi + 4 - k, 4)])
    hid_near = [send(G.at[y, zlo], G.at[y, zlo], near_dev(o)) for o in NEAR]
    hid_y = [[send(G.at[y, zlo], G.at[y, zlo], y_dev(k)) for k in FAR]]
    lax.fori_loop(8, 20, turn, 0)
    spread(y, zlo)

    def pass_on(n):
        at = lax.rem(zlo + 16 - NEAR[n], 4)
        recv(hid_near[n], G.at[y, at])
        hid_y.append([send(G.at[y, at], G.at[y, at], y_dev(k)) for k in FAR])

    pass_on(0)
    small_total(PRF, pr_f, PG)
    pr_by = back_y_first(PG)
    pass_on(1)
    pass_on(2)
    pr_bn = back_near_second(PG, pr_by)
    ch_c = dp_core(CHv, ch_x)
    lax.fori_loop(20, 32, turn, 0)
    for n in range(3):
        spread(y, lax.rem(zlo + 16 - NEAR[n], 4))
    small_done(PG, [(i, slice(None), lax.rem(zlo + 16 - o, 4)) for o, i in zip(NEAR, pr_bn)])
    PJ[d] = Xf[...].astype(BF16)
    PJv = PJ.reshape(4, 2, 80, 640)
    pj_x = dp_x(PJv)

    t1_copy.wait()
    t2_copy.wait()
    left, right = Xf[0:40, :].astype(BF16), Xf[40:80, :].astype(BF16)
    log1 = dot(left, t1_ref[:, 0:640], NT) + dot(right[:, 0:384], t1_ref[:, 640:1024], NT)
    log2 = dot(right[:, 384:640], t2_ref[...], NT)
    L1s[...] = log1
    L2s[...] = log2

    def column_stats(values, goals):
        high = jnp.max(values, axis=1, keepdims=True)
        total = jnp.sum(jnp.exp(values - high), axis=1, keepdims=True)
        hit = lanes(values.shape) == goals
        return high, total, jnp.sum(jnp.where(hit, values, 0.0), axis=1, keepdims=True)

    stat1 = column_stats(log1, goal[0:40] - v * 320)
    stat2 = column_stats(log2, goal[40:80] - v * 1664)
    lane = lanes((80, 128))
    table = jnp.zeros((80, 128), F32)
    for n in range(3):
        table = jnp.where(lane == n, jnp.concatenate([stat1[n], stat2[n]], axis=0), table)
    TS[0:80, :] = table
    TS[80:128, :] = jnp.zeros((48, 128), F32)
    TTF[zhi] = jnp.transpose(TS[...])[0:8, :]
    tail_ids = [send(TTF.at[zhi], TTF.at[zhi], far_dev(k)) for k in FAR]

    def join(slots):
        parts = [slots[i] for i in range(4)]
        m = [p[0:1] for p in parts]
        top = jnp.maximum(jnp.maximum(m[0], m[1]), jnp.maximum(m[2], m[3]))
        s = [p[1:2] * jnp.exp(mm - top) for p, mm in zip(parts, m)]
        t = [p[2:3] for p in parts]
        return top, (s[0] + s[1]) + (s[2] + s[3]), (t[0] + t[1]) + (t[2] + t[3])

    def as_tile(result):
        row = rows_of((8, result[0].shape[1]))
        return jnp.where(
            row == 0, result[0], jnp.where(row == 1, result[1], jnp.where(row == 2, result[2], 0.0))
        )

    def join_far(far, near, ids):
        for k, i in zip(FAR, ids):
            recv(i, far.at[lax.rem(zhi + 4 - k, 4)])
        near[zlo] = as_tile(join(far))
        return [send(near.at[zlo], near.at[zlo], near_dev(o)) for o in NEAR]

    def join_near(near, last, ids):
        for o, i in zip(NEAR, ids):
            recv(i, near.at[lax.rem(zlo + 16 - o, 4)])
        last[y] = as_tile(join(near))
        return [send(last.at[y], last.at[y], y_dev(k)) for k in FAR]

    def join_last(last, ids):
        for k, i in zip(FAR, ids):
            recv(i, last.at[lax.rem(y + 4 - k, 4)])
        return join(last)


    for n, ids_y in enumerate(hid_y):
        at = zlo if n == 0 else lax.rem(zlo + 16 - NEAR[n - 1], 4)
        for k, i in zip(FAR, ids_y):
            yy = lax.rem(y + 4 - k, 4)
            recv(i, G.at[yy, at])
            spread(yy, at)

    slices = []
    for k in range(1, 8):
        peer = lax.rem(d + k, 8)
        src = G.at[:, pl.ds(lax.rem(2 * peer, 4), 2), lax.div(peer, 2)]
        slices.append(send(src, HG.at[d], dp_dev(k)))

    LG[...] = dot(hwx[...], WT[...])
    words = LG[0:160, :]
    head_goal = jnp.where(cluster == 0, target, -1) - v * 160
    head_hit = rows_of((160, 256)) == head_goal
    high = jnp.max(words, axis=0, keepdims=True)
    total = jnp.sum(jnp.exp(words - high), axis=0, keepdims=True)
    picked = jnp.sum(jnp.where(head_hit, words, 0.0), axis=0, keepdims=True)
    STF[zhi] = as_tile((high, total, picked))
    head_ids = [send(STF.at[zhi], STF.at[zhi], far_dev(k)) for k in FAR]
    tail_ids = join_far(TTF, TTN, tail_ids)
    pj_c = dp_core(PJv, pj_x)
    tail_ids = join_near(TTN, TTY, tail_ids)
    head_ids = join_far(STF, STN, head_ids)
    tail_stats = join_last(TTY, tail_ids)

    tail_lse = tail_stats[0] + jnp.log(tail_stats[1])
    TS[...] = jnp.zeros_like(TS)
    TS[0:1, :] = tail_lse
    TS[1:2, :] = tail_lse - tail_stats[2]
    columns = jnp.transpose(TS[...])[0:80, :]
    lse_col = jnp.where(live, columns[:, 0:1], 1e30)
    loss_col = columns[:, 1:2]

    def tail_gradient(values, lse, goals):
        hit = (lanes(values.shape) == goals).astype(F32)
        return (SCALE * (jnp.exp(values - lse) - hit)).astype(BF16)

    own1 = tail_gradient(L1s[...], lse_col[0:40], goal[0:40] - v * 320)
    own2 = tail_gradient(L2s[...], lse_col[40:80], goal[40:80] - v * 1664)
    to_tiles(BT, dot(own1, t1_ref[...]), dot(own2, t2_ref[...]))
    bk_y = small_y(BT, BRY)

    head_ids = join_near(STN, STY, head_ids)
    INF[d] = jnp.where(lane == 0, lse_col, jnp.where(lane == 1, goal.astype(F32), 0.0))
    INFv = INF.reshape(4, 2, 80, 128)
    inf_x = dp_x(INFv)
    bk_n = small_near(BT, BRY, bk_y, BS1, BRN)
    stats = join_last(STY, head_ids)

    entry0, entry1 = LG[160:161, :], LG[161:162, :]
    top = jnp.maximum(stats[0], jnp.maximum(entry0, entry1))
    summed = stats[1] * jnp.exp(stats[0] - top) + (jnp.exp(entry0 - top) + jnp.exp(entry1 - top))
    lse = top + jnp.log(summed)
    is1, is2 = (cluster == 1).astype(F32), (cluster == 2).astype(F32)
    chosen_logit = stats[2] + (is1 * entry0 + is2 * entry1)
    tail_loss = jnp.sum(jnp.where(slot_hit, loss_col, 0.0), axis=0, keepdims=True)
    loss_ref[...] = ((lse - chosen_logit) + tail_loss)[:, 0:160]
    store(loss_ref, loss_out)

    inside = lanes((160, 256)) < 160
    grad = jnp.where(inside, SCALE * (jnp.exp(LG[0:160, :] - lse) - head_hit.astype(F32)), 0.0)
    inside1 = lanes((1, 256)) < 160
    ge0 = jnp.where(inside1, SCALE * (jnp.exp(entry0 - lse) - is1), 0.0)
    ge1 = jnp.where(inside1, SCALE * (jnp.exp(entry1 - lse) - is2), 0.0)
    GP[d, 0:160, :] = grad[:, 0:128].astype(BF16)
    rounded_rest = grad[:, 128:256]
    GP[d, 160:208, :] = pack_rest(rounded_rest, 48).astype(BF16)
    GPv = GP.reshape(4, 2, 208, 128)
    gp_x = dp_x(GPv)

    row96 = rows_of((96, 256))
    mine = (v == 0).astype(F32)
    low = jnp.where(row96 == 0, ge0 * mine, jnp.where(row96 == 1, ge1 * mine, 0.0))
    grad_ext = jnp.concatenate([grad, low], axis=0).astype(BF16)

    gh_y = []

    def part(n):
        for j in range(4 * n, 4 * n + 4):
            zz = lax.rem(z + OFFS[j], 16)
            product = dot(hwxT[pl.ds(pl.multiple_of(zz * 256, 256), 256), :], grad_ext)
            for yy in range(4):
                block = GB.at[yy, j]
                piece = product[64 * yy : 64 * yy + 64]
                block[0:64, :] = piece[:, 0:128].astype(BF16)
                block[64:80, :] = pack_rest(piece[:, 128:256], 16).astype(BF16)
        at = pl.ds(4 * n, 4)
        gh_y.append(
            [send(GB.at[lax.rem(y + k, 4), at], GRY.at[k - 1, at], y_dev(k)) for k in FAR]
        )

    part(0)
    part(1)
    bk_f = small_far(BS1, BRN, bk_n, BRF)
    part(2)
    part(3)
    entries = jnp.where(rows_of((8, 256)) % 2 == 0, ge0, ge1).astype(BF16)
    full = dot(entries, WT[...], NT)
    pair = lax.div(rows_of((8, 1024)), 2)
    packed_cl = jnp.zeros((8, 1024), F32)
    for k in range(4):
        packed_cl = jnp.where(pair == k, full[:, 1024 * k : 1024 * k + 1024], packed_cl)
    GC[d] = packed_cl
    GCv = GC.reshape(4, 2, 8, 1024)
    gc_x = dp_x(GCv)
    inf_c = dp_core(INFv, inf_x)
    gp_c = dp_core(GPv, gp_x)

    gh_z = []

    def chunk_z(n):
        at = pl.ds(4 * n, 4)
        for k, i in zip(FAR, gh_y[n]):
            recv(i, GRY.at[k - 1, at])
        for j in range(4 * n, 4 * n + 4):
            total = (GB[y, j].astype(F32) + GRY[0, j].astype(F32)) + (
                GRY[1, j].astype(F32) + GRY[2, j].astype(F32)
            )
            if OFFS[j]:
                GZS[j] = total.astype(BF16)
                gh_z.append(send(GZS.at[j], GRZ.at[j], near_dev(OFFS[j])))
            else:
                GS2[...] = total

    chunk_z(0)
    def assemble(src, dst1, dst2):
        for g in range(8):
            both = src[g].astype(F32)
            dst1[40 * g : 40 * g + 40, 0:640] = both[0:40, :]
            dst1[40 * g : 40 * g + 40, 640:1024] = both[40:80, 0:384]
            dst2[40 * g : 40 * g + 40, :] = both[40:80, 384:640]

    dp_done(PJv, pj_c)
    dp_done(INFv, inf_c)
    assemble(PJ, P1f, P2f)
    P1b[...] = P1f[...].astype(BF16)
    P2b[...] = P2f[...].astype(BF16)

    def gather_column(lo, lane_at):
        return jnp.concatenate([INF[g, lo : lo + 40, lane_at : lane_at + 1] for g in range(8)], axis=0)

    lse1, goal1 = gather_column(0, 0), gather_column(0, 1).astype(jnp.int32)
    all1 = dot(P1b[...], t1_ref[...], NT)
    base1 = jnp.where(goal1 < 0, -(1 << 20), goal1 - v * 320)
    grad1 = tail_gradient(all1, lse1, base1)
    gt1_ref[...] = dot(grad1, P1b[:, pl.ds(pl.multiple_of(d * 128, 128), 128)], TN)
    store(gt1_ref, gt1_out)

    lse2, goal2 = gather_column(40, 0), gather_column(40, 1).astype(jnp.int32)
    base2 = jnp.where(goal2 < 0, -(1 << 20), goal2 - v * 1664)
    select = jnp.where(lanes((32, 256)) == rows_of((32, 256)) + d * 32, 1.0, 0.0).astype(BF16)
    mine2 = dot(select, P2b[...], NT).astype(BF16)
    P1f[:, 0:128] = jnp.broadcast_to(lse2, (320, 128))
    P1f[:, 128:256] = jnp.broadcast_to(base2.astype(F32), (320, 128))

    def tail_two(j, _):
        at = pl.multiple_of(j * 128, 128)
        logits = dot(P2b[...], t2_ref[pl.ds(at, 128), :], NT)
        hit = (lanes((320, 128)).astype(F32) + (j * 128).astype(F32)) == P1f[:, 128:256]
        grads = (SCALE * (jnp.exp(logits - P1f[:, 0:128]) - hit.astype(F32))).astype(BF16)
        gt2_ref[:, pl.ds(at, 128)] = dot(mine2, grads)
        return 0

    chunk_z(1)
    small_total(BRF, bk_f, BG)
    bk_bn = back_near_first(BG)
    lax.fori_loop(0, 7, tail_two, 0)
    chunk_z(2)
    bk_by = back_y_second(BG, bk_bn)
    gc_c = dp_core(GCv, gc_x)
    lax.fori_loop(7, 13, tail_two, 0)
    store(gt2_ref, gt2_out)
    chunk_z(3)
    HG[d] = G[:, pl.ds(lax.rem(2 * d, 4), 2), lax.div(d, 2)]
    dp_done(GPv, gp_c)
    for k, i in zip(range(1, 8), slices):
        recv(i, HG.at[lax.rem(d + 8 - k, 8)])
    head_ref[...] = jnp.zeros_like(head_ref)

    def head_group(g, _):
        GU[:, 0:128] = GP[g, 0:160, :]
        rest = GP[g, 160:208, :].astype(F32)
        for q in range(4):
            rows = 48 if q < 3 else 16
            GU[48 * q : 48 * q + rows, 128:256] = unpack_rest(rest[0:rows], q)
        for b in range(8):
            block = HG.at[g, b % 4, b // 4]
            HU[64 * b : 64 * b + 64, 0:128] = block[0:64, :]
            packed = block[64:80, :].astype(F32)
            for q in range(4):
                HU[64 * b + 16 * q : 64 * b + 16 * q + 16, 128:256] = unpack_rest(packed, q)
        head_ref[...] += dot(GU[...], HU[...], NT)
        return 0

    lax.fori_loop(0, 8, head_group, 0)
    store(head_ref, head_out)

    small_done(BG, [(i, lax.rem(y + 4 - k, 4), None) for k, i in zip(FAR, bk_by)])
    BK[d] = Xf[...].astype(BF16)
    BKv = BK.reshape(4, 2, 80, 640)
    bk_x = dp_x(BKv)

    dp_done(GCv, gc_c)
    cl_sum = ((GC[0] + GC[1]) + (GC[2] + GC[3])) + ((GC[4] + GC[5]) + (GC[6] + GC[7]))
    for k in range(4):
        cl_ref[:, 1024 * k : 1024 * k + 1024] = cl_sum[2 * k : 2 * k + 2, :]
    store(cl_ref, cl_out)

    both = BK[d].astype(F32)
    b1a, b1b = both[0:40, :].astype(BF16), both[40:80, 0:384].astype(BF16)
    b2 = both[40:80, 384:640].astype(BF16)
    hot1 = jnp.where(slot_hit[0:40], 1.0, 0.0)
    hot2 = jnp.where(slot_hit[40:80], 1.0, 0.0)
    back_one = dot(p1_ref[:, 0:640], b1a, NT) + dot(p1_ref[:, 640:1024], b1b, NT)
    add = dot_exact(back_one, hot1) + dot_exact(dot(p2_ref[...], b2, NT), hot2)
    block = GS2[...]
    for j, i in enumerate(gh_z):
        recv(i, GRZ.at[j])
        block = block + GRZ[j].astype(F32)
    hp[:, 0:128] = block[0:64, :]
    for q in range(4):
        part_q = block[64:80, :]
        hp[16 * q : 16 * q + 16, 128:256] = part_q if q == 0 else pltpu.roll(part_q, 128 - 32 * q, 1)
    gh_ref[...] = (hp[...] + add)[:, 0:160]
    store(gh_ref, gh_out)

    bk_c = dp_core(BKv, bk_x)

    dp_done(CHv, ch_c)
    dp_done(BKv, bk_c)
    assemble(BK, P1f, P2f)
    for g in range(8):
        rows_g = CH[g].astype(F32)
        C1f[40 * g : 40 * g + 40, :] = rows_g[0:40, :]
        C2f[40 * g : 40 * g + 40, :] = rows_g[40:80, :]
    gp1_ref[...] = dot(C1f[...].astype(BF16), P1f[...].astype(BF16), TN)[0:64, :]
    store(gp1_ref, gp1_out)
    gp2_ref[...] = dot(C2f[...].astype(BF16), P2f[...].astype(BF16), TN)[0:64, :]
    store(gp2_ref, gp2_out)
    for copy in stores:
        copy.wait()

    for copy in sent:
        copy.wait_send()


def hand_over(*refs):
    for i in range(8):
        refs[8 + i][...] = refs[i][...]


def on_device(
    hidden_states, head_weight, cluster_weight, proj_one, tail_one, proj_two, tail_two,
    targets, token_cluster, tail_rows, tail_counts,
):
    vmem = pl.BlockSpec(memory_space=pltpu.VMEM)
    hbm = pl.BlockSpec(memory_space=pl.ANY)
    shapes = [
        ((1, 160), F32), ((64, 160), F32), ((160, 512), F32), ((2, 4096), F32),
        ((64, 1024), F32), ((320, 128), F32), ((64, 256), F32), ((32, 1664), F32),
    ]
    V = pltpu.VMEM
    scratch = [
        V((64, 160), BF16), V((64, 1024), BF16), V((64, 256), BF16), V((1, 160), jnp.int32),
        V((1, 160), jnp.int32), V((2, 40), jnp.int32), V((1, 2), jnp.int32),
    ] + [V(s, t) for s, t in shapes] + [
        V((320, 1024), BF16), V((1664, 256), BF16), V((2, 256), jnp.int32),
        V((64, 256), F32), V((4, 4, 4, 80, 128), BF16), V((4096, 256), BF16), V((256, 4096), BF16),
        V((4096, 256), BF16), V((8, 4, 2, 80, 128), BF16), V((512, 256), BF16),
        V((8, 80, 128), BF16), V((4, 4, 4, 8, 128), F32), V((3, 4, 4, 8, 128), F32),
        V((3, 4, 8, 128), F32), V((4, 4, 8, 128), F32), V((4, 4, 8, 128), F32),
        V((4, 4, 4, 8, 128), F32), V((80, 640), F32), V((8, 80, 640), BF16),
        V((320, 1024), F32), V((320, 256), F32), V((320, 1024), BF16), V((320, 256), BF16),
        V((4, 8, 256), F32), V((4, 8, 256), F32), V((4, 8, 256), F32),
        V((4, 8, 128), F32), V((4, 8, 128), F32), V((4, 8, 128), F32), V((128, 128), F32),
        V((256, 256), F32), V((40, 320), F32), V((40, 1664), F32), V((8, 80, 128), F32),
        V((8, 208, 128), BF16), V((160, 256), BF16), V((8, 8, 1024), F32),
        V((4, 4, 4, 8, 128), F32), V((3, 4, 4, 8, 128), F32), V((3, 4, 8, 128), F32), V((4, 4, 8, 128), F32),
        V((4, 4, 8, 128), F32), V((4, 4, 4, 8, 128), F32), V((8, 80, 640), BF16),
        V((320, 128), F32), V((320, 128), F32),
        V((4, 16, 80, 128), BF16), V((3, 16, 80, 128), BF16), V((16, 80, 128), BF16),
        V((16, 80, 128), BF16), V((80, 128), F32),
        pltpu.SemaphoreType.DMA((SEMS,)), pltpu.SemaphoreType.DMA((SEMS,)), pltpu.SemaphoreType.DMA,
        pltpu.SemaphoreType.DMA((2,)), pltpu.SemaphoreType.DMA((7,)), pltpu.SemaphoreType.DMA((8,)),
    ]
    out = pl.pallas_call(
        kernel,
        out_shape=[jax.ShapeDtypeStruct(s, t) for s, t in shapes],
        in_specs=[hbm, hbm, vmem] + [hbm] * 8,
        out_specs=[hbm] * 8,
        scratch_shapes=scratch,
        compiler_params=pltpu.CompilerParams(
            collective_id=0, has_side_effects=True, vmem_limit_bytes=56 * 1024 * 1024
        ),
    )(
        hidden_states.T, head_weight, cluster_weight, proj_one, tail_one, proj_two, tail_two,
        targets.reshape(1, 160), token_cluster.reshape(1, 160), tail_rows[0], tail_counts,
    )
    loss, gh, head, cl, gp1, gt1, gp2, gt2 = pl.pallas_call(
        hand_over,
        out_shape=[jax.ShapeDtypeStruct(s, t) for s, t in shapes],
        in_specs=[vmem] * 8,
        out_specs=[vmem] * 8,
    )(*out)
    return (
        loss.reshape(160),
        gh.T,
        head,
        cl,
        gp1,
        gt1,
        gp2,
        gt2.T,
    )


def solution(mesh):
    return jax.shard_map(
        on_device,
        mesh=mesh,
        in_specs=(
            P("dp", "vocab"), P("vocab", None), P(), P("vocab", None), P("vocab", None),
            P("vocab", None), P("vocab", None), P("dp"), P("dp"), P("dp", None, None), P("dp", None),
        ),
        out_specs=(
            P("dp"), P("dp", "vocab"), P("vocab", "dp"), P(), P("vocab", None),
            P("vocab", "dp"), P("vocab", None), P("vocab", "dp"),
        ),
        check_vma=False,
    )
```

```python
import jax
import jax.numpy as jnp
from jax import lax
from jax.experimental import pallas as pl
from jax.experimental.pallas import tpu as pltpu
from jax.sharding import PartitionSpec as P

MESH = pl.DeviceIdType.MESH
F32 = jnp.float32
BF16 = jnp.bfloat16
SCALE = 64.0
FAR = (1, 2, 3)
NEAR = (1, 15, 2)
NEAR_FROM = (15, 1, 14)
SEMS = 144
NT = (((1,), (1,)), ((), ()))
TN = (((0,), (0,)), ((), ()))
NN = (((1,), (0,)), ((), ()))


def dot(a, b, dims=NN):
    return lax.dot_general(a, b, dims, preferred_element_type=F32)


def dot_exact(a, b):
    return lax.dot_general(a, b, NN, precision=lax.Precision.HIGHEST, preferred_element_type=F32)


def lanes(shape):
    return lax.broadcasted_iota(jnp.int32, shape, len(shape) - 1)


def rows_of(shape):
    return lax.broadcasted_iota(jnp.int32, shape, len(shape) - 2)


def pack_rest(rest, height):
    out = None
    total = rest.shape[0]
    for q in range(4):
        lo, hi = q * height, min((q + 1) * height, total)
        part = rest[lo:hi]
        if q:
            part = pltpu.roll(part, 32 * q, 1)
        if hi - lo < height:
            part = jnp.concatenate([part, jnp.zeros((height - (hi - lo), 128), F32)], axis=0)
        out = part if out is None else out + part
    return out


def unpack_rest(packed, q):
    part = packed if q == 0 else pltpu.roll(packed, 128 - 32 * q, 1)
    return jnp.where(lanes(part.shape) < 32, part, 0.0).astype(BF16)


def kernel(
    hid_hbm, hw_ref, cw_ref, p1_hbm, t1_hbm, p2_hbm, t2_hbm, tgt_hbm, clu_hbm, rows_hbm, count_hbm,
    loss_out, gh_out, head_out, cl_out, gp1_out, gt1_out, gp2_out, gt2_out,
    hid_ref, p1_ref, p2_ref, tgt_ref, clu_ref, rows_ref, count_ref,
    loss_ref, gh_ref, head_ref, cl_ref, gp1_ref, gt1_ref, gp2_ref, gt2_ref,
    t1_ref, t2_ref, ids, hp, G, WT, hwx, hwxT, HG, HU,
    CH, PT, PRY, PRN, PRF, PS1, PG, Xf, PJ,
    P1f, P2f, P1b, P2b,
    STF, STN, STY, TTF, TTN, TTY, TS,
    LG, L1s, L2s, INF, GP, GU, GC,
    BT, BRY, BRN, BRF, BS1, BG, BK, C1f, C2f,
    GB, GRY, GS1, GRN, GS2, GRF,
    ssem, rsem, lsem, tsem, isem, osem,
):
    d = lax.axis_index("dp")
    v = lax.axis_index("vocab")
    x, c = lax.div(d, 2), lax.rem(d, 2)
    z, y = lax.div(v, 4), lax.rem(v, 4)
    zhi, zlo = lax.div(z, 4), lax.rem(z, 4)

    def far_dev(k):
        return (d, lax.rem(z + 4 * k, 16) * 4 + y)

    def near_dev(o):
        return (d, lax.rem(z + o, 16) * 4 + y)

    def y_dev(k):
        return (d, z * 4 + lax.rem(y + k, 4))

    def x_dev(k):
        return (lax.rem(x + k, 4) * 2 + c, v)

    core_dev = (x * 2 + 1 - c, v)

    def dp_dev(k):
        return (lax.rem(d + k, 8), v)

    counter = [0]
    sent = []

    def send(src, dst, dev):
        i = counter[0]
        counter[0] += 1
        copy = pltpu.make_async_remote_copy(
            src_ref=src, dst_ref=dst, send_sem=ssem.at[i], recv_sem=rsem.at[i],
            device_id=dev, device_id_type=MESH,
        )
        copy.start()
        sent.append(copy)
        return i

    def recv(i, slot):
        pltpu.make_async_remote_copy(
            src_ref=slot, dst_ref=slot, send_sem=ssem.at[i], recv_sem=rsem.at[i],
            device_id=core_dev, device_id_type=MESH,
        ).wait_recv()

    barrier = pltpu.get_barrier_semaphore()
    greeted = 0
    for k in FAR:
        pl.semaphore_signal(barrier, inc=1, device_id=y_dev(k), device_id_type=MESH)
        greeted += 1
    for k in FAR:
        pl.semaphore_signal(barrier, inc=1, device_id=far_dev(k), device_id_type=MESH)
        greeted += 1
    for o in NEAR_FROM:
        pl.semaphore_signal(barrier, inc=1, device_id=near_dev(o), device_id_type=MESH)
        greeted += 1
    for k in range(1, 8):
        pl.semaphore_signal(barrier, inc=1, device_id=dp_dev(k), device_id_type=MESH)
        greeted += 1

    loads = [
        pltpu.make_async_copy(src, dst, isem.at[n])
        for n, (src, dst) in enumerate(
            (
                (hid_hbm, hid_ref), (rows_hbm, rows_ref), (count_hbm, count_ref), (tgt_hbm, tgt_ref),
                (clu_hbm, clu_ref), (p1_hbm, p1_ref), (p2_hbm, p2_ref),
            )
        )
    ]
    hw_copy = pltpu.make_async_copy(hw_ref, hwx.at[0:160], lsem)
    t1_copy = pltpu.make_async_copy(t1_hbm, t1_ref, tsem.at[0])
    t2_copy = pltpu.make_async_copy(t2_hbm, t2_ref, tsem.at[1])
    for copy in loads:
        copy.start()
    hw_copy.start()
    t1_copy.start()
    t2_copy.start()
    stores = []

    def store(src, dst):
        copy = pltpu.make_async_copy(src, dst, osem.at[len(stores)])
        copy.start()
        stores.append(copy)

    for copy in loads:
        copy.wait()

    hp[...] = jnp.zeros_like(hp)
    hp[:, 0:160] = hid_ref[...].astype(F32)
    G[y, zlo, zhi, 0:64, :] = hp[:, 0:128].astype(BF16)
    G[y, zlo, zhi, 64:80, :] = pack_rest(hp[:, 128:256], 16).astype(BF16)

    TS[...] = jnp.zeros_like(TS)
    lane40 = lanes((1, 40))
    for n in range(2):
        TS[n : n + 1, 0:40] = jnp.where(
            lane40 < count_ref[0:1, n : n + 1], rows_ref[n : n + 1, :], -1
        ).astype(F32)
    turned = jnp.transpose(TS[...])
    row_col = jnp.concatenate([turned[0:40, 0:1], turned[0:40, 1:2]], axis=0).astype(jnp.int32)
    ids[...] = jnp.full((2, 256), -1, jnp.int32)
    ids[0:1, 0:160] = tgt_ref[...]
    ids[1:2, 0:160] = clu_ref[...]
    target = ids[0:1, :]
    cluster = ids[1:2, :]
    slot_hit = lanes((80, 256)) == row_col
    onehot = jnp.where(slot_hit, 1.0, 0.0).astype(BF16)
    live = row_col >= 0
    goal = jnp.sum(jnp.where(slot_hit, target, 0).astype(F32), axis=1, keepdims=True).astype(jnp.int32)
    goal = jnp.where(live, goal, -1)

    hidb = hp[...].astype(BF16)
    chosen = dot(onehot, hidb, NT)
    CH[d, :, 64:128] = jnp.zeros((80, 64), BF16)
    CH[d, :, 0:64] = chosen.astype(BF16)
    part1 = dot(chosen[0:40].astype(BF16), p1_ref[...])
    part2 = dot(chosen[40:80].astype(BF16), p2_ref[...])

    def to_tiles(tiles, a, b):
        for t in range(64):
            at = tiles.at[t // 16, (t // 4) % 4, t % 4]
            i, j = t // 10, t % 10
            if t >= 50:
                at[...] = jnp.zeros((8, 128), F32)
            elif j < 8:
                at[...] = a[8 * i : 8 * i + 8, 128 * j : 128 * j + 128]
            else:
                at[...] = b[8 * i : 8 * i + 8, 128 * j - 1024 : 128 * j - 896]

    to_tiles(PT, part1, part2)

    pl.semaphore_wait(barrier, greeted)

    own = G.at[y, zlo, zhi]
    hid_far = [send(own, own, far_dev(k)) for k in FAR]

    def small_y(tiles, slots):
        return [send(tiles.at[lax.rem(y + k, 4)], slots.at[k - 1], y_dev(k)) for k in FAR]

    def small_near(tiles, slots, ids, sums, nslots):
        for n, i in enumerate(ids):
            recv(i, slots.at[n])
        sums[...] = (tiles[y] + slots[0]) + (slots[1] + slots[2])
        return [
            send(sums.at[lax.rem(zlo + o, 4)], nslots.at[n], near_dev(o))
            for n, o in enumerate(NEAR)
        ]

    def small_far(sums, nslots, ids, fslots):
        for n, i in enumerate(ids):
            recv(i, nslots.at[n])
        fslots[zhi] = (sums[zlo] + nslots[0]) + (nslots[1] + nslots[2])
        return [send(fslots.at[zhi], fslots.at[zhi], far_dev(k)) for k in FAR]

    def small_total(fslots, ids, full):
        for k, i in zip(FAR, ids):
            recv(i, fslots.at[lax.rem(zhi + 4 - k, 4)])
        full[y, zlo] = (fslots[0] + fslots[1]) + (fslots[2] + fslots[3])

    def back_y_first(full):
        return [send(full.at[y, zlo], full.at[y, zlo], y_dev(k)) for k in FAR]

    def back_near_second(full, ids):
        for k, i in zip(FAR, ids):
            recv(i, full.at[lax.rem(y + 4 - k, 4), zlo])
        return [send(full.at[:, zlo], full.at[:, zlo], near_dev(o)) for o in NEAR]

    def back_near_first(full):
        return [send(full.at[y, zlo], full.at[y, zlo], near_dev(o)) for o in NEAR]

    def back_y_second(full, ids):
        for o, i in zip(NEAR, ids):
            recv(i, full.at[y, lax.rem(zlo + 16 - o, 4)])
        return [send(full.at[y], full.at[y], y_dev(k)) for k in FAR]

    def small_done(full, waits):
        for i, yy, zl in waits:
            recv(i, full.at[yy] if zl is None else full.at[yy, zl])
        for t in range(50):
            i, j = t // 10, t % 10
            r, l = (8 * i, 128 * j) if j < 5 else (40 + 8 * i, 128 * j - 640)
            Xf[r : r + 8, l : l + 128] = full[t // 16, (t // 4) % 4, t % 4]

    def dp_x(buf):
        return [send(buf.at[x, c], buf.at[x, c], x_dev(k)) for k in FAR]

    def dp_core(buf, ids):
        for k, i in zip(FAR, ids):
            recv(i, buf.at[lax.rem(x + 4 - k, 4), c])
        return send(buf.at[:, c], buf.at[:, c], core_dev)

    def dp_done(buf, i):
        recv(i, buf.at[:, 1 - c])

    pr_y = small_y(PT, PRY)
    CHv = CH.reshape(4, 2, 80, 128)
    ch_x = dp_x(CHv)

    cw = cw_ref[...].astype(F32)
    row16 = rows_of((16, 4096))
    hwx[160:176, :] = jnp.where(
        row16 == 0, cw[0:1, :], jnp.where(row16 == 1, cw[1:2, :], 0.0)
    ).astype(BF16)
    hwx[176:256, :] = jnp.zeros((80, 4096), BF16)
    hw_copy.wait()

    def turn(j, _):
        at = pl.ds(pl.multiple_of(j * 128, 128), 128)
        hwxT[at, :] = jnp.transpose(hwx[:, at])
        return 0

    def spread(yy, zl):
        for zh in range(4):
            block = G.at[yy, zl, zh]
            base = pl.multiple_of(((zh * 4 + zl) * 4 + yy) * 64, 64)
            WT[pl.ds(base, 64), 0:128] = block[0:64, :]
            packed = block[64:80, :].astype(F32)
            for q in range(4):
                WT[pl.ds(pl.multiple_of(base + 16 * q, 16), 16), 128:256] = unpack_rest(packed, q)

    pr_n = small_near(PT, PRY, pr_y, PS1, PRN)
    lax.fori_loop(0, 8, turn, 0)
    pr_f = small_far(PS1, PRN, pr_n, PRF)
    for k, i in zip(FAR, hid_far):
        recv(i, G.at[y, zlo, lax.rem(zhi + 4 - k, 4)])
    hid_near = [send(G.at[y, zlo], G.at[y, zlo], near_dev(o)) for o in NEAR]
    hid_y = [[send(G.at[y, zlo], G.at[y, zlo], y_dev(k)) for k in FAR]]
    lax.fori_loop(8, 20, turn, 0)
    spread(y, zlo)

    def pass_on(n):
        at = lax.rem(zlo + 16 - NEAR[n], 4)
        recv(hid_near[n], G.at[y, at])
        hid_y.append([send(G.at[y, at], G.at[y, at], y_dev(k)) for k in FAR])

    pass_on(0)
    small_total(PRF, pr_f, PG)
    pr_by = back_y_first(PG)
    pass_on(1)
    pass_on(2)
    pr_bn = back_near_second(PG, pr_by)
    ch_c = dp_core(CHv, ch_x)
    lax.fori_loop(20, 32, turn, 0)
    for n in range(3):
        spread(y, lax.rem(zlo + 16 - NEAR[n], 4))
    small_done(PG, [(i, slice(None), lax.rem(zlo + 16 - o, 4)) for o, i in zip(NEAR, pr_bn)])
    PJ[d] = Xf[...].astype(BF16)
    PJv = PJ.reshape(4, 2, 80, 640)
    pj_x = dp_x(PJv)

    t1_copy.wait()
    t2_copy.wait()
    left, right = Xf[0:40, :].astype(BF16), Xf[40:80, :].astype(BF16)
    log1 = dot(left, t1_ref[:, 0:640], NT) + dot(right[:, 0:384], t1_ref[:, 640:1024], NT)
    log2 = dot(right[:, 384:640], t2_ref[...], NT)
    L1s[...] = log1
    L2s[...] = log2

    def column_stats(values, goals):
        high = jnp.max(values, axis=1, keepdims=True)
        total = jnp.sum(jnp.exp(values - high), axis=1, keepdims=True)
        hit = lanes(values.shape) == goals
        return high, total, jnp.sum(jnp.where(hit, values, 0.0), axis=1, keepdims=True)

    stat1 = column_stats(log1, goal[0:40] - v * 320)
    stat2 = column_stats(log2, goal[40:80] - v * 1664)
    lane = lanes((80, 128))
    table = jnp.zeros((80, 128), F32)
    for n in range(3):
        table = jnp.where(lane == n, jnp.concatenate([stat1[n], stat2[n]], axis=0), table)
    TS[0:80, :] = table
    TS[80:128, :] = jnp.zeros((48, 128), F32)
    TTF[zhi] = jnp.transpose(TS[...])[0:8, :]
    tail_ids = [send(TTF.at[zhi], TTF.at[zhi], far_dev(k)) for k in FAR]

    def join(slots):
        parts = [slots[i] for i in range(4)]
        m = [p[0:1] for p in parts]
        top = jnp.maximum(jnp.maximum(m[0], m[1]), jnp.maximum(m[2], m[3]))
        s = [p[1:2] * jnp.exp(mm - top) for p, mm in zip(parts, m)]
        t = [p[2:3] for p in parts]
        return top, (s[0] + s[1]) + (s[2] + s[3]), (t[0] + t[1]) + (t[2] + t[3])

    def as_tile(result):
        row = rows_of((8, result[0].shape[1]))
        return jnp.where(
            row == 0, result[0], jnp.where(row == 1, result[1], jnp.where(row == 2, result[2], 0.0))
        )

    def join_far(far, near, ids):
        for k, i in zip(FAR, ids):
            recv(i, far.at[lax.rem(zhi + 4 - k, 4)])
        near[zlo] = as_tile(join(far))
        return [send(near.at[zlo], near.at[zlo], near_dev(o)) for o in NEAR]

    def join_near(near, last, ids):
        for o, i in zip(NEAR, ids):
            recv(i, near.at[lax.rem(zlo + 16 - o, 4)])
        last[y] = as_tile(join(near))
        return [send(last.at[y], last.at[y], y_dev(k)) for k in FAR]

    def join_last(last, ids):
        for k, i in zip(FAR, ids):
            recv(i, last.at[lax.rem(y + 4 - k, 4)])
        return join(last)


    for n, ids_y in enumerate(hid_y):
        at = zlo if n == 0 else lax.rem(zlo + 16 - NEAR[n - 1], 4)
        for k, i in zip(FAR, ids_y):
            yy = lax.rem(y + 4 - k, 4)
            recv(i, G.at[yy, at])
            spread(yy, at)

    slices = []
    for k in range(1, 8):
        peer = lax.rem(d + k, 8)
        src = G.at[:, pl.ds(lax.rem(2 * peer, 4), 2), lax.div(peer, 2)]
        slices.append(send(src, HG.at[d], dp_dev(k)))

    LG[...] = dot(hwx[...], WT[...])
    words = LG[0:160, :]
    head_goal = jnp.where(cluster == 0, target, -1) - v * 160
    head_hit = rows_of((160, 256)) == head_goal
    high = jnp.max(words, axis=0, keepdims=True)
    total = jnp.sum(jnp.exp(words - high), axis=0, keepdims=True)
    picked = jnp.sum(jnp.where(head_hit, words, 0.0), axis=0, keepdims=True)
    STF[zhi] = as_tile((high, total, picked))
    head_ids = [send(STF.at[zhi], STF.at[zhi], far_dev(k)) for k in FAR]
    tail_ids = join_far(TTF, TTN, tail_ids)
    pj_c = dp_core(PJv, pj_x)
    tail_ids = join_near(TTN, TTY, tail_ids)
    head_ids = join_far(STF, STN, head_ids)
    tail_stats = join_last(TTY, tail_ids)

    tail_lse = tail_stats[0] + jnp.log(tail_stats[1])
    TS[...] = jnp.zeros_like(TS)
    TS[0:1, :] = tail_lse
    TS[1:2, :] = tail_lse - tail_stats[2]
    columns = jnp.transpose(TS[...])[0:80, :]
    lse_col = jnp.where(live, columns[:, 0:1], 1e30)
    loss_col = columns[:, 1:2]

    def tail_gradient(values, lse, goals):
        hit = (lanes(values.shape) == goals).astype(F32)
        return (SCALE * (jnp.exp(values - lse) - hit)).astype(BF16)

    own1 = tail_gradient(L1s[...], lse_col[0:40], goal[0:40] - v * 320)
    own2 = tail_gradient(L2s[...], lse_col[40:80], goal[40:80] - v * 1664)
    to_tiles(BT, dot(own1, t1_ref[...]), dot(own2, t2_ref[...]))
    bk_y = small_y(BT, BRY)

    head_ids = join_near(STN, STY, head_ids)
    INF[d] = jnp.where(lane == 0, lse_col, jnp.where(lane == 1, goal.astype(F32), 0.0))
    INFv = INF.reshape(4, 2, 80, 128)
    inf_x = dp_x(INFv)
    bk_n = small_near(BT, BRY, bk_y, BS1, BRN)
    stats = join_last(STY, head_ids)

    entry0, entry1 = LG[160:161, :], LG[161:162, :]
    top = jnp.maximum(stats[0], jnp.maximum(entry0, entry1))
    summed = stats[1] * jnp.exp(stats[0] - top) + (jnp.exp(entry0 - top) + jnp.exp(entry1 - top))
    lse = top + jnp.log(summed)
    is1, is2 = (cluster == 1).astype(F32), (cluster == 2).astype(F32)
    chosen_logit = stats[2] + (is1 * entry0 + is2 * entry1)
    tail_loss = jnp.sum(jnp.where(slot_hit, loss_col, 0.0), axis=0, keepdims=True)
    loss_ref[...] = ((lse - chosen_logit) + tail_loss)[:, 0:160]
    store(loss_ref, loss_out)

    inside = lanes((160, 256)) < 160
    grad = jnp.where(inside, SCALE * (jnp.exp(LG[0:160, :] - lse) - head_hit.astype(F32)), 0.0)
    inside1 = lanes((1, 256)) < 160
    ge0 = jnp.where(inside1, SCALE * (jnp.exp(entry0 - lse) - is1), 0.0)
    ge1 = jnp.where(inside1, SCALE * (jnp.exp(entry1 - lse) - is2), 0.0)
    GP[d, 0:160, :] = grad[:, 0:128].astype(BF16)
    rounded_rest = grad[:, 128:256]
    GP[d, 160:208, :] = pack_rest(rounded_rest, 48).astype(BF16)
    GPv = GP.reshape(4, 2, 208, 128)
    gp_x = dp_x(GPv)

    row96 = rows_of((96, 256))
    mine = (v == 0).astype(F32)
    low = jnp.where(row96 == 0, ge0 * mine, jnp.where(row96 == 1, ge1 * mine, 0.0))
    grad_ext = jnp.concatenate([grad, low], axis=0).astype(BF16)

    gh_y = []

    def part(o):
        at = lax.rem(zlo + o, 4)
        for zh in range(4):
            rows = pl.ds(pl.multiple_of((zh * 4 + at) * 256, 256), 256)
            product = dot(hwxT[rows, :], grad_ext)
            for yy in range(4):
                block = GB.at[yy, at, zh]
                piece = product[64 * yy : 64 * yy + 64]
                block[0:64, :] = piece[:, 0:128].astype(BF16)
                block[64:80, :] = pack_rest(piece[:, 128:256], 16).astype(BF16)
        gh_y.append(
            [send(GB.at[lax.rem(y + k, 4), at], GRY.at[k - 1, at], y_dev(k)) for k in FAR]
        )

    part(NEAR[0])
    part(NEAR[2])
    bk_f = small_far(BS1, BRN, bk_n, BRF)
    part(NEAR[1])
    part(0)
    entries = jnp.where(rows_of((8, 256)) % 2 == 0, ge0, ge1).astype(BF16)
    full = dot(entries, WT[...], NT)
    pair = lax.div(rows_of((8, 1024)), 2)
    packed_cl = jnp.zeros((8, 1024), F32)
    for k in range(4):
        packed_cl = jnp.where(pair == k, full[:, 1024 * k : 1024 * k + 1024], packed_cl)
    GC[d] = packed_cl
    GCv = GC.reshape(4, 2, 8, 1024)
    gc_x = dp_x(GCv)
    order = (0, 2, 1)
    gh_n = {}

    def y_sum(at, ids):
        for k, i in zip(FAR, ids):
            recv(i, GRY.at[k - 1, at])
        return (GB[y, at].astype(F32) + GRY[0, at].astype(F32)) + (
            GRY[1, at].astype(F32) + GRY[2, at].astype(F32)
        )

    def chunk_near(turn_at):
        n = order[turn_at]
        GS1[n] = y_sum(lax.rem(zlo + NEAR[n], 4), gh_y[turn_at]).astype(BF16)
        gh_n[n] = send(GS1.at[n], GRN.at[n], near_dev(NEAR[n]))

    chunk_near(0)
    inf_c = dp_core(INFv, inf_x)
    gp_c = dp_core(GPv, gp_x)
    def assemble(src, dst1, dst2):
        for g in range(8):
            both = src[g].astype(F32)
            dst1[40 * g : 40 * g + 40, 0:640] = both[0:40, :]
            dst1[40 * g : 40 * g + 40, 640:1024] = both[40:80, 0:384]
            dst2[40 * g : 40 * g + 40, :] = both[40:80, 384:640]

    dp_done(PJv, pj_c)
    dp_done(INFv, inf_c)
    assemble(PJ, P1f, P2f)
    P1b[...] = P1f[...].astype(BF16)
    P2b[...] = P2f[...].astype(BF16)

    def gather_column(lo, lane_at):
        return jnp.concatenate([INF[g, lo : lo + 40, lane_at : lane_at + 1] for g in range(8)], axis=0)

    lse1, goal1 = gather_column(0, 0), gather_column(0, 1).astype(jnp.int32)
    all1 = dot(P1b[...], t1_ref[...], NT)
    base1 = jnp.where(goal1 < 0, -(1 << 20), goal1 - v * 320)
    grad1 = tail_gradient(all1, lse1, base1)
    gt1_ref[...] = dot(grad1, P1b[:, pl.ds(pl.multiple_of(d * 128, 128), 128)], TN)
    store(gt1_ref, gt1_out)

    lse2, goal2 = gather_column(40, 0), gather_column(40, 1).astype(jnp.int32)
    base2 = jnp.where(goal2 < 0, -(1 << 20), goal2 - v * 1664)
    select = jnp.where(lanes((32, 256)) == rows_of((32, 256)) + d * 32, 1.0, 0.0).astype(BF16)
    mine2 = dot(select, P2b[...], NT).astype(BF16)
    P1f[:, 0:128] = jnp.broadcast_to(lse2, (320, 128))
    P1f[:, 128:256] = jnp.broadcast_to(base2.astype(F32), (320, 128))

    def tail_two(j, _):
        at = pl.multiple_of(j * 128, 128)
        logits = dot(P2b[...], t2_ref[pl.ds(at, 128), :], NT)
        hit = (lanes((320, 128)).astype(F32) + (j * 128).astype(F32)) == P1f[:, 128:256]
        grads = (SCALE * (jnp.exp(logits - P1f[:, 0:128]) - hit.astype(F32))).astype(BF16)
        gt2_ref[:, pl.ds(at, 128)] = dot(mine2, grads)
        return 0

    chunk_near(1)
    small_total(BRF, bk_f, BG)
    bk_bn = back_near_first(BG)
    lax.fori_loop(0, 6, tail_two, 0)
    chunk_near(2)
    bk_by = back_y_second(BG, bk_bn)
    mine_sum = y_sum(zlo, gh_y[3])
    for n in range(3):
        recv(gh_n[n], GRN.at[n])
    GS2[...] = mine_sum + (
        GRN[0].astype(F32) + (GRN[1].astype(F32) + GRN[2].astype(F32))
    )
    for k in FAR:
        GRF[2 + k] = GS2[lax.rem(zhi + k, 4)].astype(BF16)
    gh_f = [send(GRF.at[2 + k], GRF.at[k - 1], far_dev(k)) for k in FAR]
    small_done(BG, [(i, lax.rem(y + 4 - k, 4), None) for k, i in zip(FAR, bk_by)])
    BK[d] = Xf[...].astype(BF16)
    BKv = BK.reshape(4, 2, 80, 640)
    bk_x = dp_x(BKv)

    gc_c = dp_core(GCv, gc_x)
    lax.fori_loop(6, 13, tail_two, 0)
    store(gt2_ref, gt2_out)
    HG[d] = G[:, pl.ds(lax.rem(2 * d, 4), 2), lax.div(d, 2)]
    dp_done(GPv, gp_c)
    for k, i in zip(range(1, 8), slices):
        recv(i, HG.at[lax.rem(d + 8 - k, 8)])
    head_ref[...] = jnp.zeros_like(head_ref)

    def head_group(g, _):
        GU[:, 0:128] = GP[g, 0:160, :]
        rest = GP[g, 160:208, :].astype(F32)
        for q in range(4):
            rows = 48 if q < 3 else 16
            GU[48 * q : 48 * q + rows, 128:256] = unpack_rest(rest[0:rows], q)
        for b in range(8):
            block = HG.at[g, b % 4, b // 4]
            HU[64 * b : 64 * b + 64, 0:128] = block[0:64, :]
            packed = block[64:80, :].astype(F32)
            for q in range(4):
                HU[64 * b + 16 * q : 64 * b + 16 * q + 16, 128:256] = unpack_rest(packed, q)
        head_ref[...] += dot(GU[...], HU[...], NT)
        return 0

    lax.fori_loop(0, 8, head_group, 0)
    store(head_ref, head_out)

    dp_done(GCv, gc_c)
    cl_sum = ((GC[0] + GC[1]) + (GC[2] + GC[3])) + ((GC[4] + GC[5]) + (GC[6] + GC[7]))
    for k in range(4):
        cl_ref[:, 1024 * k : 1024 * k + 1024] = cl_sum[2 * k : 2 * k + 2, :]
    store(cl_ref, cl_out)

    both = BK[d].astype(F32)
    b1a, b1b = both[0:40, :].astype(BF16), both[40:80, 0:384].astype(BF16)
    b2 = both[40:80, 384:640].astype(BF16)
    hot1 = jnp.where(slot_hit[0:40], 1.0, 0.0)
    hot2 = jnp.where(slot_hit[40:80], 1.0, 0.0)
    back_one = dot(p1_ref[:, 0:640], b1a, NT) + dot(p1_ref[:, 640:1024], b1b, NT)
    add = dot_exact(back_one, hot1) + dot_exact(dot(p2_ref[...], b2, NT), hot2)
    bk_c = dp_core(BKv, bk_x)

    for n, i in enumerate(gh_f):
        recv(i, GRF.at[n])
    block = GS2[zhi] + (GRF[0].astype(F32) + (GRF[1].astype(F32) + GRF[2].astype(F32)))
    hp[:, 0:128] = block[0:64, :]
    for q in range(4):
        part_q = block[64:80, :]
        hp[16 * q : 16 * q + 16, 128:256] = part_q if q == 0 else pltpu.roll(part_q, 128 - 32 * q, 1)
    gh_ref[...] = (hp[...] + add)[:, 0:160]
    store(gh_ref, gh_out)

    dp_done(CHv, ch_c)
    dp_done(BKv, bk_c)
    assemble(BK, P1f, P2f)
    for g in range(8):
        rows_g = CH[g].astype(F32)
        C1f[40 * g : 40 * g + 40, :] = rows_g[0:40, :]
        C2f[40 * g : 40 * g + 40, :] = rows_g[40:80, :]
    gp1_ref[...] = dot(C1f[...].astype(BF16), P1f[...].astype(BF16), TN)[0:64, :]
    store(gp1_ref, gp1_out)
    gp2_ref[...] = dot(C2f[...].astype(BF16), P2f[...].astype(BF16), TN)[0:64, :]
    store(gp2_ref, gp2_out)
    for copy in stores:
        copy.wait()

    for copy in sent:
        copy.wait_send()


def hand_over(*refs):
    for i in range(8):
        refs[8 + i][...] = refs[i][...]


def on_device(
    hidden_states, head_weight, cluster_weight, proj_one, tail_one, proj_two, tail_two,
    targets, token_cluster, tail_rows, tail_counts,
):
    vmem = pl.BlockSpec(memory_space=pltpu.VMEM)
    hbm = pl.BlockSpec(memory_space=pl.ANY)
    shapes = [
        ((1, 160), F32), ((64, 160), F32), ((160, 512), F32), ((2, 4096), F32),
        ((64, 1024), F32), ((320, 128), F32), ((64, 256), F32), ((32, 1664), F32),
    ]
    V = pltpu.VMEM
    scratch = [
        V((64, 160), BF16), V((64, 1024), BF16), V((64, 256), BF16), V((1, 160), jnp.int32),
        V((1, 160), jnp.int32), V((2, 40), jnp.int32), V((1, 2), jnp.int32),
    ] + [V(s, t) for s, t in shapes] + [
        V((320, 1024), BF16), V((1664, 256), BF16), V((2, 256), jnp.int32),
        V((64, 256), F32), V((4, 4, 4, 80, 128), BF16), V((4096, 256), BF16), V((256, 4096), BF16),
        V((4096, 256), BF16), V((8, 4, 2, 80, 128), BF16), V((512, 256), BF16),
        V((8, 80, 128), BF16), V((4, 4, 4, 8, 128), F32), V((3, 4, 4, 8, 128), F32),
        V((3, 4, 8, 128), F32), V((4, 4, 8, 128), F32), V((4, 4, 8, 128), F32),
        V((4, 4, 4, 8, 128), F32), V((80, 640), F32), V((8, 80, 640), BF16),
        V((320, 1024), F32), V((320, 256), F32), V((320, 1024), BF16), V((320, 256), BF16),
        V((4, 8, 256), F32), V((4, 8, 256), F32), V((4, 8, 256), F32),
        V((4, 8, 128), F32), V((4, 8, 128), F32), V((4, 8, 128), F32), V((128, 128), F32),
        V((256, 256), F32), V((40, 320), F32), V((40, 1664), F32), V((8, 80, 128), F32),
        V((8, 208, 128), BF16), V((160, 256), BF16), V((8, 8, 1024), F32),
        V((4, 4, 4, 8, 128), F32), V((3, 4, 4, 8, 128), F32), V((3, 4, 8, 128), F32), V((4, 4, 8, 128), F32),
        V((4, 4, 8, 128), F32), V((4, 4, 4, 8, 128), F32), V((8, 80, 640), BF16),
        V((320, 128), F32), V((320, 128), F32),
        V((4, 4, 4, 80, 128), BF16), V((3, 4, 4, 80, 128), BF16), V((3, 4, 80, 128), BF16),
        V((3, 4, 80, 128), BF16), V((4, 80, 128), F32), V((6, 80, 128), BF16),
        pltpu.SemaphoreType.DMA((SEMS,)), pltpu.SemaphoreType.DMA((SEMS,)), pltpu.SemaphoreType.DMA,
        pltpu.SemaphoreType.DMA((2,)), pltpu.SemaphoreType.DMA((7,)), pltpu.SemaphoreType.DMA((8,)),
    ]
    out = pl.pallas_call(
        kernel,
        out_shape=[jax.ShapeDtypeStruct(s, t) for s, t in shapes],
        in_specs=[hbm, hbm, vmem] + [hbm] * 8,
        out_specs=[hbm] * 8,
        scratch_shapes=scratch,
        compiler_params=pltpu.CompilerParams(
            collective_id=0, has_side_effects=True, vmem_limit_bytes=56 * 1024 * 1024
        ),
    )(
        hidden_states.T, head_weight, cluster_weight, proj_one, tail_one, proj_two, tail_two,
        targets.reshape(1, 160), token_cluster.reshape(1, 160), tail_rows[0], tail_counts,
    )
    loss, gh, head, cl, gp1, gt1, gp2, gt2 = pl.pallas_call(
        hand_over,
        out_shape=[jax.ShapeDtypeStruct(s, t) for s, t in shapes],
        in_specs=[vmem] * 8,
        out_specs=[vmem] * 8,
    )(*out)
    return (
        loss.reshape(160),
        gh.T,
        head,
        cl,
        gp1,
        gt1,
        gp2,
        gt2.T,
    )


def solution(mesh):
    return jax.shard_map(
        on_device,
        mesh=mesh,
        in_specs=(
            P("dp", "vocab"), P("vocab", None), P(), P("vocab", None), P("vocab", None),
            P("vocab", None), P("vocab", None), P("dp"), P("dp"), P("dp", None, None), P("dp", None),
        ),
        out_specs=(
            P("dp"), P("dp", "vocab"), P("vocab", "dp"), P(), P("vocab", None),
            P("vocab", "dp"), P("vocab", None), P("vocab", "dp"),
        ),
        check_vma=False,
    )
```

```python
import jax
import jax.numpy as jnp
from jax import lax
from jax.experimental import pallas as pl
from jax.experimental.pallas import tpu as pltpu
from jax.sharding import PartitionSpec as P

MESH = pl.DeviceIdType.MESH
F32 = jnp.float32
BF16 = jnp.bfloat16
SCALE = 64.0
FAR = (1, 2, 3)
NEAR = (1, 15, 2)
PAIRS = tuple((o, k) for o in (0,) + NEAR for k in (0,) + FAR)[1:]
SEMS = 176
NT = (((1,), (1,)), ((), ()))
TN = (((0,), (0,)), ((), ()))
NN = (((1,), (0,)), ((), ()))


def dot(a, b, dims=NN):
    return lax.dot_general(a, b, dims, preferred_element_type=F32)


def dot_exact(a, b):
    return lax.dot_general(a, b, NN, precision=lax.Precision.HIGHEST, preferred_element_type=F32)


def lanes(shape):
    return lax.broadcasted_iota(jnp.int32, shape, len(shape) - 1)


def rows_of(shape):
    return lax.broadcasted_iota(jnp.int32, shape, len(shape) - 2)


def pack_rest(rest, height):
    out = None
    total = rest.shape[0]
    for q in range(4):
        lo, hi = q * height, min((q + 1) * height, total)
        part = rest[lo:hi]
        if q:
            part = pltpu.roll(part, 32 * q, 1)
        if hi - lo < height:
            part = jnp.concatenate([part, jnp.zeros((height - (hi - lo), 128), F32)], axis=0)
        out = part if out is None else out + part
    return out


def unpack_rest(packed, q):
    part = packed if q == 0 else pltpu.roll(packed, 128 - 32 * q, 1)
    return jnp.where(lanes(part.shape) < 32, part, 0.0).astype(BF16)


def kernel(
    hid_hbm, hw_ref, cw_ref, p1_hbm, t1_hbm, p2_hbm, t2_hbm, tgt_hbm, clu_hbm, rows_hbm, count_hbm,
    loss_out, gh_out, head_out, cl_out, gp1_out, gt1_out, gp2_out, gt2_out,
    hid_ref, p1_ref, p2_ref, tgt_ref, clu_ref, rows_ref, count_ref,
    loss_ref, gh_ref, head_ref, cl_ref, gp1_ref, gt1_ref, gp2_ref, gt2_ref,
    t1_ref, t2_ref, ids, hp, G, WT, hwx, hwxT, HG, HU,
    CH, PT, PRY, PRN, PRF, PS1, PG, Xf, PJ,
    P1f, P2f, P1b, P2b,
    STF, STN, TTF, TTN, TS,
    LG, L1s, L2s, INF, GP, GU, GC,
    BT, BRY, BRN, BRF, BS1, BG, BK, C1f, C2f,
    GB, GRY, GS1, GRN, GS2, GRF,
    ssem, rsem, lsem, tsem, isem, osem,
):
    d = lax.axis_index("dp")
    v = lax.axis_index("vocab")
    x, c = lax.div(d, 2), lax.rem(d, 2)
    z, y = lax.div(v, 4), lax.rem(v, 4)
    zhi, zlo = lax.div(z, 4), lax.rem(z, 4)

    def far_dev(k):
        return (d, lax.rem(z + 4 * k, 16) * 4 + y)

    def near_dev(o):
        return (d, lax.rem(z + o, 16) * 4 + y)

    def pair_dev(o, k):
        return (d, lax.rem(z + o, 16) * 4 + lax.rem(y + k, 4))

    def y_dev(k):
        return (d, z * 4 + lax.rem(y + k, 4))

    def x_dev(k):
        return (lax.rem(x + k, 4) * 2 + c, v)

    core_dev = (x * 2 + 1 - c, v)

    def dp_dev(k):
        return (lax.rem(d + k, 8), v)

    counter = [0]
    sent = []

    def send(src, dst, dev):
        i = counter[0]
        counter[0] += 1
        copy = pltpu.make_async_remote_copy(
            src_ref=src, dst_ref=dst, send_sem=ssem.at[i], recv_sem=rsem.at[i],
            device_id=dev, device_id_type=MESH,
        )
        copy.start()
        sent.append(copy)
        return i

    def recv(i, slot):
        pltpu.make_async_remote_copy(
            src_ref=slot, dst_ref=slot, send_sem=ssem.at[i], recv_sem=rsem.at[i],
            device_id=core_dev, device_id_type=MESH,
        ).wait_recv()

    barrier = pltpu.get_barrier_semaphore()
    greeted = 0
    for k in FAR:
        pl.semaphore_signal(barrier, inc=1, device_id=far_dev(k), device_id_type=MESH)
        greeted += 1
    for o, k in PAIRS:
        pl.semaphore_signal(barrier, inc=1, device_id=pair_dev(16 - o, 4 - k), device_id_type=MESH)
        greeted += 1
    for k in range(1, 8):
        pl.semaphore_signal(barrier, inc=1, device_id=dp_dev(k), device_id_type=MESH)
        greeted += 1

    loads = [
        pltpu.make_async_copy(src, dst, isem.at[n])
        for n, (src, dst) in enumerate(
            (
                (hid_hbm, hid_ref), (rows_hbm, rows_ref), (count_hbm, count_ref), (tgt_hbm, tgt_ref),
                (clu_hbm, clu_ref), (p1_hbm, p1_ref), (p2_hbm, p2_ref),
            )
        )
    ]
    hw_copy = pltpu.make_async_copy(hw_ref, hwx.at[0:160], lsem)
    t1_copy = pltpu.make_async_copy(t1_hbm, t1_ref, tsem.at[0])
    t2_copy = pltpu.make_async_copy(t2_hbm, t2_ref, tsem.at[1])
    for copy in loads:
        copy.start()
    hw_copy.start()
    t1_copy.start()
    t2_copy.start()
    stores = []

    def store(src, dst):
        copy = pltpu.make_async_copy(src, dst, osem.at[len(stores)])
        copy.start()
        stores.append(copy)

    for copy in loads:
        copy.wait()

    hp[...] = jnp.zeros_like(hp)
    hp[:, 0:160] = hid_ref[...].astype(F32)
    G[y, zlo, zhi, 0:64, :] = hp[:, 0:128].astype(BF16)
    G[y, zlo, zhi, 64:80, :] = pack_rest(hp[:, 128:256], 16).astype(BF16)

    TS[...] = jnp.zeros_like(TS)
    lane40 = lanes((1, 40))
    for n in range(2):
        TS[n : n + 1, 0:40] = jnp.where(
            lane40 < count_ref[0:1, n : n + 1], rows_ref[n : n + 1, :], -1
        ).astype(F32)
    turned = jnp.transpose(TS[...])
    row_col = jnp.concatenate([turned[0:40, 0:1], turned[0:40, 1:2]], axis=0).astype(jnp.int32)
    ids[...] = jnp.full((2, 256), -1, jnp.int32)
    ids[0:1, 0:160] = tgt_ref[...]
    ids[1:2, 0:160] = clu_ref[...]
    target = ids[0:1, :]
    cluster = ids[1:2, :]
    slot_hit = lanes((80, 256)) == row_col
    onehot = jnp.where(slot_hit, 1.0, 0.0).astype(BF16)
    live = row_col >= 0
    goal = jnp.sum(jnp.where(slot_hit, target, 0).astype(F32), axis=1, keepdims=True).astype(jnp.int32)
    goal = jnp.where(live, goal, -1)

    hidb = hp[...].astype(BF16)
    chosen = dot(onehot, hidb, NT)
    CH[d, :, 64:128] = jnp.zeros((80, 64), BF16)
    CH[d, :, 0:64] = chosen.astype(BF16)
    part1 = dot(chosen[0:40].astype(BF16), p1_ref[...])
    part2 = dot(chosen[40:80].astype(BF16), p2_ref[...])

    def to_tiles(tiles, a, b):
        for t in range(64):
            at = tiles.at[t // 16, (t // 4) % 4, t % 4]
            i, j = t // 10, t % 10
            if t >= 50:
                at[...] = jnp.zeros((8, 128), F32)
            elif j < 8:
                at[...] = a[8 * i : 8 * i + 8, 128 * j : 128 * j + 128]
            else:
                at[...] = b[8 * i : 8 * i + 8, 128 * j - 1024 : 128 * j - 896]

    to_tiles(PT, part1, part2)

    pl.semaphore_wait(barrier, greeted)

    own = G.at[y, zlo, zhi]
    hid_far = [send(own, own, far_dev(k)) for k in FAR]

    def small_y(tiles, slots):
        return [send(tiles.at[lax.rem(y + k, 4)], slots.at[k - 1], y_dev(k)) for k in FAR]

    def small_near(tiles, slots, ids, sums, nslots):
        for n, i in enumerate(ids):
            recv(i, slots.at[n])
        sums[...] = (tiles[y] + slots[0]) + (slots[1] + slots[2])
        return [
            send(sums.at[lax.rem(zlo + o, 4)], nslots.at[n], near_dev(o))
            for n, o in enumerate(NEAR)
        ]

    def small_far(sums, nslots, ids, fslots):
        for n, i in enumerate(ids):
            recv(i, nslots.at[n])
        fslots[zhi] = (sums[zlo] + nslots[0]) + (nslots[1] + nslots[2])
        return [send(fslots.at[zhi], fslots.at[zhi], far_dev(k)) for k in FAR]

    def small_total(fslots, ids, full):
        for k, i in zip(FAR, ids):
            recv(i, fslots.at[lax.rem(zhi + 4 - k, 4)])
        full[y, zlo] = (fslots[0] + fslots[1]) + (fslots[2] + fslots[3])

    def pair_send(full):
        own_entry = full.at[y, zlo]
        return [send(own_entry, own_entry, pair_dev(o, k)) for o, k in PAIRS]

    def pair_wait(full, ids):
        for (o, k), i in zip(PAIRS, ids):
            recv(i, full.at[lax.rem(y + 4 - k, 4), lax.rem(zlo + 16 - o, 4)])

    def small_done(full, ids):
        pair_wait(full, ids)
        for t in range(50):
            i, j = t // 10, t % 10
            r, l = (8 * i, 128 * j) if j < 5 else (40 + 8 * i, 128 * j - 640)
            Xf[r : r + 8, l : l + 128] = full[t // 16, (t // 4) % 4, t % 4]

    def dp_x(buf):
        return [send(buf.at[x, c], buf.at[x, c], x_dev(k)) for k in FAR]

    def dp_core(buf, ids):
        for k, i in zip(FAR, ids):
            recv(i, buf.at[lax.rem(x + 4 - k, 4), c])
        return send(buf.at[:, c], buf.at[:, c], core_dev)

    def dp_done(buf, i):
        recv(i, buf.at[:, 1 - c])

    pr_y = small_y(PT, PRY)
    CHv = CH.reshape(4, 2, 80, 128)
    ch_x = dp_x(CHv)

    cw = cw_ref[...].astype(F32)
    row16 = rows_of((16, 4096))
    hwx[160:176, :] = jnp.where(
        row16 == 0, cw[0:1, :], jnp.where(row16 == 1, cw[1:2, :], 0.0)
    ).astype(BF16)
    hwx[176:256, :] = jnp.zeros((80, 4096), BF16)
    hw_copy.wait()

    def turn(j, _):
        at = pl.ds(pl.multiple_of(j * 128, 128), 128)
        hwxT[at, :] = jnp.transpose(hwx[:, at])
        return 0

    def spread(yy, zl):
        for zh in range(4):
            block = G.at[yy, zl, zh]
            base = pl.multiple_of(((zh * 4 + zl) * 4 + yy) * 64, 64)
            WT[pl.ds(base, 64), 0:128] = block[0:64, :]
            packed = block[64:80, :].astype(F32)
            for q in range(4):
                WT[pl.ds(pl.multiple_of(base + 16 * q, 16), 16), 128:256] = unpack_rest(packed, q)

    pr_n = small_near(PT, PRY, pr_y, PS1, PRN)
    lax.fori_loop(0, 8, turn, 0)
    pr_f = small_far(PS1, PRN, pr_n, PRF)
    for k, i in zip(FAR, hid_far):
        recv(i, G.at[y, zlo, lax.rem(zhi + 4 - k, 4)])
    hid_near = [send(G.at[y, zlo], G.at[y, zlo], near_dev(o)) for o in NEAR]
    hid_y = [[send(G.at[y, zlo], G.at[y, zlo], y_dev(k)) for k in FAR]]
    lax.fori_loop(8, 20, turn, 0)
    spread(y, zlo)

    def pass_on(n):
        at = lax.rem(zlo + 16 - NEAR[n], 4)
        recv(hid_near[n], G.at[y, at])
        hid_y.append([send(G.at[y, at], G.at[y, at], y_dev(k)) for k in FAR])

    pass_on(0)
    small_total(PRF, pr_f, PG)
    pr_all = pair_send(PG)
    pass_on(1)
    pass_on(2)
    ch_c = dp_core(CHv, ch_x)
    lax.fori_loop(20, 32, turn, 0)
    for n in range(3):
        spread(y, lax.rem(zlo + 16 - NEAR[n], 4))
    small_done(PG, pr_all)
    PJ[d] = Xf[...].astype(BF16)
    PJv = PJ.reshape(4, 2, 80, 640)
    pj_x = dp_x(PJv)

    t1_copy.wait()
    t2_copy.wait()
    left, right = Xf[0:40, :].astype(BF16), Xf[40:80, :].astype(BF16)
    log1 = dot(left, t1_ref[:, 0:640], NT) + dot(right[:, 0:384], t1_ref[:, 640:1024], NT)
    log2 = dot(right[:, 384:640], t2_ref[...], NT)
    L1s[...] = log1
    L2s[...] = log2

    def column_stats(values, goals):
        high = jnp.max(values, axis=1, keepdims=True)
        total = jnp.sum(jnp.exp(values - high), axis=1, keepdims=True)
        hit = lanes(values.shape) == goals
        return high, total, jnp.sum(jnp.where(hit, values, 0.0), axis=1, keepdims=True)

    stat1 = column_stats(log1, goal[0:40] - v * 320)
    stat2 = column_stats(log2, goal[40:80] - v * 1664)
    lane = lanes((80, 128))
    table = jnp.zeros((80, 128), F32)
    for n in range(3):
        table = jnp.where(lane == n, jnp.concatenate([stat1[n], stat2[n]], axis=0), table)
    TS[0:80, :] = table
    TS[80:128, :] = jnp.zeros((48, 128), F32)
    TTF[zhi] = jnp.transpose(TS[...])[0:8, :]
    tail_ids = [send(TTF.at[zhi], TTF.at[zhi], far_dev(k)) for k in FAR]

    def join(parts):
        top = parts[0][0:1]
        for p in parts[1:]:
            top = jnp.maximum(top, p[0:1])
        total, picked = 0.0, 0.0
        for p in parts:
            total = total + p[1:2] * jnp.exp(p[0:1] - top)
            picked = picked + p[2:3]
        return top, total, picked

    def as_tile(result):
        row = rows_of((8, result[0].shape[1]))
        return jnp.where(
            row == 0, result[0], jnp.where(row == 1, result[1], jnp.where(row == 2, result[2], 0.0))
        )

    def join_far(far, near, ids):
        for k, i in zip(FAR, ids):
            recv(i, far.at[lax.rem(zhi + 4 - k, 4)])
        near[y, zlo] = as_tile(join([far[n] for n in range(4)]))
        return pair_send(near)

    def join_all(near, ids):
        pair_wait(near, ids)
        return join([near[m, n] for m in range(4) for n in range(4)])


    for n, ids_y in enumerate(hid_y):
        at = zlo if n == 0 else lax.rem(zlo + 16 - NEAR[n - 1], 4)
        for k, i in zip(FAR, ids_y):
            yy = lax.rem(y + 4 - k, 4)
            recv(i, G.at[yy, at])
            spread(yy, at)

    slices = []
    for k in range(1, 8):
        peer = lax.rem(d + k, 8)
        src = G.at[:, pl.ds(lax.rem(2 * peer, 4), 2), lax.div(peer, 2)]
        slices.append(send(src, HG.at[d], dp_dev(k)))

    LG[...] = dot(hwx[...], WT[...])
    words = LG[0:160, :]
    head_goal = jnp.where(cluster == 0, target, -1) - v * 160
    head_hit = rows_of((160, 256)) == head_goal
    high = jnp.max(words, axis=0, keepdims=True)
    total = jnp.sum(jnp.exp(words - high), axis=0, keepdims=True)
    picked = jnp.sum(jnp.where(head_hit, words, 0.0), axis=0, keepdims=True)
    STF[zhi] = as_tile((high, total, picked))
    head_ids = [send(STF.at[zhi], STF.at[zhi], far_dev(k)) for k in FAR]
    tail_ids = join_far(TTF, TTN, tail_ids)
    pj_c = dp_core(PJv, pj_x)
    tail_stats = join_all(TTN, tail_ids)

    tail_lse = tail_stats[0] + jnp.log(tail_stats[1])
    TS[...] = jnp.zeros_like(TS)
    TS[0:1, :] = tail_lse
    TS[1:2, :] = tail_lse - tail_stats[2]
    columns = jnp.transpose(TS[...])[0:80, :]
    lse_col = jnp.where(live, columns[:, 0:1], 1e30)
    loss_col = columns[:, 1:2]

    def tail_gradient(values, lse, goals):
        hit = (lanes(values.shape) == goals).astype(F32)
        return (SCALE * (jnp.exp(values - lse) - hit)).astype(BF16)

    own1 = tail_gradient(L1s[...], lse_col[0:40], goal[0:40] - v * 320)
    own2 = tail_gradient(L2s[...], lse_col[40:80], goal[40:80] - v * 1664)
    to_tiles(BT, dot(own1, t1_ref[...]), dot(own2, t2_ref[...]))
    bk_y = small_y(BT, BRY)

    head_ids = join_far(STF, STN, head_ids)
    INF[d] = jnp.where(lane == 0, lse_col, jnp.where(lane == 1, goal.astype(F32), 0.0))
    INFv = INF.reshape(4, 2, 80, 128)
    inf_x = dp_x(INFv)
    bk_n = small_near(BT, BRY, bk_y, BS1, BRN)
    stats = join_all(STN, head_ids)

    entry0, entry1 = LG[160:161, :], LG[161:162, :]
    top = jnp.maximum(stats[0], jnp.maximum(entry0, entry1))
    summed = stats[1] * jnp.exp(stats[0] - top) + (jnp.exp(entry0 - top) + jnp.exp(entry1 - top))
    lse = top + jnp.log(summed)
    is1, is2 = (cluster == 1).astype(F32), (cluster == 2).astype(F32)
    chosen_logit = stats[2] + (is1 * entry0 + is2 * entry1)
    tail_loss = jnp.sum(jnp.where(slot_hit, loss_col, 0.0), axis=0, keepdims=True)
    loss_ref[...] = ((lse - chosen_logit) + tail_loss)[:, 0:160]
    store(loss_ref, loss_out)

    inside = lanes((160, 256)) < 160
    grad = jnp.where(inside, SCALE * (jnp.exp(LG[0:160, :] - lse) - head_hit.astype(F32)), 0.0)
    inside1 = lanes((1, 256)) < 160
    ge0 = jnp.where(inside1, SCALE * (jnp.exp(entry0 - lse) - is1), 0.0)
    ge1 = jnp.where(inside1, SCALE * (jnp.exp(entry1 - lse) - is2), 0.0)
    GP[d, 0:160, :] = grad[:, 0:128].astype(BF16)
    rounded_rest = grad[:, 128:256]
    GP[d, 160:208, :] = pack_rest(rounded_rest, 48).astype(BF16)
    GPv = GP.reshape(4, 2, 208, 128)
    gp_x = dp_x(GPv)

    row96 = rows_of((96, 256))
    mine = (v == 0).astype(F32)
    low = jnp.where(row96 == 0, ge0 * mine, jnp.where(row96 == 1, ge1 * mine, 0.0))
    grad_ext = jnp.concatenate([grad, low], axis=0).astype(BF16)

    gh_y = []

    def part(o):
        at = lax.rem(zlo + o, 4)
        for zh in range(4):
            rows = pl.ds(pl.multiple_of((zh * 4 + at) * 256, 256), 256)
            product = dot(hwxT[rows, :], grad_ext)
            for yy in range(4):
                block = GB.at[yy, at, zh]
                piece = product[64 * yy : 64 * yy + 64]
                block[0:64, :] = piece[:, 0:128].astype(BF16)
                block[64:80, :] = pack_rest(piece[:, 128:256], 16).astype(BF16)
        gh_y.append(
            [send(GB.at[lax.rem(y + k, 4), at], GRY.at[k - 1, at], y_dev(k)) for k in FAR]
        )

    part(NEAR[0])
    part(NEAR[2])
    bk_f = small_far(BS1, BRN, bk_n, BRF)
    part(NEAR[1])
    part(0)
    entries = jnp.where(rows_of((8, 256)) % 2 == 0, ge0, ge1).astype(BF16)
    full = dot(entries, WT[...], NT)
    pair = lax.div(rows_of((8, 1024)), 2)
    packed_cl = jnp.zeros((8, 1024), F32)
    for k in range(4):
        packed_cl = jnp.where(pair == k, full[:, 1024 * k : 1024 * k + 1024], packed_cl)
    GC[d] = packed_cl
    GCv = GC.reshape(4, 2, 8, 1024)
    gc_x = dp_x(GCv)
    order = (0, 2, 1)
    gh_n = {}

    def y_sum(at, ids):
        for k, i in zip(FAR, ids):
            recv(i, GRY.at[k - 1, at])
        return (GB[y, at].astype(F32) + GRY[0, at].astype(F32)) + (
            GRY[1, at].astype(F32) + GRY[2, at].astype(F32)
        )

    def chunk_near(turn_at):
        n = order[turn_at]
        GS1[n] = y_sum(lax.rem(zlo + NEAR[n], 4), gh_y[turn_at]).astype(BF16)
        gh_n[n] = send(GS1.at[n], GRN.at[n], near_dev(NEAR[n]))

    chunk_near(0)
    inf_c = dp_core(INFv, inf_x)
    gp_c = dp_core(GPv, gp_x)
    def assemble(src, dst1, dst2):
        for g in range(8):
            both = src[g].astype(F32)
            dst1[40 * g : 40 * g + 40, 0:640] = both[0:40, :]
            dst1[40 * g : 40 * g + 40, 640:1024] = both[40:80, 0:384]
            dst2[40 * g : 40 * g + 40, :] = both[40:80, 384:640]

    dp_done(PJv, pj_c)
    dp_done(INFv, inf_c)
    assemble(PJ, P1f, P2f)
    P1b[...] = P1f[...].astype(BF16)
    P2b[...] = P2f[...].astype(BF16)

    def gather_column(lo, lane_at):
        return jnp.concatenate([INF[g, lo : lo + 40, lane_at : lane_at + 1] for g in range(8)], axis=0)

    lse1, goal1 = gather_column(0, 0), gather_column(0, 1).astype(jnp.int32)
    all1 = dot(P1b[...], t1_ref[...], NT)
    base1 = jnp.where(goal1 < 0, -(1 << 20), goal1 - v * 320)
    grad1 = tail_gradient(all1, lse1, base1)
    gt1_ref[...] = dot(grad1, P1b[:, pl.ds(pl.multiple_of(d * 128, 128), 128)], TN)
    store(gt1_ref, gt1_out)

    lse2, goal2 = gather_column(40, 0), gather_column(40, 1).astype(jnp.int32)
    base2 = jnp.where(goal2 < 0, -(1 << 20), goal2 - v * 1664)
    select = jnp.where(lanes((32, 256)) == rows_of((32, 256)) + d * 32, 1.0, 0.0).astype(BF16)
    mine2 = dot(select, P2b[...], NT).astype(BF16)
    P1f[:, 0:128] = jnp.broadcast_to(lse2, (320, 128))
    P1f[:, 128:256] = jnp.broadcast_to(base2.astype(F32), (320, 128))

    def tail_two(j, _):
        at = pl.multiple_of(j * 128, 128)
        logits = dot(P2b[...], t2_ref[pl.ds(at, 128), :], NT)
        hit = (lanes((320, 128)).astype(F32) + (j * 128).astype(F32)) == P1f[:, 128:256]
        grads = (SCALE * (jnp.exp(logits - P1f[:, 0:128]) - hit.astype(F32))).astype(BF16)
        gt2_ref[:, pl.ds(at, 128)] = dot(mine2, grads)
        return 0

    chunk_near(1)
    small_total(BRF, bk_f, BG)
    bk_all = pair_send(BG)
    lax.fori_loop(0, 6, tail_two, 0)
    chunk_near(2)
    mine_sum = y_sum(zlo, gh_y[3])
    for n in range(3):
        recv(gh_n[n], GRN.at[n])
    GS2[...] = mine_sum + (
        GRN[0].astype(F32) + (GRN[1].astype(F32) + GRN[2].astype(F32))
    )
    for k in FAR:
        GRF[2 + k] = GS2[lax.rem(zhi + k, 4)].astype(BF16)
    gh_f = [send(GRF.at[2 + k], GRF.at[k - 1], far_dev(k)) for k in FAR]
    small_done(BG, bk_all)
    BK[d] = Xf[...].astype(BF16)
    BKv = BK.reshape(4, 2, 80, 640)
    bk_x = dp_x(BKv)

    gc_c = dp_core(GCv, gc_x)
    lax.fori_loop(6, 13, tail_two, 0)
    store(gt2_ref, gt2_out)
    HG[d] = G[:, pl.ds(lax.rem(2 * d, 4), 2), lax.div(d, 2)]
    dp_done(GPv, gp_c)
    for k, i in zip(range(1, 8), slices):
        recv(i, HG.at[lax.rem(d + 8 - k, 8)])
    head_ref[...] = jnp.zeros_like(head_ref)

    def head_group(g, _):
        GU[:, 0:128] = GP[g, 0:160, :]
        rest = GP[g, 160:208, :].astype(F32)
        for q in range(4):
            rows = 48 if q < 3 else 16
            GU[48 * q : 48 * q + rows, 128:256] = unpack_rest(rest[0:rows], q)
        for b in range(8):
            block = HG.at[g, b % 4, b // 4]
            HU[64 * b : 64 * b + 64, 0:128] = block[0:64, :]
            packed = block[64:80, :].astype(F32)
            for q in range(4):
                HU[64 * b + 16 * q : 64 * b + 16 * q + 16, 128:256] = unpack_rest(packed, q)
        head_ref[...] += dot(GU[...], HU[...], NT)
        return 0

    lax.fori_loop(0, 8, head_group, 0)
    store(head_ref, head_out)

    dp_done(GCv, gc_c)
    cl_sum = ((GC[0] + GC[1]) + (GC[2] + GC[3])) + ((GC[4] + GC[5]) + (GC[6] + GC[7]))
    for k in range(4):
        cl_ref[:, 1024 * k : 1024 * k + 1024] = cl_sum[2 * k : 2 * k + 2, :]
    store(cl_ref, cl_out)

    both = BK[d].astype(F32)
    b1a, b1b = both[0:40, :].astype(BF16), both[40:80, 0:384].astype(BF16)
    b2 = both[40:80, 384:640].astype(BF16)
    hot1 = jnp.where(slot_hit[0:40], 1.0, 0.0)
    hot2 = jnp.where(slot_hit[40:80], 1.0, 0.0)
    back_one = dot(p1_ref[:, 0:640], b1a, NT) + dot(p1_ref[:, 640:1024], b1b, NT)
    add = dot_exact(back_one, hot1) + dot_exact(dot(p2_ref[...], b2, NT), hot2)
    bk_c = dp_core(BKv, bk_x)

    for n, i in enumerate(gh_f):
        recv(i, GRF.at[n])
    block = GS2[zhi] + (GRF[0].astype(F32) + (GRF[1].astype(F32) + GRF[2].astype(F32)))
    hp[:, 0:128] = block[0:64, :]
    for q in range(4):
        part_q = block[64:80, :]
        hp[16 * q : 16 * q + 16, 128:256] = part_q if q == 0 else pltpu.roll(part_q, 128 - 32 * q, 1)
    gh_ref[...] = (hp[...] + add)[:, 0:160]
    store(gh_ref, gh_out)

    dp_done(CHv, ch_c)
    dp_done(BKv, bk_c)
    assemble(BK, P1f, P2f)
    for g in range(8):
        rows_g = CH[g].astype(F32)
        C1f[40 * g : 40 * g + 40, :] = rows_g[0:40, :]
        C2f[40 * g : 40 * g + 40, :] = rows_g[40:80, :]
    gp1_ref[...] = dot(C1f[...].astype(BF16), P1f[...].astype(BF16), TN)[0:64, :]
    store(gp1_ref, gp1_out)
    gp2_ref[...] = dot(C2f[...].astype(BF16), P2f[...].astype(BF16), TN)[0:64, :]
    store(gp2_ref, gp2_out)
    for copy in stores:
        copy.wait()

    for copy in sent:
        copy.wait_send()


def hand_over(*refs):
    for i in range(8):
        refs[8 + i][...] = refs[i][...]


def on_device(
    hidden_states, head_weight, cluster_weight, proj_one, tail_one, proj_two, tail_two,
    targets, token_cluster, tail_rows, tail_counts,
):
    vmem = pl.BlockSpec(memory_space=pltpu.VMEM)
    hbm = pl.BlockSpec(memory_space=pl.ANY)
    shapes = [
        ((1, 160), F32), ((64, 160), F32), ((160, 512), F32), ((2, 4096), F32),
        ((64, 1024), F32), ((320, 128), F32), ((64, 256), F32), ((32, 1664), F32),
    ]
    V = pltpu.VMEM
    scratch = [
        V((64, 160), BF16), V((64, 1024), BF16), V((64, 256), BF16), V((1, 160), jnp.int32),
        V((1, 160), jnp.int32), V((2, 40), jnp.int32), V((1, 2), jnp.int32),
    ] + [V(s, t) for s, t in shapes] + [
        V((320, 1024), BF16), V((1664, 256), BF16), V((2, 256), jnp.int32),
        V((64, 256), F32), V((4, 4, 4, 80, 128), BF16), V((4096, 256), BF16), V((256, 4096), BF16),
        V((4096, 256), BF16), V((8, 4, 2, 80, 128), BF16), V((512, 256), BF16),
        V((8, 80, 128), BF16), V((4, 4, 4, 8, 128), F32), V((3, 4, 4, 8, 128), F32),
        V((3, 4, 8, 128), F32), V((4, 4, 8, 128), F32), V((4, 4, 8, 128), F32),
        V((4, 4, 4, 8, 128), F32), V((80, 640), F32), V((8, 80, 640), BF16),
        V((320, 1024), F32), V((320, 256), F32), V((320, 1024), BF16), V((320, 256), BF16),
        V((4, 8, 256), F32), V((4, 4, 8, 256), F32),
        V((4, 8, 128), F32), V((4, 4, 8, 128), F32), V((128, 128), F32),
        V((256, 256), F32), V((40, 320), F32), V((40, 1664), F32), V((8, 80, 128), F32),
        V((8, 208, 128), BF16), V((160, 256), BF16), V((8, 8, 1024), F32),
        V((4, 4, 4, 8, 128), F32), V((3, 4, 4, 8, 128), F32), V((3, 4, 8, 128), F32), V((4, 4, 8, 128), F32),
        V((4, 4, 8, 128), F32), V((4, 4, 4, 8, 128), F32), V((8, 80, 640), BF16),
        V((320, 128), F32), V((320, 128), F32),
        V((4, 4, 4, 80, 128), BF16), V((3, 4, 4, 80, 128), BF16), V((3, 4, 80, 128), BF16),
        V((3, 4, 80, 128), BF16), V((4, 80, 128), F32), V((6, 80, 128), BF16),
        pltpu.SemaphoreType.DMA((SEMS,)), pltpu.SemaphoreType.DMA((SEMS,)), pltpu.SemaphoreType.DMA,
        pltpu.SemaphoreType.DMA((2,)), pltpu.SemaphoreType.DMA((7,)), pltpu.SemaphoreType.DMA((8,)),
    ]
    out = pl.pallas_call(
        kernel,
        out_shape=[jax.ShapeDtypeStruct(s, t) for s, t in shapes],
        in_specs=[hbm, hbm, vmem] + [hbm] * 8,
        out_specs=[hbm] * 8,
        scratch_shapes=scratch,
        compiler_params=pltpu.CompilerParams(
            collective_id=0, has_side_effects=True, vmem_limit_bytes=56 * 1024 * 1024
        ),
    )(
        hidden_states.T, head_weight, cluster_weight, proj_one, tail_one, proj_two, tail_two,
        targets.reshape(1, 160), token_cluster.reshape(1, 160), tail_rows[0], tail_counts,
    )
    loss, gh, head, cl, gp1, gt1, gp2, gt2 = pl.pallas_call(
        hand_over,
        out_shape=[jax.ShapeDtypeStruct(s, t) for s, t in shapes],
        in_specs=[vmem] * 8,
        out_specs=[vmem] * 8,
    )(*out)
    return (
        loss.reshape(160),
        gh.T,
        head,
        cl,
        gp1,
        gt1,
        gp2,
        gt2.T,
    )


def solution(mesh):
    return jax.shard_map(
        on_device,
        mesh=mesh,
        in_specs=(
            P("dp", "vocab"), P("vocab", None), P(), P("vocab", None), P("vocab", None),
            P("vocab", None), P("vocab", None), P("dp"), P("dp"), P("dp", None, None), P("dp", None),
        ),
        out_specs=(
            P("dp"), P("dp", "vocab"), P("vocab", "dp"), P(), P("vocab", None),
            P("vocab", "dp"), P("vocab", None), P("vocab", "dp"),
        ),
        check_vma=False,
    )
```

```python
import jax
import jax.numpy as jnp
from jax import lax
from jax.experimental import pallas as pl
from jax.experimental.pallas import tpu as pltpu
from jax.sharding import PartitionSpec as P

MESH = pl.DeviceIdType.MESH
F32 = jnp.float32
BF16 = jnp.bfloat16
SCALE = 64.0
FAR = (1, 2, 3)
NEAR = (1, 15, 2)
PAIRS = tuple((o, k) for o in (0,) + NEAR for k in (0,) + FAR)[1:]
SEMS = 176
NT = (((1,), (1,)), ((), ()))
TN = (((0,), (0,)), ((), ()))
NN = (((1,), (0,)), ((), ()))


def dot(a, b, dims=NN):
    return lax.dot_general(a, b, dims, preferred_element_type=F32)


def dot_exact(a, b):
    return lax.dot_general(a, b, NN, precision=lax.Precision.HIGHEST, preferred_element_type=F32)


def lanes(shape):
    return lax.broadcasted_iota(jnp.int32, shape, len(shape) - 1)


def rows_of(shape):
    return lax.broadcasted_iota(jnp.int32, shape, len(shape) - 2)


def pack_rest(rest, height):
    out = None
    total = rest.shape[0]
    for q in range(4):
        lo, hi = q * height, min((q + 1) * height, total)
        part = rest[lo:hi]
        if q:
            part = pltpu.roll(part, 32 * q, 1)
        if hi - lo < height:
            part = jnp.concatenate([part, jnp.zeros((height - (hi - lo), 128), F32)], axis=0)
        out = part if out is None else out + part
    return out


def unpack_rest(packed, q):
    part = packed if q == 0 else pltpu.roll(packed, 128 - 32 * q, 1)
    return jnp.where(lanes(part.shape) < 32, part, 0.0).astype(BF16)


def kernel(
    hid_hbm, hw_ref, cw_ref, p1_hbm, t1_hbm, p2_hbm, t2_hbm, tgt_hbm, clu_hbm, rows_hbm, count_hbm,
    loss_out, gh_out, head_out, cl_out, gp1_out, gt1_out, gp2_out, gt2_out,
    hid_ref, p1_ref, p2_ref, tgt_ref, clu_ref, rows_ref, count_ref,
    loss_ref, gh_ref, head_ref, cl_ref, gp1_ref, gt1_ref, gp2_ref, gt2_ref,
    t1_ref, t2_ref, ids, hp, G, WT, hwx, hwxT, HG, HU,
    CH, PT, PRY, PRN, PRF, PS1, PG, Xf, PJ,
    P1f, P2f, P1b, P2b,
    STF, STN, TTF, TTN, TS,
    LG, L1s, L2s, INF, GP, GU, GC,
    BT, BRY, BRN, BRF, BS1, BG, BK, C1f, C2f,
    GB, GRY, GS1, GRN, GS2, GRF,
    ssem, rsem, lsem, tsem, isem, osem,
):
    d = lax.axis_index("dp")
    v = lax.axis_index("vocab")
    x, c = lax.div(d, 2), lax.rem(d, 2)
    z, y = lax.div(v, 4), lax.rem(v, 4)
    zhi, zlo = lax.div(z, 4), lax.rem(z, 4)

    def far_dev(k):
        return (d, lax.rem(z + 4 * k, 16) * 4 + y)

    def near_dev(o):
        return (d, lax.rem(z + o, 16) * 4 + y)

    def pair_dev(o, k):
        return (d, lax.rem(z + o, 16) * 4 + lax.rem(y + k, 4))

    def y_dev(k):
        return (d, z * 4 + lax.rem(y + k, 4))

    def x_dev(k):
        return (lax.rem(x + k, 4) * 2 + c, v)

    core_dev = (x * 2 + 1 - c, v)

    def dp_dev(k):
        return (lax.rem(d + k, 8), v)

    counter = [0]
    sent = []

    def send(src, dst, dev):
        i = counter[0]
        counter[0] += 1
        copy = pltpu.make_async_remote_copy(
            src_ref=src, dst_ref=dst, send_sem=ssem.at[i], recv_sem=rsem.at[i],
            device_id=dev, device_id_type=MESH,
        )
        copy.start()
        sent.append(copy)
        return i

    def recv(i, slot):
        pltpu.make_async_remote_copy(
            src_ref=slot, dst_ref=slot, send_sem=ssem.at[i], recv_sem=rsem.at[i],
            device_id=core_dev, device_id_type=MESH,
        ).wait_recv()

    barrier = pltpu.get_barrier_semaphore()
    greeted = 0
    for k in FAR:
        pl.semaphore_signal(barrier, inc=1, device_id=far_dev(k), device_id_type=MESH)
        greeted += 1
    for o, k in PAIRS:
        pl.semaphore_signal(barrier, inc=1, device_id=pair_dev(16 - o, 4 - k), device_id_type=MESH)
        greeted += 1
    for k in range(1, 8):
        pl.semaphore_signal(barrier, inc=1, device_id=dp_dev(k), device_id_type=MESH)
        greeted += 1

    loads = [
        pltpu.make_async_copy(src, dst, isem.at[n])
        for n, (src, dst) in enumerate(
            (
                (hid_hbm, hid_ref), (rows_hbm, rows_ref), (count_hbm, count_ref), (tgt_hbm, tgt_ref),
                (clu_hbm, clu_ref), (p1_hbm, p1_ref), (p2_hbm, p2_ref),
            )
        )
    ]
    hw_copy = pltpu.make_async_copy(hw_ref, hwx.at[0:160], lsem)
    t1_copy = pltpu.make_async_copy(t1_hbm, t1_ref, tsem.at[0])
    t2_copy = pltpu.make_async_copy(t2_hbm, t2_ref, tsem.at[1])
    for copy in loads:
        copy.start()
    hw_copy.start()
    t1_copy.start()
    t2_copy.start()
    stores = []

    def store(src, dst):
        copy = pltpu.make_async_copy(src, dst, osem.at[len(stores)])
        copy.start()
        stores.append(copy)

    for copy in loads:
        copy.wait()

    hp[...] = jnp.zeros_like(hp)
    hp[:, 0:160] = hid_ref[...].astype(F32)
    G[y, zlo, zhi, 0:64, :] = hp[:, 0:128].astype(BF16)
    G[y, zlo, zhi, 64:80, :] = pack_rest(hp[:, 128:256], 16).astype(BF16)

    TS[...] = jnp.zeros_like(TS)
    lane40 = lanes((1, 40))
    for n in range(2):
        TS[n : n + 1, 0:40] = jnp.where(
            lane40 < count_ref[0:1, n : n + 1], rows_ref[n : n + 1, :], -1
        ).astype(F32)
    turned = jnp.transpose(TS[...])
    row_col = jnp.concatenate([turned[0:40, 0:1], turned[0:40, 1:2]], axis=0).astype(jnp.int32)
    ids[...] = jnp.full((2, 256), -1, jnp.int32)
    ids[0:1, 0:160] = tgt_ref[...]
    ids[1:2, 0:160] = clu_ref[...]
    target = ids[0:1, :]
    cluster = ids[1:2, :]
    slot_hit = lanes((80, 256)) == row_col
    onehot = jnp.where(slot_hit, 1.0, 0.0).astype(BF16)
    live = row_col >= 0
    goal = jnp.sum(jnp.where(slot_hit, target, 0).astype(F32), axis=1, keepdims=True).astype(jnp.int32)
    goal = jnp.where(live, goal, -1)

    hidb = hp[...].astype(BF16)
    chosen = dot(onehot, hidb, NT)
    CH[d, :, 64:128] = jnp.zeros((80, 64), BF16)
    CH[d, :, 0:64] = chosen.astype(BF16)
    part1 = dot(chosen[0:40].astype(BF16), p1_ref[...])
    part2 = dot(chosen[40:80].astype(BF16), p2_ref[...])

    def to_tiles(tiles, a, b):
        for t in range(64):
            at = tiles.at[t // 16, (t // 4) % 4, t % 4]
            i, j = t // 10, t % 10
            if t >= 50:
                at[...] = jnp.zeros((8, 128), F32)
            elif j < 8:
                at[...] = a[8 * i : 8 * i + 8, 128 * j : 128 * j + 128]
            else:
                at[...] = b[8 * i : 8 * i + 8, 128 * j - 1024 : 128 * j - 896]

    to_tiles(PT, part1, part2)

    pl.semaphore_wait(barrier, greeted)

    own = G.at[y, zlo, zhi]
    hid_far = [send(own, own, far_dev(k)) for k in FAR]

    def small_y(tiles, slots):
        return [send(tiles.at[lax.rem(y + k, 4)], slots.at[k - 1], y_dev(k)) for k in FAR]

    def small_near(tiles, slots, ids, sums, nslots):
        for n, i in enumerate(ids):
            recv(i, slots.at[n])
        sums[...] = (tiles[y] + slots[0]) + (slots[1] + slots[2])
        return [
            send(sums.at[lax.rem(zlo + o, 4)], nslots.at[n], near_dev(o))
            for n, o in enumerate(NEAR)
        ]

    def small_far(sums, nslots, ids, fslots):
        for n, i in enumerate(ids):
            recv(i, nslots.at[n])
        fslots[zhi] = (sums[zlo] + nslots[0]) + (nslots[1] + nslots[2])
        return [send(fslots.at[zhi], fslots.at[zhi], far_dev(k)) for k in FAR]

    def small_total(fslots, ids, full):
        for k, i in zip(FAR, ids):
            recv(i, fslots.at[lax.rem(zhi + 4 - k, 4)])
        full[y, zlo] = (fslots[0] + fslots[1]) + (fslots[2] + fslots[3])

    def pair_send(full):
        own_entry = full.at[y, zlo]
        return [send(own_entry, own_entry, pair_dev(o, k)) for o, k in PAIRS]

    def pair_wait(full, ids):
        for (o, k), i in zip(PAIRS, ids):
            recv(i, full.at[lax.rem(y + 4 - k, 4), lax.rem(zlo + 16 - o, 4)])

    def small_done(full, ids):
        pair_wait(full, ids)
        for t in range(50):
            i, j = t // 10, t % 10
            r, l = (8 * i, 128 * j) if j < 5 else (40 + 8 * i, 128 * j - 640)
            Xf[r : r + 8, l : l + 128] = full[t // 16, (t // 4) % 4, t % 4]

    def dp_x(buf):
        return [send(buf.at[x, c], buf.at[x, c], x_dev(k)) for k in FAR]

    def dp_core(buf, ids):
        for k, i in zip(FAR, ids):
            recv(i, buf.at[lax.rem(x + 4 - k, 4), c])
        return send(buf.at[:, c], buf.at[:, c], core_dev)

    def dp_done(buf, i):
        recv(i, buf.at[:, 1 - c])

    pr_y = small_y(PT, PRY)
    CHv = CH.reshape(4, 2, 80, 128)
    ch_x = dp_x(CHv)

    cw = cw_ref[...].astype(F32)
    row16 = rows_of((16, 4096))
    hwx[160:176, :] = jnp.where(
        row16 == 0, cw[0:1, :], jnp.where(row16 == 1, cw[1:2, :], 0.0)
    ).astype(BF16)
    hwx[176:256, :] = jnp.zeros((80, 4096), BF16)
    hw_copy.wait()

    def turn(j, _):
        at = pl.ds(pl.multiple_of(j * 128, 128), 128)
        hwxT[at, :] = jnp.transpose(hwx[:, at])
        return 0

    def spread(yy, zl):
        for zh in range(4):
            block = G.at[yy, zl, zh]
            base = pl.multiple_of(((zh * 4 + zl) * 4 + yy) * 64, 64)
            WT[pl.ds(base, 64), 0:128] = block[0:64, :]
            packed = block[64:80, :].astype(F32)
            for q in range(4):
                WT[pl.ds(pl.multiple_of(base + 16 * q, 16), 16), 128:256] = unpack_rest(packed, q)

    pr_n = small_near(PT, PRY, pr_y, PS1, PRN)
    lax.fori_loop(0, 8, turn, 0)
    pr_f = small_far(PS1, PRN, pr_n, PRF)
    for k, i in zip(FAR, hid_far):
        recv(i, G.at[y, zlo, lax.rem(zhi + 4 - k, 4)])
    hid_near = [send(G.at[y, zlo], G.at[y, zlo], near_dev(o)) for o in NEAR]
    hid_y = [[send(G.at[y, zlo], G.at[y, zlo], y_dev(k)) for k in FAR]]
    lax.fori_loop(8, 20, turn, 0)
    spread(y, zlo)

    def pass_on(n):
        at = lax.rem(zlo + 16 - NEAR[n], 4)
        recv(hid_near[n], G.at[y, at])
        hid_y.append([send(G.at[y, at], G.at[y, at], y_dev(k)) for k in FAR])

    small_total(PRF, pr_f, PG)
    pr_all = pair_send(PG)
    pass_on(0)
    pass_on(1)
    pass_on(2)
    ch_c = dp_core(CHv, ch_x)
    lax.fori_loop(20, 32, turn, 0)
    for n in range(3):
        spread(y, lax.rem(zlo + 16 - NEAR[n], 4))
    small_done(PG, pr_all)
    PJ[d] = Xf[...].astype(BF16)
    PJv = PJ.reshape(4, 2, 80, 640)
    pj_x = dp_x(PJv)

    t1_copy.wait()
    t2_copy.wait()
    left, right = Xf[0:40, :].astype(BF16), Xf[40:80, :].astype(BF16)
    log1 = dot(left, t1_ref[:, 0:640], NT) + dot(right[:, 0:384], t1_ref[:, 640:1024], NT)
    log2 = dot(right[:, 384:640], t2_ref[...], NT)
    L1s[...] = log1
    L2s[...] = log2

    def column_stats(values, goals):
        high = jnp.max(values, axis=1, keepdims=True)
        total = jnp.sum(jnp.exp(values - high), axis=1, keepdims=True)
        hit = lanes(values.shape) == goals
        return high, total, jnp.sum(jnp.where(hit, values, 0.0), axis=1, keepdims=True)

    stat1 = column_stats(log1, goal[0:40] - v * 320)
    stat2 = column_stats(log2, goal[40:80] - v * 1664)
    lane = lanes((80, 128))
    table = jnp.zeros((80, 128), F32)
    for n in range(3):
        table = jnp.where(lane == n, jnp.concatenate([stat1[n], stat2[n]], axis=0), table)
    TS[0:80, :] = table
    TS[80:128, :] = jnp.zeros((48, 128), F32)
    TTF[zhi] = jnp.transpose(TS[...])[0:8, :]
    tail_ids = [send(TTF.at[zhi], TTF.at[zhi], far_dev(k)) for k in FAR]

    def join(parts):
        top = parts[0][0:1]
        for p in parts[1:]:
            top = jnp.maximum(top, p[0:1])
        total, picked = 0.0, 0.0
        for p in parts:
            total = total + p[1:2] * jnp.exp(p[0:1] - top)
            picked = picked + p[2:3]
        return top, total, picked

    def as_tile(result):
        row = rows_of((8, result[0].shape[1]))
        return jnp.where(
            row == 0, result[0], jnp.where(row == 1, result[1], jnp.where(row == 2, result[2], 0.0))
        )

    def join_far(far, near, ids):
        for k, i in zip(FAR, ids):
            recv(i, far.at[lax.rem(zhi + 4 - k, 4)])
        near[y, zlo] = as_tile(join([far[n] for n in range(4)]))
        return pair_send(near)

    def join_all(near, ids):
        pair_wait(near, ids)
        return join([near[m, n] for m in range(4) for n in range(4)])


    for n, ids_y in enumerate(hid_y):
        at = zlo if n == 0 else lax.rem(zlo + 16 - NEAR[n - 1], 4)
        for k, i in zip(FAR, ids_y):
            yy = lax.rem(y + 4 - k, 4)
            recv(i, G.at[yy, at])
            spread(yy, at)

    slices = []
    for k in range(1, 8):
        peer = lax.rem(d + k, 8)
        src = G.at[:, pl.ds(lax.rem(2 * peer, 4), 2), lax.div(peer, 2)]
        slices.append(send(src, HG.at[d], dp_dev(k)))

    LG[...] = dot(hwx[...], WT[...])
    words = LG[0:160, :]
    head_goal = jnp.where(cluster == 0, target, -1) - v * 160
    head_hit = rows_of((160, 256)) == head_goal
    high = jnp.max(words, axis=0, keepdims=True)
    total = jnp.sum(jnp.exp(words - high), axis=0, keepdims=True)
    picked = jnp.sum(jnp.where(head_hit, words, 0.0), axis=0, keepdims=True)
    STF[zhi] = as_tile((high, total, picked))
    head_ids = [send(STF.at[zhi], STF.at[zhi], far_dev(k)) for k in FAR]
    tail_ids = join_far(TTF, TTN, tail_ids)
    pj_c = dp_core(PJv, pj_x)
    tail_stats = join_all(TTN, tail_ids)

    tail_lse = tail_stats[0] + jnp.log(tail_stats[1])
    TS[...] = jnp.zeros_like(TS)
    TS[0:1, :] = tail_lse
    TS[1:2, :] = tail_lse - tail_stats[2]
    columns = jnp.transpose(TS[...])[0:80, :]
    lse_col = jnp.where(live, columns[:, 0:1], 1e30)
    loss_col = columns[:, 1:2]

    def tail_gradient(values, lse, goals):
        hit = (lanes(values.shape) == goals).astype(F32)
        return (SCALE * (jnp.exp(values - lse) - hit)).astype(BF16)

    own1 = tail_gradient(L1s[...], lse_col[0:40], goal[0:40] - v * 320)
    own2 = tail_gradient(L2s[...], lse_col[40:80], goal[40:80] - v * 1664)
    to_tiles(BT, dot(own1, t1_ref[...]), dot(own2, t2_ref[...]))
    bk_y = small_y(BT, BRY)

    head_ids = join_far(STF, STN, head_ids)
    INF[d] = jnp.where(lane == 0, lse_col, jnp.where(lane == 1, goal.astype(F32), 0.0))
    INFv = INF.reshape(4, 2, 80, 128)
    inf_x = dp_x(INFv)
    bk_n = small_near(BT, BRY, bk_y, BS1, BRN)
    stats = join_all(STN, head_ids)

    entry0, entry1 = LG[160:161, :], LG[161:162, :]
    top = jnp.maximum(stats[0], jnp.maximum(entry0, entry1))
    summed = stats[1] * jnp.exp(stats[0] - top) + (jnp.exp(entry0 - top) + jnp.exp(entry1 - top))
    lse = top + jnp.log(summed)
    is1, is2 = (cluster == 1).astype(F32), (cluster == 2).astype(F32)
    chosen_logit = stats[2] + (is1 * entry0 + is2 * entry1)
    tail_loss = jnp.sum(jnp.where(slot_hit, loss_col, 0.0), axis=0, keepdims=True)
    loss_ref[...] = ((lse - chosen_logit) + tail_loss)[:, 0:160]
    store(loss_ref, loss_out)

    inside = lanes((160, 256)) < 160
    grad = jnp.where(inside, SCALE * (jnp.exp(LG[0:160, :] - lse) - head_hit.astype(F32)), 0.0)
    inside1 = lanes((1, 256)) < 160
    ge0 = jnp.where(inside1, SCALE * (jnp.exp(entry0 - lse) - is1), 0.0)
    ge1 = jnp.where(inside1, SCALE * (jnp.exp(entry1 - lse) - is2), 0.0)
    GP[d, 0:160, :] = grad[:, 0:128].astype(BF16)
    rounded_rest = grad[:, 128:256]
    GP[d, 160:208, :] = pack_rest(rounded_rest, 48).astype(BF16)
    GPv = GP.reshape(4, 2, 208, 128)
    gp_x = dp_x(GPv)

    row96 = rows_of((96, 256))
    mine = (v == 0).astype(F32)
    low = jnp.where(row96 == 0, ge0 * mine, jnp.where(row96 == 1, ge1 * mine, 0.0))
    grad_ext = jnp.concatenate([grad, low], axis=0).astype(BF16)

    gh_y = []

    def part(o):
        at = lax.rem(zlo + o, 4)
        for zh in range(4):
            rows = pl.ds(pl.multiple_of((zh * 4 + at) * 256, 256), 256)
            product = dot(hwxT[rows, :], grad_ext)
            for yy in range(4):
                block = GB.at[yy, at, zh]
                piece = product[64 * yy : 64 * yy + 64]
                block[0:64, :] = piece[:, 0:128].astype(BF16)
                block[64:80, :] = pack_rest(piece[:, 128:256], 16).astype(BF16)
        gh_y.append(
            [send(GB.at[lax.rem(y + k, 4), at], GRY.at[k - 1, at], y_dev(k)) for k in FAR]
        )

    part(NEAR[0])
    part(NEAR[2])
    bk_f = small_far(BS1, BRN, bk_n, BRF)
    part(NEAR[1])
    part(0)
    entries = jnp.where(rows_of((8, 256)) % 2 == 0, ge0, ge1).astype(BF16)
    full = dot(entries, WT[...], NT)
    pair = lax.div(rows_of((8, 1024)), 2)
    packed_cl = jnp.zeros((8, 1024), F32)
    for k in range(4):
        packed_cl = jnp.where(pair == k, full[:, 1024 * k : 1024 * k + 1024], packed_cl)
    GC[d] = packed_cl
    GCv = GC.reshape(4, 2, 8, 1024)
    gc_x = dp_x(GCv)
    order = (0, 2, 1)
    gh_n = {}

    def y_sum(at, ids):
        for k, i in zip(FAR, ids):
            recv(i, GRY.at[k - 1, at])
        return (GB[y, at].astype(F32) + GRY[0, at].astype(F32)) + (
            GRY[1, at].astype(F32) + GRY[2, at].astype(F32)
        )

    def chunk_near(turn_at):
        n = order[turn_at]
        GS1[n] = y_sum(lax.rem(zlo + NEAR[n], 4), gh_y[turn_at]).astype(BF16)
        gh_n[n] = send(GS1.at[n], GRN.at[n], near_dev(NEAR[n]))

    chunk_near(0)
    inf_c = dp_core(INFv, inf_x)
    gp_c = dp_core(GPv, gp_x)
    def assemble(src, dst1, dst2):
        for g in range(8):
            both = src[g].astype(F32)
            dst1[40 * g : 40 * g + 40, 0:640] = both[0:40, :]
            dst1[40 * g : 40 * g + 40, 640:1024] = both[40:80, 0:384]
            dst2[40 * g : 40 * g + 40, :] = both[40:80, 384:640]

    dp_done(PJv, pj_c)
    dp_done(INFv, inf_c)
    assemble(PJ, P1f, P2f)
    P1b[...] = P1f[...].astype(BF16)
    P2b[...] = P2f[...].astype(BF16)

    def gather_column(lo, lane_at):
        return jnp.concatenate([INF[g, lo : lo + 40, lane_at : lane_at + 1] for g in range(8)], axis=0)

    lse1, goal1 = gather_column(0, 0), gather_column(0, 1).astype(jnp.int32)
    all1 = dot(P1b[...], t1_ref[...], NT)
    base1 = jnp.where(goal1 < 0, -(1 << 20), goal1 - v * 320)
    grad1 = tail_gradient(all1, lse1, base1)
    gt1_ref[...] = dot(grad1, P1b[:, pl.ds(pl.multiple_of(d * 128, 128), 128)], TN)
    store(gt1_ref, gt1_out)

    lse2, goal2 = gather_column(40, 0), gather_column(40, 1).astype(jnp.int32)
    base2 = jnp.where(goal2 < 0, -(1 << 20), goal2 - v * 1664)
    select = jnp.where(lanes((32, 256)) == rows_of((32, 256)) + d * 32, 1.0, 0.0).astype(BF16)
    mine2 = dot(select, P2b[...], NT).astype(BF16)
    P1f[:, 0:128] = jnp.broadcast_to(lse2, (320, 128))
    P1f[:, 128:256] = jnp.broadcast_to(base2.astype(F32), (320, 128))

    def tail_two(j, _):
        at = pl.multiple_of(j * 128, 128)
        logits = dot(P2b[...], t2_ref[pl.ds(at, 128), :], NT)
        hit = (lanes((320, 128)).astype(F32) + (j * 128).astype(F32)) == P1f[:, 128:256]
        grads = (SCALE * (jnp.exp(logits - P1f[:, 0:128]) - hit.astype(F32))).astype(BF16)
        gt2_ref[:, pl.ds(at, 128)] = dot(mine2, grads)
        return 0

    chunk_near(1)
    small_total(BRF, bk_f, BG)
    bk_all = pair_send(BG)
    lax.fori_loop(0, 6, tail_two, 0)
    chunk_near(2)
    mine_sum = y_sum(zlo, gh_y[3])
    for n in range(3):
        recv(gh_n[n], GRN.at[n])
    GS2[...] = mine_sum + (
        GRN[0].astype(F32) + (GRN[1].astype(F32) + GRN[2].astype(F32))
    )
    for k in FAR:
        GRF[2 + k] = GS2[lax.rem(zhi + k, 4)].astype(BF16)
    gh_f = [send(GRF.at[2 + k], GRF.at[k - 1], far_dev(k)) for k in FAR]
    small_done(BG, bk_all)
    BK[d] = Xf[...].astype(BF16)
    BKv = BK.reshape(4, 2, 80, 640)
    bk_x = dp_x(BKv)

    gc_c = dp_core(GCv, gc_x)
    lax.fori_loop(6, 13, tail_two, 0)
    store(gt2_ref, gt2_out)
    HG[d] = G[:, pl.ds(lax.rem(2 * d, 4), 2), lax.div(d, 2)]
    dp_done(GPv, gp_c)
    for k, i in zip(range(1, 8), slices):
        recv(i, HG.at[lax.rem(d + 8 - k, 8)])
    head_ref[...] = jnp.zeros_like(head_ref)

    def head_group(g, _):
        GU[:, 0:128] = GP[g, 0:160, :]
        rest = GP[g, 160:208, :].astype(F32)
        for q in range(4):
            rows = 48 if q < 3 else 16
            GU[48 * q : 48 * q + rows, 128:256] = unpack_rest(rest[0:rows], q)
        for b in range(8):
            block = HG.at[g, b % 4, b // 4]
            HU[64 * b : 64 * b + 64, 0:128] = block[0:64, :]
            packed = block[64:80, :].astype(F32)
            for q in range(4):
                HU[64 * b + 16 * q : 64 * b + 16 * q + 16, 128:256] = unpack_rest(packed, q)
        head_ref[...] += dot(GU[...], HU[...], NT)
        return 0

    lax.fori_loop(0, 8, head_group, 0)
    store(head_ref, head_out)

    dp_done(GCv, gc_c)
    cl_sum = ((GC[0] + GC[1]) + (GC[2] + GC[3])) + ((GC[4] + GC[5]) + (GC[6] + GC[7]))
    for k in range(4):
        cl_ref[:, 1024 * k : 1024 * k + 1024] = cl_sum[2 * k : 2 * k + 2, :]
    store(cl_ref, cl_out)

    both = BK[d].astype(F32)
    b1a, b1b = both[0:40, :].astype(BF16), both[40:80, 0:384].astype(BF16)
    b2 = both[40:80, 384:640].astype(BF16)
    hot1 = jnp.where(slot_hit[0:40], 1.0, 0.0)
    hot2 = jnp.where(slot_hit[40:80], 1.0, 0.0)
    back_one = dot(p1_ref[:, 0:640], b1a, NT) + dot(p1_ref[:, 640:1024], b1b, NT)
    add = dot_exact(back_one, hot1) + dot_exact(dot(p2_ref[...], b2, NT), hot2)
    bk_c = dp_core(BKv, bk_x)

    for n, i in enumerate(gh_f):
        recv(i, GRF.at[n])
    block = GS2[zhi] + (GRF[0].astype(F32) + (GRF[1].astype(F32) + GRF[2].astype(F32)))
    hp[:, 0:128] = block[0:64, :]
    for q in range(4):
        part_q = block[64:80, :]
        hp[16 * q : 16 * q + 16, 128:256] = part_q if q == 0 else pltpu.roll(part_q, 128 - 32 * q, 1)
    gh_ref[...] = (hp[...] + add)[:, 0:160]
    store(gh_ref, gh_out)

    dp_done(CHv, ch_c)
    dp_done(BKv, bk_c)
    assemble(BK, P1f, P2f)
    for g in range(8):
        rows_g = CH[g].astype(F32)
        C1f[40 * g : 40 * g + 40, :] = rows_g[0:40, :]
        C2f[40 * g : 40 * g + 40, :] = rows_g[40:80, :]
    gp1_ref[...] = dot(C1f[...].astype(BF16), P1f[...].astype(BF16), TN)[0:64, :]
    store(gp1_ref, gp1_out)
    gp2_ref[...] = dot(C2f[...].astype(BF16), P2f[...].astype(BF16), TN)[0:64, :]
    store(gp2_ref, gp2_out)
    for copy in stores:
        copy.wait()

    for copy in sent:
        copy.wait_send()


def hand_over(*refs):
    for i in range(8):
        refs[8 + i][...] = refs[i][...]


def on_device(
    hidden_states, head_weight, cluster_weight, proj_one, tail_one, proj_two, tail_two,
    targets, token_cluster, tail_rows, tail_counts,
):
    vmem = pl.BlockSpec(memory_space=pltpu.VMEM)
    hbm = pl.BlockSpec(memory_space=pl.ANY)
    shapes = [
        ((1, 160), F32), ((64, 160), F32), ((160, 512), F32), ((2, 4096), F32),
        ((64, 1024), F32), ((320, 128), F32), ((64, 256), F32), ((32, 1664), F32),
    ]
    V = pltpu.VMEM
    scratch = [
        V((64, 160), BF16), V((64, 1024), BF16), V((64, 256), BF16), V((1, 160), jnp.int32),
        V((1, 160), jnp.int32), V((2, 40), jnp.int32), V((1, 2), jnp.int32),
    ] + [V(s, t) for s, t in shapes] + [
        V((320, 1024), BF16), V((1664, 256), BF16), V((2, 256), jnp.int32),
        V((64, 256), F32), V((4, 4, 4, 80, 128), BF16), V((4096, 256), BF16), V((256, 4096), BF16),
        V((4096, 256), BF16), V((8, 4, 2, 80, 128), BF16), V((512, 256), BF16),
        V((8, 80, 128), BF16), V((4, 4, 4, 8, 128), F32), V((3, 4, 4, 8, 128), F32),
        V((3, 4, 8, 128), F32), V((4, 4, 8, 128), F32), V((4, 4, 8, 128), F32),
        V((4, 4, 4, 8, 128), F32), V((80, 640), F32), V((8, 80, 640), BF16),
        V((320, 1024), F32), V((320, 256), F32), V((320, 1024), BF16), V((320, 256), BF16),
        V((4, 8, 256), F32), V((4, 4, 8, 256), F32),
        V((4, 8, 128), F32), V((4, 4, 8, 128), F32), V((128, 128), F32),
        V((256, 256), F32), V((40, 320), F32), V((40, 1664), F32), V((8, 80, 128), F32),
        V((8, 208, 128), BF16), V((160, 256), BF16), V((8, 8, 1024), F32),
        V((4, 4, 4, 8, 128), F32), V((3, 4, 4, 8, 128), F32), V((3, 4, 8, 128), F32), V((4, 4, 8, 128), F32),
        V((4, 4, 8, 128), F32), V((4, 4, 4, 8, 128), F32), V((8, 80, 640), BF16),
        V((320, 128), F32), V((320, 128), F32),
        V((4, 4, 4, 80, 128), BF16), V((3, 4, 4, 80, 128), BF16), V((3, 4, 80, 128), BF16),
        V((3, 4, 80, 128), BF16), V((4, 80, 128), F32), V((6, 80, 128), BF16),
        pltpu.SemaphoreType.DMA((SEMS,)), pltpu.SemaphoreType.DMA((SEMS,)), pltpu.SemaphoreType.DMA,
        pltpu.SemaphoreType.DMA((2,)), pltpu.SemaphoreType.DMA((7,)), pltpu.SemaphoreType.DMA((8,)),
    ]
    out = pl.pallas_call(
        kernel,
        out_shape=[jax.ShapeDtypeStruct(s, t) for s, t in shapes],
        in_specs=[hbm, hbm, vmem] + [hbm] * 8,
        out_specs=[hbm] * 8,
        scratch_shapes=scratch,
        compiler_params=pltpu.CompilerParams(
            collective_id=0, has_side_effects=True, vmem_limit_bytes=56 * 1024 * 1024
        ),
    )(
        hidden_states.T, head_weight, cluster_weight, proj_one, tail_one, proj_two, tail_two,
        targets.reshape(1, 160), token_cluster.reshape(1, 160), tail_rows[0], tail_counts,
    )
    loss, gh, head, cl, gp1, gt1, gp2, gt2 = pl.pallas_call(
        hand_over,
        out_shape=[jax.ShapeDtypeStruct(s, t) for s, t in shapes],
        in_specs=[vmem] * 8,
        out_specs=[vmem] * 8,
    )(*out)
    return (
        loss.reshape(160),
        gh.T,
        head,
        cl,
        gp1,
        gt1,
        gp2,
        gt2.T,
    )


def solution(mesh):
    return jax.shard_map(
        on_device,
        mesh=mesh,
        in_specs=(
            P("dp", "vocab"), P("vocab", None), P(), P("vocab", None), P("vocab", None),
            P("vocab", None), P("vocab", None), P("dp"), P("dp"), P("dp", None, None), P("dp", None),
        ),
        out_specs=(
            P("dp"), P("dp", "vocab"), P("vocab", "dp"), P(), P("vocab", None),
            P("vocab", "dp"), P("vocab", None), P("vocab", "dp"),
        ),
        check_vma=False,
    )
```
